32 devices in a mesh: groups: 2 (over y), space: 8 (over z, x), inst: 2 (over core).
Axes of the slice: x: 2, y: 2, z: 4, core: 2. Of those that a mesh axis runs over, the one named last changes fastest.
Arguments:
- flow_state: float32 [12, 8, 64, 256], P('groups', 'inst', 'space'), parts along dimension 0, may hold values from -6 to 6
- jac_pitch: float32 [12, 6], P('groups'), parts along dimension 0, may hold values from -2.5 to 2.5
- jac_axial: float32 [12, 6], P('groups'), parts along dimension 0, may hold values from -2.5 to 2.5
- pseudo_step: float32 [64, 512], P('space', 'groups'), parts along dimension 1, may hold values from 0.05 to 0.5
- partner: int32 [4, 8], P('groups'), parts along dimension 0, may hold values from 0 to 7, as said below
- iface_index: int32 [4, 64], P('groups', 'space'), parts along dimension 0, may hold values from 0 to 63, as said below
Outputs:
- new_state: float32 [12, 8, 64, 256], P('groups', 'inst', 'space'), parts along dimension 0
- smoothed: float32 [12, 8, 64, 256], P('groups', 'inst', 'space'), parts along dimension 0
The draws below stay inside these ranges and needn't reach their ends.
There are 2 independent parts, one for each index of `groups`. The reference program is written for one: setup_inputs(seed, part) draws one part's arguments, and reference() takes and returns one part's arrays. A program takes and returns all parts, laid end to end along the dimension named above; each array names one. Nothing has to cross between parts.
Inputs may be any that keep to these rules, and one draw needn't show every extreme that they name: Row k of partner is the cyclic shift n -> (n + s_k) mod 8 with s_k from 1 to 7. Row k of iface_index is the cyclic shift p -> (p + o_k) mod 64 of the pitch positions.
All inputs are finite; a program needn't handle non-finite values.
Results may differ from the reference program's by a relative error of at most 0.000088.
Values sent between devices are 32-bit elements; how exact they have to be, the bound alone decides.
No kernel may reach another device: no remote copies, remote signals or barrier semaphores. Data moves between devices by JAX's collectives and lax.ppermute only.
A program may use at most 64 MiB of HBM per device.

```python
import math
import jax
import jax.numpy as jnp
from jax import lax

VARS = 6
INST = 8
NA = 256
IFACES = 2
SWEEPS = 3
NP = 64


def draw_partner(key, part):
    key = jax.random.fold_in(key, 11)
    shifts = jax.random.randint(key, (IFACES, 1), 1, INST)
    return ((jnp.arange(INST)[None, :] + shifts) % INST).astype(jnp.int32)


def draw_iface_index(key, part):
    key = jax.random.fold_in(key, 23)
    offsets = jax.random.randint(key, (IFACES, 1), 0, NP)
    return ((jnp.arange(NP)[None, :] + offsets) % NP).astype(jnp.int32)


def levels(own_key, extent, split, smallest, largest):
    factor_of, own = 1.0, jax.random.fold_in(own_key, 6)
    for dim, parts in split:
        heights = jnp.exp(jax.random.uniform(jax.random.fold_in(own, dim), (parts,), jnp.float32, smallest / len(split), largest / len(split)))
        factor_of = factor_of * jnp.repeat(heights, extent[dim] // parts).reshape([-1 if axis == dim else 1 for axis in range(len(extent))])
    return factor_of


def scatter_about(key, shape, scale, most, pieces=(), kind=jnp.bfloat16):
    entries = jax.random.normal(key, shape, jnp.float32) * scale
    if len(pieces) > 0:
        entries = levels(key, shape, pieces, -0.22, 0.18) * entries
    return jnp.clip(entries, min=-most, max=most).astype(kind)


def setup_inputs(seed: int = 0, part: int = 0) -> dict:
    seeds = jax.random.split(jax.random.key(seed), 7)
    part_splits = jax.random.split(jax.random.fold_in(seeds[6], part), 7)
    return {
        "flow_state": scatter_about(part_splits[0], (VARS, INST, NP, NA), 1.0, 6.0, ((1, 2), (2, 8)), jnp.float32),
        "jac_pitch": scatter_about(part_splits[1], (VARS, VARS), VARS ** -0.5, 2.5, (), jnp.float32),
        "jac_axial": scatter_about(part_splits[2], (VARS, VARS), VARS ** -0.5, 2.5, (), jnp.float32),
        "pseudo_step": jnp.clip(jnp.exp(math.log(0.5) - 2.3025851 * jax.random.uniform(part_splits[3], (NP, NA), jnp.float32) ** levels(part_splits[3], (NP, NA), ((0, 8),), -0.2, 0.2)), 0.05, 0.5),
        "partner": draw_partner(jax.random.fold_in(jax.random.fold_in(seeds[6], part), 71), part),
        "iface_index": draw_iface_index(jax.random.fold_in(jax.random.fold_in(seeds[6], part), 71), part),
    }


VISCOUS = 0.25
SMOOTHING = 1.0

def spectral_table(instances):
    rows = jnp.arange(instances)[:, None]
    cols = jnp.arange(instances)[None, :]
    sign = (1 - 2 * ((rows - cols) % 2)).astype(jnp.float32)
    spacing = jnp.where(rows == cols, 0.5, (rows - cols).astype(jnp.float32))
    values = 0.5 * sign / jnp.tan(jnp.pi * spacing / instances)
    return jnp.where(rows == cols, 0.0, values).astype(jnp.float32)

def interface_planes(axial_cells, planes_count):
    return [(plane_no + 1) * axial_cells // (planes_count + 1) for plane_no in range(planes_count)]

def mix_vars(matrix, field):
    return jnp.einsum('uv,vnpa->unpa', matrix, field, precision=lax.Precision.HIGHEST)

def flux_terms(centre, pitch_next, pitch_prev, time_term, inflow, jac_pitch, jac_axial, planes):
    zeros_edge = jnp.zeros_like(centre[..., :1])
    upstream = jnp.concatenate([zeros_edge, centre[..., :-1]], axis=3)
    downstream = jnp.concatenate([centre[..., 1:], centre[..., -1:]], axis=3)
    for plane_no, plane in enumerate(planes):
        upstream = upstream.at[..., plane].set(inflow[plane_no])
        downstream = downstream.at[..., plane - 1].set(centre[..., plane - 1])
    pitch_part = mix_vars(jac_pitch, 0.5 * (pitch_next - pitch_prev))
    axial_part = mix_vars(jac_axial, centre - upstream)
    spread = pitch_next + pitch_prev + upstream + downstream - 4.0 * centre
    return pitch_part + axial_part - VISCOUS * spread + time_term

def relax(source, pitch_pair, current):
    axial_prev = jnp.pad(current[..., :-1], ((0, 0), (0, 0), (0, 0), (1, 0)))
    axial_next = jnp.pad(current[..., 1:], ((0, 0), (0, 0), (0, 0), (0, 1)))
    return (source + SMOOTHING * (pitch_pair + axial_prev + axial_next)) / (1.0 + 4.0 * SMOOTHING)

def reference(flow_state, jac_pitch, jac_axial, pseudo_step, partner, iface_index):
    spectral = spectral_table(INST)
    time_term = jnp.einsum('nj,vjpa->vnpa', spectral, flow_state, precision=lax.Precision.HIGHEST)
    planes = interface_planes(NA, IFACES)
    inflow = []
    for plane_no, plane in enumerate(planes):
        plane_line = flow_state[:, :, :, plane - 1]
        plane_line = jnp.take(plane_line, iface_index[plane_no], axis=2)
        plane_line = jnp.take(plane_line, partner[plane_no], axis=1)
        inflow.append(plane_line)
    pitch_next = jnp.roll(flow_state, -1, axis=2)
    pitch_prev = jnp.roll(flow_state, 1, axis=2)
    residual = flux_terms(flow_state, pitch_next, pitch_prev, time_term, inflow, jac_pitch, jac_axial, planes)
    smoothed = residual
    for sweep_no in range(SWEEPS):
        pair_sum = jnp.roll(smoothed, -1, axis=2) + jnp.roll(smoothed, 1, axis=2)
        smoothed = relax(residual, pair_sum, smoothed)
    new_state = flow_state - pseudo_step[None, None] * smoothed
    return (new_state, smoothed)
```

```python
import functools
import math

import jax
import jax.numpy as jnp
from jax import lax
from jax.experimental import pallas as pl
from jax.experimental.pallas import tpu as pltpu
from jax.sharding import PartitionSpec as P

IFACES = 2
SWEEPS = 3
VISCOUS = 0.25
SMOOTHING = 1.0
HALO = 4
ROWS = 8
LANES = 128


def spectral_entry(shift, instances):
    shift %= instances
    if shift == 0:
        return 0.0
    return 0.5 * (-1) ** shift / math.tan(math.pi * shift / instances)


def interface_planes(axial_cells, planes_count):
    return [(plane_no + 1) * axial_cells // (planes_count + 1) for plane_no in range(planes_count)]


def pack_kernel(planes, own_ref, oth_ref, line_ref, edge_ref):
    core = lax.axis_index("inst")
    low = lax.rem(lax.axis_index("space") + core, 2) == 0
    nvar, ninst = own_ref.shape[:2]
    lane = lax.broadcasted_iota(jnp.int32, (ROWS, LANES), 1)
    line = jnp.zeros((ROWS, LANES), jnp.float32)
    for plane_no, plane in enumerate(planes):
        for v in range(nvar):
            for half, ref in enumerate((own_ref, oth_ref)):
                for n in range(ninst):
                    at = (plane_no * nvar + v) * 2 * ninst + half * ninst + n
                    cell = jnp.broadcast_to(ref[v, n, :, plane - 1 : plane], (ROWS, LANES))
                    line = jnp.where(lane == at, cell, line)
    swapped = jnp.where(
        lax.rem(lane, 2 * ninst) < ninst,
        pltpu.roll(line, LANES - ninst, 1),
        pltpu.roll(line, ninst, 1),
    )
    line_ref[...] = jnp.where(core == 0, line, swapped)
    axial = own_ref.shape[3]
    row = lax.broadcasted_iota(jnp.int32, (ROWS, axial), 0)
    for v in range(nvar):
        for n in range(ninst):
            own, oth = own_ref[v, n], oth_ref[v, n]
            first = jnp.where(core == 0, own, oth)
            second = jnp.where(core == 0, oth, own)
            low_rows = jnp.where(row < HALO, first, pltpu.roll(second, HALO, 0))
            high_rows = jnp.where(row < HALO, pltpu.roll(first, HALO, 0), second)
            edge_ref[v, n] = jnp.where(low, low_rows, high_rows)


def step_kernel(
    planes,
    spaces,
    jac_pitch_ref,
    jac_axial_ref,
    partner_ref,
    index_ref,
    own_ref,
    oth_ref,
    near_ref,
    far_ref,
    lines_ref,
    step_ref,
    new_ref,
    out_ref,
    field_ref,
    window_ref,
    res_ref,
):
    core = lax.axis_index("inst")
    space = lax.axis_index("space")
    low = lax.rem(space + core, 2) == 0
    nvar, ninst, _, axial = own_ref.shape
    row8 = lax.broadcasted_iota(jnp.int32, (ROWS, axial), 0)
    for v in range(nvar):
        for n in range(ninst):
            near, far = near_ref[v, n], far_ref[v, n]
            below = jnp.where(low, near, far)
            above = jnp.where(low, far, near)
            field_ref[core, v, n, 0:ROWS] = own_ref[v, n]
            field_ref[1 - core, v, n, 0:ROWS] = oth_ref[v, n]
            field_ref[0, v, n, ROWS : 2 * ROWS] = jnp.where(
                row8 < HALO, above, pltpu.roll(below, HALO, 0)
            )
            field_ref[1, v, n, ROWS : 2 * ROWS] = jnp.where(
                row8 < HALO, pltpu.roll(above, HALO, 0), below
            )
    lane8 = lax.broadcasted_iota(jnp.int32, (ROWS, LANES), 1)
    row_l = lax.broadcasted_iota(jnp.int32, (ROWS, LANES), 0)
    facing = []
    for plane_no in range(len(planes)):
        first = index_ref[plane_no, 0]
        block, offset = first // ROWS, lax.rem(first, ROWS)
        for k in range(4):
            node = lax.rem(block + (spaces - 1 + k), spaces)
            at = pl.multiple_of((space ^ node) * ROWS, ROWS)
            window_ref[plane_no, pl.ds(k * ROWS, ROWS), :] = lines_ref[pl.ds(at, ROWS), :]
        mine = window_ref[plane_no, pl.ds(ROWS + offset, ROWS), :]
        after = window_ref[plane_no, pl.ds(2 * ROWS + offset, ROWS), :]
        before = window_ref[plane_no, pl.ds(offset, ROWS), :]
        shift = lax.rem(partner_ref[plane_no, 0], 2 * ninst)
        tiles = []
        for tile in (mine, jnp.where(row_l < HALO, after, before)):
            turned = jnp.where(
                lax.rem(lane8, 2 * ninst) + shift < 2 * ninst,
                pltpu.roll(tile, LANES - shift, 1),
                pltpu.roll(tile, 2 * ninst - shift, 1),
            )
            tiles.append(pltpu.roll(turned, lax.rem(LANES - ninst * core, LANES), 1))
        facing.append(jnp.concatenate(tiles, 0))

    lane = lax.broadcasted_iota(jnp.int32, (2 * ROWS, axial), 1)
    for n in range(ninst):
        centre, slope, inward, spread = [], [], [], []
        for v in range(nvar):
            c = field_ref[core, v, n]
            nxt, prv = pltpu.roll(c, 2 * ROWS - 1, 0), pltpu.roll(c, 1, 0)
            up = jnp.where(lane == 0, 0.0, pltpu.roll(c, 1, 1))
            down = jnp.where(lane == axial - 1, c, pltpu.roll(c, axial - 1, 1))
            for plane_no, plane in enumerate(planes):
                at = (plane_no * nvar + v) * 2 * ninst + n
                up = jnp.where(lane == plane, facing[plane_no][:, at : at + 1], up)
                down = jnp.where(lane == plane - 1, c, down)
            centre.append(c)
            slope.append(0.5 * (nxt - prv))
            inward.append(c - up)
            spread.append(nxt + prv + up + down - 4.0 * c)
        for u in range(nvar):
            total = -VISCOUS * spread[u]
            for v in range(nvar):
                total += jac_pitch_ref[u, v] * slope[v]
                total += jac_axial_ref[u, v] * inward[v]
            for j in range(ninst):
                if j != n:
                    total += spectral_entry(n - j, 2 * ninst) * field_ref[core, u, j]
                total += spectral_entry(n - j - ninst, 2 * ninst) * field_ref[1 - core, u, j]
            res_ref[u, n] = total

    scale = 1.0 / (1.0 + 4.0 * SMOOTHING)
    step = step_ref[...]
    for n in range(ninst):
        for u in range(nvar):
            res = res_ref[u, n]
            s = res
            for _ in range(SWEEPS):
                pair = pltpu.roll(s, 2 * ROWS - 1, 0) + pltpu.roll(s, 1, 0)
                prv = jnp.where(lane == 0, 0.0, pltpu.roll(s, 1, 1))
                nxt = jnp.where(lane == axial - 1, 0.0, pltpu.roll(s, axial - 1, 1))
                s = (res + SMOOTHING * (pair + prv + nxt)) * scale
            smoothed = s[0:ROWS]
            out_ref[u, n] = smoothed
            new_ref[u, n] = own_ref[u, n] - step * smoothed


def shards(flow_state, jac_pitch, jac_axial, pseudo_step, partner, iface_index):
    nvar, ninst, rows, axial = flow_state.shape
    spaces = lax.axis_size("space")
    planes = interface_planes(axial, IFACES)
    both = ("space", "inst")
    vmem = pl.BlockSpec(memory_space=pltpu.VMEM)
    smem = pl.BlockSpec(memory_space=pltpu.SMEM)

    other = lax.ppermute(flow_state, "inst", [(0, 1), (1, 0)])
    line, edge = pl.pallas_call(
        functools.partial(pack_kernel, planes),
        out_shape=(
            jax.ShapeDtypeStruct((rows, LANES), jnp.float32),
            jax.ShapeDtypeStruct((nvar, ninst, rows, axial), jnp.float32),
        ),
        in_specs=[vmem, vmem],
        out_specs=(vmem, vmem),
    )(flow_state, other)

    pairs = []
    for i in range(spaces):
        odd = (i + 1) % spaces if i % 2 else (i - 1) % spaces
        pairs += [(2 * i, 2 * odd), (2 * i + 1, 2 * (i ^ 1) + 1)]
    near = lax.ppermute(edge, both, pairs)
    far = lax.ppermute(near, "inst", [(0, 1), (1, 0)])

    lines, bit = line, 1
    while bit < spaces:
        got = lax.ppermute(lines, both, [(2 * i + 1, 2 * (i ^ bit) + 1) for i in range(spaces)])
        lines = jnp.concatenate([lines, got], axis=0)
        bit *= 2
    sent = lax.ppermute(lines, "inst", [(1, 0)])
    lines = jnp.where(lax.axis_index("inst") == 0, sent, lines)

    return pl.pallas_call(
        functools.partial(step_kernel, planes, spaces),
        out_shape=(
            jax.ShapeDtypeStruct(flow_state.shape, jnp.float32),
            jax.ShapeDtypeStruct(flow_state.shape, jnp.float32),
        ),
        in_specs=[smem] * 4 + [vmem] * 6,
        out_specs=(vmem, vmem),
        scratch_shapes=[
            pltpu.VMEM((2, nvar, ninst, 2 * rows, axial), jnp.float32),
            pltpu.VMEM((IFACES, 4 * rows + rows, LANES), jnp.float32),
            pltpu.VMEM((nvar, ninst, 2 * rows, axial), jnp.float32),
        ],
    )(
        jac_pitch, jac_axial, partner, iface_index,
        flow_state, other, near, far, lines, pseudo_step,
    )


def solution(mesh):
    in_specs = (
        P("groups", "inst", "space", None),
        P("groups", None),
        P("groups", None),
        P("space", "groups"),
        P("groups", None),
        P("groups", "space"),
    )
    out_specs = (P("groups", "inst", "space", None), P("groups", "inst", "space", None))
    return jax.shard_map(shards, mesh=mesh, in_specs=in_specs, out_specs=out_specs, check_vma=False)
```

```python
import functools
import math

import jax
import jax.numpy as jnp
from jax import lax
from jax.experimental import pallas as pl
from jax.experimental.pallas import tpu as pltpu
from jax.sharding import PartitionSpec as P

IFACES = 2
SWEEPS = 3
VISCOUS = 0.25
SMOOTHING = 1.0
HALO = 4
ROWS = 8
LANES = 128
VMEM_LIMIT = 16 * 1024 * 1024


def spectral_entry(shift, instances):
    shift %= instances
    if shift == 0:
        return 0.0
    return 0.5 * (-1) ** shift / math.tan(math.pi * shift / instances)


def interface_planes(axial_cells, planes_count):
    return [(plane_no + 1) * axial_cells // (planes_count + 1) for plane_no in range(planes_count)]


def stage_kernel(flow_ref, own_ref):
    own_ref[...] = flow_ref[...]


def pack_kernel(planes, own_ref, oth_ref, line_ref, edge_ref):
    core = lax.axis_index("inst")
    low = lax.rem(lax.axis_index("space") + core, 2) == 1
    nvar, ninst = own_ref.shape[:2]
    lane = lax.broadcasted_iota(jnp.int32, (ROWS, LANES), 1)
    line = jnp.zeros((ROWS, LANES), jnp.float32)
    for plane_no, plane in enumerate(planes):
        for v in range(nvar):
            for half, ref in enumerate((own_ref, oth_ref)):
                for n in range(ninst):
                    at = (plane_no * nvar + v) * 2 * ninst + half * ninst + n
                    cell = jnp.broadcast_to(ref[v, n, :, plane - 1 : plane], (ROWS, LANES))
                    line = jnp.where(lane == at, cell, line)
    swapped = jnp.where(
        lax.rem(lane, 2 * ninst) < ninst,
        pltpu.roll(line, LANES - ninst, 1),
        pltpu.roll(line, ninst, 1),
    )
    line_ref[...] = jnp.where(core == 0, line, swapped)
    axial = own_ref.shape[3]
    row = lax.broadcasted_iota(jnp.int32, (ROWS, axial), 0)
    for v in range(nvar):
        for n in range(ninst):
            own, oth = own_ref[v, n], oth_ref[v, n]
            first = jnp.where(core == 0, own, oth)
            second = jnp.where(core == 0, oth, own)
            low_rows = jnp.where(row < HALO, first, pltpu.roll(second, HALO, 0))
            high_rows = jnp.where(row < HALO, pltpu.roll(first, HALO, 0), second)
            edge_ref[v, n] = jnp.where(low, low_rows, high_rows)


def step_kernel(
    planes,
    spaces,
    jac_pitch_ref,
    jac_axial_ref,
    partner_ref,
    index_ref,
    own_ref,
    oth_ref,
    near_ref,
    far_ref,
    lines_ref,
    step_ref,
    new_ref,
    out_ref,
    field_ref,
    window_ref,
    res_ref,
):
    core = lax.axis_index("inst")
    space = lax.axis_index("space")
    low = lax.rem(space + core, 2) == 1
    nvar, ninst, _, axial = own_ref.shape
    row8 = lax.broadcasted_iota(jnp.int32, (ROWS, axial), 0)
    for v in range(nvar):
        for n in range(ninst):
            near, far = near_ref[v, n], far_ref[v, n]
            below = jnp.where(low, near, far)
            above = jnp.where(low, far, near)
            field_ref[core, v, n, 0:ROWS] = own_ref[v, n]
            field_ref[1 - core, v, n, 0:ROWS] = oth_ref[v, n]
            field_ref[0, v, n, ROWS : 2 * ROWS] = jnp.where(
                row8 < HALO, above, pltpu.roll(below, HALO, 0)
            )
            field_ref[1, v, n, ROWS : 2 * ROWS] = jnp.where(
                row8 < HALO, pltpu.roll(above, HALO, 0), below
            )
    lane8 = lax.broadcasted_iota(jnp.int32, (ROWS, LANES), 1)
    row_l = lax.broadcasted_iota(jnp.int32, (ROWS, LANES), 0)
    facing = []
    for plane_no in range(len(planes)):
        first = index_ref[plane_no, 0]
        block, offset = first // ROWS, lax.rem(first, ROWS)
        for k in range(4):
            node = lax.rem(block + (spaces - 1 + k), spaces)
            at = pl.multiple_of((space ^ node) * ROWS, ROWS)
            window_ref[plane_no, pl.ds(k * ROWS, ROWS), :] = lines_ref[pl.ds(at, ROWS), :]
        mine = window_ref[plane_no, pl.ds(ROWS + offset, ROWS), :]
        after = window_ref[plane_no, pl.ds(2 * ROWS + offset, ROWS), :]
        before = window_ref[plane_no, pl.ds(offset, ROWS), :]
        shift = lax.rem(partner_ref[plane_no, 0], 2 * ninst)
        tiles = []
        for tile in (mine, jnp.where(row_l < HALO, after, before)):
            turned = jnp.where(
                lax.rem(lane8, 2 * ninst) + shift < 2 * ninst,
                pltpu.roll(tile, LANES - shift, 1),
                pltpu.roll(tile, 2 * ninst - shift, 1),
            )
            tiles.append(pltpu.roll(turned, lax.rem(LANES - ninst * core, LANES), 1))
        facing.append(jnp.concatenate(tiles, 0))

    lane = lax.broadcasted_iota(jnp.int32, (2 * ROWS, axial), 1)
    for n in range(ninst):
        centre, slope, inward, spread = [], [], [], []
        for v in range(nvar):
            c = field_ref[core, v, n]
            nxt, prv = pltpu.roll(c, 2 * ROWS - 1, 0), pltpu.roll(c, 1, 0)
            up = jnp.where(lane == 0, 0.0, pltpu.roll(c, 1, 1))
            down = jnp.where(lane == axial - 1, c, pltpu.roll(c, axial - 1, 1))
            for plane_no, plane in enumerate(planes):
                at = (plane_no * nvar + v) * 2 * ninst + n
                up = jnp.where(lane == plane, facing[plane_no][:, at : at + 1], up)
                down = jnp.where(lane == plane - 1, c, down)
            centre.append(c)
            slope.append(0.5 * (nxt - prv))
            inward.append(c - up)
            spread.append(nxt + prv + up + down - 4.0 * c)
        for u in range(nvar):
            total = -VISCOUS * spread[u]
            for v in range(nvar):
                total += jac_pitch_ref[u, v] * slope[v]
                total += jac_axial_ref[u, v] * inward[v]
            for j in range(ninst):
                if j != n:
                    total += spectral_entry(n - j, 2 * ninst) * field_ref[core, u, j]
                total += spectral_entry(n - j - ninst, 2 * ninst) * field_ref[1 - core, u, j]
            res_ref[u, n] = total

    step = step_ref[...]
    lane = lax.broadcasted_iota(jnp.int32, (ROWS, axial), 1)
    k = SMOOTHING / (1.0 + 4.0 * SMOOTHING)
    base = 1.0 / (1.0 + 4.0 * SMOOTHING)
    c0, c1, c2, c3 = base, base * k, base * k * k, k * k * k
    for n in range(ninst):
        for u in range(nvar):
            r0 = res_ref[u, n]
            r1 = pltpu.roll(r0, 2 * ROWS - 1, 0) + pltpu.roll(r0, 1, 0)
            r2 = pltpu.roll(r1, 2 * ROWS - 1, 0) + pltpu.roll(r1, 1, 0)
            r3 = pltpu.roll(r2, 2 * ROWS - 1, 0) + pltpu.roll(r2, 1, 0)
            r0, r1, r2, r3 = (r[0:ROWS] for r in (r0, r1, r2, r3))
            s = c3 * r0
            for more in (
                c2 * r0 + 3.0 * c3 * r1,
                c1 * r0 + 2.0 * c2 * r1 + 3.0 * c3 * r2,
                c0 * r0 + c1 * r1 + c2 * r2 + c3 * r3,
            ):
                prv = jnp.where(lane == 0, 0.0, pltpu.roll(s, 1, 1))
                nxt = jnp.where(lane == axial - 1, 0.0, pltpu.roll(s, axial - 1, 1))
                s = more + prv + nxt
            out_ref[u, n] = s
            new_ref[u, n] = own_ref[u, n] - step * s


def here(array):
    return pltpu.with_memory_space_constraint(array, pltpu.VMEM)


def scalars(array):
    return pltpu.with_memory_space_constraint(array, pltpu.SMEM)


def shards(flow_state, jac_pitch, jac_axial, pseudo_step, partner, iface_index):
    nvar, ninst, rows, axial = flow_state.shape
    spaces = lax.axis_size("space")
    planes = interface_planes(axial, IFACES)
    both = ("space", "inst")
    vmem = pl.BlockSpec(memory_space=pltpu.VMEM)
    smem = pl.BlockSpec(memory_space=pltpu.SMEM)

    other = lax.ppermute(flow_state, "inst", [(0, 1), (1, 0)])
    own = pl.pallas_call(
        stage_kernel,
        out_shape=pltpu.VMEM(flow_state.shape, jnp.float32),
        in_specs=[vmem],
        out_specs=vmem,
        compiler_params=pltpu.CompilerParams(vmem_limit_bytes=VMEM_LIMIT),
    )(flow_state)
    other = here(other)
    line, edge = pl.pallas_call(
        functools.partial(pack_kernel, planes),
        out_shape=(
            pltpu.VMEM((rows, LANES), jnp.float32),
            pltpu.VMEM((nvar, ninst, rows, axial), jnp.float32),
        ),
        in_specs=[vmem, vmem],
        out_specs=(vmem, vmem),
        compiler_params=pltpu.CompilerParams(vmem_limit_bytes=VMEM_LIMIT),
    )(here(own), other)

    pairs = []
    for i in range(spaces):
        odd = (i + 1) % spaces if i % 2 else (i - 1) % spaces
        pairs += [(2 * i, 2 * (i ^ 1)), (2 * i + 1, 2 * odd + 1)]
    near = lax.ppermute(edge, both, pairs)
    far = lax.ppermute(near, "inst", [(0, 1), (1, 0)])

    lines, bit = line, 1
    while bit < spaces:
        got = lax.ppermute(
            lines, both, [(2 * i + c, 2 * (i ^ bit) + 1 - c) for i in range(spaces) for c in (0, 1)]
        )
        lines = jnp.concatenate([lines, got], axis=0)
        bit *= 2

    return pl.pallas_call(
        functools.partial(step_kernel, planes, spaces),
        out_shape=(
            jax.ShapeDtypeStruct(flow_state.shape, jnp.float32),
            jax.ShapeDtypeStruct(flow_state.shape, jnp.float32),
        ),
        in_specs=[smem] * 4 + [vmem] * 6,
        out_specs=(vmem, vmem),
        compiler_params=pltpu.CompilerParams(vmem_limit_bytes=VMEM_LIMIT),
        scratch_shapes=[
            pltpu.VMEM((2, nvar, ninst, 2 * rows, axial), jnp.float32),
            pltpu.VMEM((IFACES, 4 * rows + rows, LANES), jnp.float32),
            pltpu.VMEM((nvar, ninst, 2 * rows, axial), jnp.float32),
        ],
    )(
        *[scalars(a) for a in (jac_pitch, jac_axial, partner, iface_index)],
        here(own), other, here(near), here(far), here(lines), here(pseudo_step),
    )


def solution(mesh):
    in_specs = (
        P("groups", "inst", "space", None),
        P("groups", None),
        P("groups", None),
        P("space", "groups"),
        P("groups", None),
        P("groups", "space"),
    )
    out_specs = (P("groups", "inst", "space", None), P("groups", "inst", "space", None))
    return jax.shard_map(shards, mesh=mesh, in_specs=in_specs, out_specs=out_specs, check_vma=False)
```

```python
import functools
import math

import jax
import jax.numpy as jnp
from jax import lax
from jax.experimental import pallas as pl
from jax.experimental.pallas import tpu as pltpu
from jax.sharding import PartitionSpec as P

IFACES = 2
SWEEPS = 3
VISCOUS = 0.25
SMOOTHING = 1.0
HALO = 4
ROWS = 8
LANES = 128
GROUP = 8
VMEM_LIMIT = 16 * 1024 * 1024


def spectral_entry(shift, instances):
    shift %= instances
    if shift == 0:
        return 0.0
    return 0.5 * (-1) ** shift / math.tan(math.pi * shift / instances)


def interface_planes(axial_cells, planes_count):
    return [(plane_no + 1) * axial_cells // (planes_count + 1) for plane_no in range(planes_count)]


def sweep_weights():
    k = SMOOTHING / (1.0 + 4.0 * SMOOTHING)
    base = 1.0 / (1.0 + 4.0 * SMOOTHING)
    return [base * k**m for m in range(SWEEPS)] + [k**SWEEPS]


def spread_weight(m, distance):
    weights = sweep_weights() + [0.0] * 4
    paths = {0: {0: 1, 2: 2}, 1: {1: 1, 3: 3}, 2: {2: 1}, 3: {3: 1}}[distance]
    return sum(count * math.comb(m + j, m) * weights[m + j] for j, count in paths.items())


def round_bits(spaces):
    bits = list(range(spaces.bit_length() - 1))
    return bits[1:] + bits[:1]


def stage_kernel(flow_ref, own_ref):
    own_ref[...] = flow_ref[...]


def line_kernel(planes, own_ref, oth_ref, line_ref):
    core = lax.axis_index("inst")
    nvar, ninst = own_ref.shape[:2]
    lane = lax.broadcasted_iota(jnp.int32, (ROWS, LANES), 1)
    line = jnp.zeros((ROWS, LANES), jnp.float32)
    for plane_no, plane in enumerate(planes):
        for v in range(nvar):
            for half, ref in enumerate((own_ref, oth_ref)):
                for n in range(ninst):
                    at = (plane_no * nvar + v) * 2 * ninst + half * ninst + n
                    cell = jnp.broadcast_to(ref[v, n, :, plane - 1 : plane], (ROWS, LANES))
                    line = jnp.where(lane == at, cell, line)
    swapped = jnp.where(
        lax.rem(lane, 2 * ninst) < ninst,
        pltpu.roll(line, LANES - ninst, 1),
        pltpu.roll(line, ninst, 1),
    )
    line_ref[...] = jnp.where(core == 0, line, swapped)


def low_side():
    return lax.rem(lax.axis_index("space") + lax.axis_index("inst"), 2) == 1


def edge_kernel(own_ref, oth_ref, after_ref, edge_ref):
    del after_ref
    core = lax.axis_index("inst")
    low = low_side()
    nvar, ninst, _, axial = own_ref.shape
    row = lax.broadcasted_iota(jnp.int32, (ROWS, axial), 0)
    for v in range(nvar):
        for n in range(ninst):
            own, oth = own_ref[v, n], oth_ref[v, n]
            first = jnp.where(core == 0, own, oth)
            second = jnp.where(core == 0, oth, own)
            low_rows = jnp.where(row < HALO, first, pltpu.roll(second, HALO, 0))
            high_rows = jnp.where(row < HALO, pltpu.roll(first, HALO, 0), second)
            edge_ref[v, n] = jnp.where(low, low_rows, high_rows)


def local_terms(planes, jac, own, oth, n):
    nvar, ninst, rows, axial = own.shape
    lane = lax.broadcasted_iota(jnp.int32, (rows, axial), 1)
    inward, spread = [], []
    for v in range(nvar):
        c = own[v, n]
        up, down = pltpu.roll(c, 1, 1), pltpu.roll(c, axial - 1, 1)
        for plane in [0, *planes]:
            up = jnp.where(lane == plane, 0.0, up)
        for plane in [*planes, axial]:
            down = jnp.where(lane == plane - 1, c, down)
        inward.append(c - up)
        spread.append(up + down - 4.0 * c)
    terms = []
    for u in range(nvar):
        total = -VISCOUS * spread[u]
        for v in range(nvar):
            total += jac(u, v) * inward[v]
        for j in range(ninst):
            if j != n:
                total += spectral_entry(n - j, 2 * ninst) * own[u, j]
            total += spectral_entry(n - j - ninst, 2 * ninst) * oth[u, j]
        terms.append(total)
    return terms


def prepare_kernel(
    planes,
    spaces,
    jac_pitch_ref,
    jac_axial_ref,
    partner_ref,
    index_ref,
    own_ref,
    oth_ref,
    after_ref,
    local_ref,
    jac_ref,
    pick_ref,
    mix_ref,
):
    del after_ref
    core, space = lax.axis_index("inst"), lax.axis_index("space")
    nvar, ninst, _, axial = own_ref.shape
    for n in range(ninst):
        terms = local_terms(planes, lambda u, v: jac_axial_ref[u, v], own_ref, oth_ref, n)
        for u in range(nvar):
            local_ref[u, n] = terms[u]
    for which, ref in enumerate((jac_pitch_ref, jac_axial_ref)):
        for u in range(nvar):
            for v in range(nvar):
                at = (which * nvar + u) * nvar + v
                jac_ref[at : at + 1, :] = jnp.full((1, axial), ref[u, v], jnp.float32)

    total = spaces * ROWS
    row = lax.broadcasted_iota(jnp.int32, (2 * ROWS, total), 0)
    ahead = jnp.where(row < ROWS + HALO, row, row - 2 * ROWS)
    lane = lax.broadcasted_iota(jnp.int32, (2 * ROWS, total), 1)
    for plane_no in range(len(planes)):
        pitch = index_ref[plane_no, 0] + ahead
        pitch = jnp.where(pitch < 0, pitch + total, pitch)
        pitch = jnp.where(pitch >= total, pitch - total, pitch)
        apart = (pitch >> 3) ^ space
        place = pitch & 7
        for turn, bit in enumerate(round_bits(spaces)):
            place += ((apart >> bit) & 1) << (turn + 3)
        pick_ref[pl.ds(plane_no * 2 * ROWS, 2 * ROWS), :] = jnp.where(lane == place, 1.0, 0.0)

    lane = lax.broadcasted_iota(jnp.int32, (ROWS, 2 * LANES), 1) // GROUP
    row = lax.broadcasted_iota(jnp.int32, (ROWS, 2 * LANES), 0)
    to_var, to_inst = lane // ninst, lax.rem(lane, ninst) + ninst * core
    mix_ref[...] = jnp.zeros(mix_ref.shape, jnp.float32)
    for v in range(nvar):
        block = jnp.zeros((ROWS, 2 * LANES), jnp.float32)
        for u in range(nvar):
            value = -jac_axial_ref[u, v] - (VISCOUS if u == v else 0.0)
            block = jnp.where(to_var == u, value, block)
        for plane_no in range(len(planes)):
            source = lax.rem(to_inst + partner_ref[plane_no, 0], 2 * ninst)
            at = (plane_no * nvar + v) * 2 * ninst
            mix_ref[plane_no, at : at + ROWS, :] = jnp.where(row == source, block, 0.0)


def sweep_kernel(
    planes, own_ref, oth_ref, near_ref, *refs
):
    *far_refs, local_ref, jac_ref, swept_ref, halo_own, halo_oth = refs
    core = lax.axis_index("inst")
    low = low_side()
    nvar, ninst, _, axial = own_ref.shape
    cut = nvar // len(far_refs)
    row = lax.broadcasted_iota(jnp.int32, (ROWS, axial), 0)
    for v in range(nvar):
        for n in range(ninst):
            near, far = near_ref[v, n], far_refs[v // cut][v % cut, n]
            below = jnp.where(low, near, far)
            above = jnp.where(low, far, near)
            first = jnp.where(row < HALO, above, pltpu.roll(below, HALO, 0))
            second = jnp.where(row < HALO, pltpu.roll(above, HALO, 0), below)
            halo_own[v, n] = jnp.where(core == 0, first, second)
            halo_oth[v, n] = jnp.where(core == 0, second, first)
    c0, c1, c2, c3 = sweep_weights()
    lane = lax.broadcasted_iota(jnp.int32, (ROWS, axial), 1)

    def jac(which, u, v):
        at = (which * nvar + u) * nvar + v
        return jac_ref[at : at + 1, :]

    for n in range(ninst):
        terms = local_terms(planes, functools.partial(jac, 1), halo_own, halo_oth, n)
        slope, spread = [], []
        for v in range(nvar):
            c = jnp.concatenate([own_ref[v, n], halo_own[v, n]], axis=0)
            nxt, prv = pltpu.roll(c, 2 * ROWS - 1, 0), pltpu.roll(c, 1, 0)
            slope.append(0.5 * (nxt - prv))
            spread.append(nxt + prv)
        for u in range(nvar):
            r0 = jnp.concatenate([local_ref[u, n], terms[u]], axis=0) - VISCOUS * spread[u]
            for v in range(nvar):
                r0 += jac(0, u, v) * slope[v]
            r1 = pltpu.roll(r0, 2 * ROWS - 1, 0) + pltpu.roll(r0, 1, 0)
            r2 = pltpu.roll(r1, 2 * ROWS - 1, 0) + pltpu.roll(r1, 1, 0)
            r3 = pltpu.roll(r2, 2 * ROWS - 1, 0) + pltpu.roll(r2, 1, 0)
            r0, r1, r2, r3 = (r[0:ROWS] for r in (r0, r1, r2, r3))
            s = c3 * r0
            for more in (
                c2 * r0 + 3.0 * c3 * r1,
                c1 * r0 + 2.0 * c2 * r1 + 3.0 * c3 * r2,
                c0 * r0 + c1 * r1 + c2 * r2 + c3 * r3,
            ):
                prv = jnp.where(lane == 0, 0.0, pltpu.roll(s, 1, 1))
                nxt = jnp.where(lane == axial - 1, 0.0, pltpu.roll(s, axial - 1, 1))
                s = more + prv + nxt
            swept_ref[u, n] = s


def finish_kernel(
    planes, own_ref, swept_ref, lines_ref, pick_ref, mix_ref, step_ref, new_ref, out_ref
):
    nvar, ninst, _, axial = own_ref.shape
    exact = dict(precision=lax.Precision.HIGHEST, preferred_element_type=jnp.float32)
    facing = jnp.dot(pick_ref[...], lines_ref[...], **exact)
    lane = lax.rem(lax.broadcasted_iota(jnp.int32, (ROWS, 2 * LANES), 1), GROUP)
    spread = []
    for plane_no in range(len(planes)):
        power = jnp.dot(
            facing[plane_no * 2 * ROWS : (plane_no + 1) * 2 * ROWS], mix_ref[plane_no], **exact
        )
        total = jnp.zeros((ROWS, 2 * LANES), jnp.float32)
        for m in range(SWEEPS + 1):
            weight = jnp.zeros((ROWS, 2 * LANES), jnp.float32)
            for d in range(-SWEEPS, SWEEPS + 1):
                weight = jnp.where(lane == d + SWEEPS, spread_weight(m, abs(d)), weight)
            total += weight * power[0:ROWS]
            if m < SWEEPS:
                power = pltpu.roll(power, 2 * ROWS - 1, 0) + pltpu.roll(power, 1, 0)
        spread.append(total)
    step = step_ref[...]
    lane = lax.broadcasted_iota(jnp.int32, (ROWS, LANES), 1)
    for n in range(ninst):
        for u in range(nvar):
            tiles = [swept_ref[u, n, :, t : t + LANES] for t in range(0, axial, LANES)]
            group = (u * ninst + n) * GROUP
            for plane_no, plane in enumerate(planes):
                tile, at = divmod(plane - SWEEPS, LANES)
                assert at + GROUP <= LANES
                start = group // LANES * LANES
                moved = pltpu.roll(
                    spread[plane_no][:, start : start + LANES], (at - group) % LANES, 1
                )
                inside = (lane >= at) & (lane < at + GROUP)
                tiles[tile] = tiles[tile] + jnp.where(inside, moved, 0.0)
            swept = jnp.concatenate(tiles, axis=1)
            out_ref[u, n] = swept
            new_ref[u, n] = own_ref[u, n] - step * swept


def here(array):
    return pltpu.with_memory_space_constraint(array, pltpu.VMEM)


def shards(flow_state, jac_pitch, jac_axial, pseudo_step, partner, iface_index):
    nvar, ninst, rows, axial = flow_state.shape
    spaces = lax.axis_size("space")
    planes = interface_planes(axial, IFACES)
    both = ("space", "inst")
    vmem = pl.BlockSpec(memory_space=pltpu.VMEM)
    smem = pl.BlockSpec(memory_space=pltpu.SMEM)
    anywhere = pl.BlockSpec(memory_space=pl.ANY)
    params = pltpu.CompilerParams(vmem_limit_bytes=VMEM_LIMIT)
    block = pltpu.VMEM(flow_state.shape, jnp.float32)
    cores = [(0, 1), (1, 0)]

    other = here(lax.ppermute(flow_state, "inst", cores))
    own = here(
        pl.pallas_call(
            stage_kernel, out_shape=block, in_specs=[vmem], out_specs=vmem, compiler_params=params
        )(flow_state)
    )
    line = pl.pallas_call(
        functools.partial(line_kernel, planes),
        out_shape=pltpu.VMEM((rows, LANES), jnp.float32),
        in_specs=[vmem, vmem],
        out_specs=vmem,
        compiler_params=params,
    )(own, other)

    lines, got = line, []
    for bit in round_bits(spaces):
        got.append(
            lax.ppermute(
                lines, both, [(2 * i + c, 2 * (i ^ (1 << bit)) + 1 - c) for i in range(spaces) for c in (0, 1)]
            )
        )
        lines = jnp.concatenate([lines, got[-1]], axis=0)

    edge = pl.pallas_call(
        edge_kernel,
        out_shape=block,
        in_specs=[vmem, vmem, anywhere],
        out_specs=vmem,
        compiler_params=params,
    )(own, other, line)
    pairs = []
    for i in range(spaces):
        odd = (i + 1) % spaces if i % 2 else (i - 1) % spaces
        pairs += [(2 * i, 2 * (i ^ 1)), (2 * i + 1, 2 * odd + 1)]
    near = lax.ppermute(edge, both, pairs)
    cut = nvar // 2
    far = [
        here(lax.ppermute(near[v : v + cut], "inst", cores)) for v in range(0, nvar, cut)
    ]

    local, jac, pick, mix = pl.pallas_call(
        functools.partial(prepare_kernel, planes, spaces),
        out_shape=(
            block,
            pltpu.VMEM((2 * nvar * nvar, axial), jnp.float32),
            pltpu.VMEM((IFACES * 2 * rows, spaces * rows), jnp.float32),
            pltpu.VMEM((IFACES, LANES, 2 * LANES), jnp.float32),
        ),
        in_specs=[smem] * 4 + [vmem] * 2 + [anywhere],
        out_specs=(vmem,) * 4,
        compiler_params=params,
    )(jac_pitch, jac_axial, partner, iface_index, own, other, got[0])

    swept = pl.pallas_call(
        functools.partial(sweep_kernel, planes),
        out_shape=block,
        in_specs=[vmem] * (5 + len(far)),
        out_specs=vmem,
        scratch_shapes=[block, block],
        compiler_params=params,
    )(own, other, here(near), *far, here(local), here(jac))

    return pl.pallas_call(
        functools.partial(finish_kernel, planes),
        out_shape=(jax.ShapeDtypeStruct(flow_state.shape, jnp.float32),) * 2,
        in_specs=[vmem] * 6,
        out_specs=(vmem, vmem),
        compiler_params=params,
    )(own, here(swept), here(lines), here(pick), here(mix), here(pseudo_step))


def solution(mesh):
    in_specs = (
        P("groups", "inst", "space", None),
        P("groups", None),
        P("groups", None),
        P("space", "groups"),
        P("groups", None),
        P("groups", "space"),
    )
    out_specs = (P("groups", "inst", "space", None), P("groups", "inst", "space", None))
    return jax.shard_map(shards, mesh=mesh, in_specs=in_specs, out_specs=out_specs, check_vma=False)
```

```python
import functools
import math

import jax
import jax.numpy as jnp
from jax import lax
from jax.experimental import pallas as pl
from jax.experimental.pallas import tpu as pltpu
from jax.sharding import PartitionSpec as P

IFACES = 2
SWEEPS = 3
VISCOUS = 0.25
SMOOTHING = 1.0
HALO = 4
ROWS = 8
LANES = 128
GROUP = 8
VMEM_LIMIT = 16 * 1024 * 1024


def spectral_entry(shift, instances):
    shift %= instances
    if shift == 0:
        return 0.0
    return 0.5 * (-1) ** shift / math.tan(math.pi * shift / instances)


def interface_planes(axial_cells, planes_count):
    return [(plane_no + 1) * axial_cells // (planes_count + 1) for plane_no in range(planes_count)]


def sweep_weights():
    k = SMOOTHING / (1.0 + 4.0 * SMOOTHING)
    base = 1.0 / (1.0 + 4.0 * SMOOTHING)
    return [base * k**m for m in range(SWEEPS)] + [k**SWEEPS]


def spread_weight(m, distance):
    weights = sweep_weights() + [0.0] * 4
    paths = {0: {0: 1, 2: 2}, 1: {1: 1, 3: 3}, 2: {2: 1}, 3: {3: 1}}[distance]
    return sum(count * math.comb(m + j, m) * weights[m + j] for j, count in paths.items())


def round_bits(spaces):
    bits = list(range(spaces.bit_length() - 1))
    return bits[1:] + bits[:1]


def stage_kernel(planes, flow_ref, own_ref, shift_ref, sweep_ref):
    own_ref[...] = flow_ref[...]
    axial = flow_ref.shape[3]
    source = lax.broadcasted_iota(jnp.int32, (axial, axial), 0)
    target = lax.broadcasted_iota(jnp.int32, (axial, axial), 1)
    ahead = target - source
    up, down = jnp.where(ahead == 1, 1.0, 0.0), jnp.where(ahead == -1, 1.0, 0.0)
    once = up + down
    for plane in planes:
        up = jnp.where(target == plane, 0.0, up)
    for plane in [*planes, axial]:
        down = jnp.where(target == plane - 1, jnp.where(ahead == 0, 1.0, 0.0), down)
    shift_ref[0:axial, :] = up.astype(jnp.bfloat16)
    shift_ref[axial : 2 * axial, :] = (VISCOUS * (up + down)).astype(jnp.bfloat16)
    far, edges = jnp.abs(ahead), source + target
    corner = (edges == 0) | (edges == 2 * axial - 2)
    beside = (edges == 1) | (edges == 2 * axial - 3)
    twice = jnp.where(far == 2, 1.0, jnp.where(far == 0, jnp.where(corner, 1.0, 2.0), 0.0))
    thrice = jnp.where(far == 3, 1.0, jnp.where(far == 1, jnp.where(beside, 2.0, 3.0), 0.0))
    for power, value in enumerate((once, twice, thrice)):
        sweep_ref[power * axial : (power + 1) * axial, :] = value.astype(jnp.bfloat16)


def line_kernel(planes, own_ref, oth_ref, line_ref):
    core = lax.axis_index("inst")
    nvar, ninst = own_ref.shape[:2]
    lane = lax.broadcasted_iota(jnp.int32, (ROWS, LANES), 1)
    line = jnp.zeros((ROWS, LANES), jnp.float32)
    for plane_no, plane in enumerate(planes):
        for v in range(nvar):
            for half, ref in enumerate((own_ref, oth_ref)):
                for n in range(ninst):
                    at = (plane_no * nvar + v) * 2 * ninst + half * ninst + n
                    cell = jnp.broadcast_to(ref[v, n, :, plane - 1 : plane], (ROWS, LANES))
                    line = jnp.where(lane == at, cell, line)
    swapped = jnp.where(
        lax.rem(lane, 2 * ninst) < ninst,
        pltpu.roll(line, LANES - ninst, 1),
        pltpu.roll(line, ninst, 1),
    )
    line_ref[...] = jnp.where(core == 0, line, swapped)


def low_side():
    return lax.rem(lax.axis_index("space") + lax.axis_index("inst"), 2) == 1


def edge_kernel(own_ref, oth_ref, after_ref, edge_ref):
    del after_ref
    core = lax.axis_index("inst")
    low = low_side()
    nvar, ninst, _, axial = own_ref.shape
    row = lax.broadcasted_iota(jnp.int32, (ROWS, axial), 0)
    for v in range(nvar):
        for n in range(ninst):
            own, oth = own_ref[v, n], oth_ref[v, n]
            first = jnp.where(core == 0, own, oth)
            second = jnp.where(core == 0, oth, own)
            low_rows = jnp.where(row < HALO, first, pltpu.roll(second, HALO, 0))
            high_rows = jnp.where(row < HALO, pltpu.roll(first, HALO, 0), second)
            edge_ref[v, n] = jnp.where(low, low_rows, high_rows)


def local_terms(planes, jac, own, oth, n):
    nvar, ninst, rows, axial = own.shape
    lane = lax.broadcasted_iota(jnp.int32, (rows, axial), 1)
    inward, spread = [], []
    for v in range(nvar):
        c = own[v, n]
        up, down = pltpu.roll(c, 1, 1), pltpu.roll(c, axial - 1, 1)
        for plane in [0, *planes]:
            up = jnp.where(lane == plane, 0.0, up)
        for plane in [*planes, axial]:
            down = jnp.where(lane == plane - 1, c, down)
        inward.append(c - up)
        spread.append(up + down - 4.0 * c)
    terms = []
    for u in range(nvar):
        total = -VISCOUS * spread[u]
        for v in range(nvar):
            total += jac(u, v) * inward[v]
        for j in range(ninst):
            if j != n:
                total += spectral_entry(n - j, 2 * ninst) * own[u, j]
            total += spectral_entry(n - j - ninst, 2 * ninst) * oth[u, j]
        terms.append(total)
    return terms


def prepare_kernel(
    planes,
    spaces,
    jac_pitch_ref,
    jac_axial_ref,
    partner_ref,
    index_ref,
    own_ref,
    oth_ref,
    step_in_ref,
    after_ref,
    step_ref,
    local_ref,
    jac_ref,
    pick_ref,
    mix_ref,
):
    del after_ref
    step_ref[...] = step_in_ref[...]
    core, space = lax.axis_index("inst"), lax.axis_index("space")
    nvar, ninst, _, axial = own_ref.shape
    for n in range(ninst):
        terms = local_terms(planes, lambda u, v: jac_axial_ref[u, v], own_ref, oth_ref, n)
        for u in range(nvar):
            local_ref[u, n] = terms[u]
    for which, ref in enumerate((jac_pitch_ref, jac_axial_ref)):
        for u in range(nvar):
            for v in range(nvar):
                at = (which * nvar + u) * nvar + v
                jac_ref[at : at + 1, :] = jnp.full((1, axial), ref[u, v], jnp.float32)

    total = spaces * ROWS
    row = lax.broadcasted_iota(jnp.int32, (2 * ROWS, total), 0)
    ahead = jnp.where(row < ROWS + HALO, row, row - 2 * ROWS)
    lane = lax.broadcasted_iota(jnp.int32, (2 * ROWS, total), 1)
    for plane_no in range(len(planes)):
        pitch = index_ref[plane_no, 0] + ahead
        pitch = jnp.where(pitch < 0, pitch + total, pitch)
        pitch = jnp.where(pitch >= total, pitch - total, pitch)
        apart = (pitch >> 3) ^ space
        place = pitch & 7
        for turn, bit in enumerate(round_bits(spaces)):
            place += ((apart >> bit) & 1) << (turn + 3)
        pick_ref[pl.ds(plane_no * 2 * ROWS, 2 * ROWS), :] = jnp.where(lane == place, 1.0, 0.0)

    lane = lax.broadcasted_iota(jnp.int32, (ROWS, 2 * LANES), 1) // GROUP
    row = lax.broadcasted_iota(jnp.int32, (ROWS, 2 * LANES), 0)
    to_var, to_inst = lane // ninst, lax.rem(lane, ninst) + ninst * core
    mix_ref[...] = jnp.zeros(mix_ref.shape, jnp.float32)
    for v in range(nvar):
        block = jnp.zeros((ROWS, 2 * LANES), jnp.float32)
        for u in range(nvar):
            value = -jac_axial_ref[u, v] - (VISCOUS if u == v else 0.0)
            block = jnp.where(to_var == u, value, block)
        for plane_no in range(len(planes)):
            source = lax.rem(to_inst + partner_ref[plane_no, 0], 2 * ninst)
            at = (plane_no * nvar + v) * 2 * ninst
            mix_ref[plane_no, at : at + ROWS, :] = jnp.where(row == source, block, 0.0)


def times(left, right):
    first = left.astype(jnp.bfloat16)
    second = (left - first.astype(jnp.float32)).astype(jnp.bfloat16)
    return jnp.dot(first, right, preferred_element_type=jnp.float32) + jnp.dot(
        second, right, preferred_element_type=jnp.float32
    )


def inflow_spread(planes, lines_ref, pick_ref, mix_ref):
    exact = dict(precision=lax.Precision.HIGHEST, preferred_element_type=jnp.float32)
    facing = jnp.dot(pick_ref[...], lines_ref[...], **exact)
    lane = lax.rem(lax.broadcasted_iota(jnp.int32, (ROWS, 2 * LANES), 1), GROUP)
    spread = []
    for plane_no in range(len(planes)):
        power = jnp.dot(
            facing[plane_no * 2 * ROWS : (plane_no + 1) * 2 * ROWS], mix_ref[plane_no], **exact
        )
        total = jnp.zeros((ROWS, 2 * LANES), jnp.float32)
        for m in range(SWEEPS + 1):
            weight = jnp.zeros((ROWS, 2 * LANES), jnp.float32)
            for d in range(-SWEEPS, SWEEPS + 1):
                weight = jnp.where(lane == d + SWEEPS, spread_weight(m, abs(d)), weight)
            total += weight * power[0:ROWS]
            if m < SWEEPS:
                power = pltpu.roll(power, 2 * ROWS - 1, 0) + pltpu.roll(power, 1, 0)
        spread.append(total)
    return spread


def step_kernel(planes, cuts, *refs):
    own_ref, oth_ref, near_ref, *refs = refs
    far_refs, refs = refs[:cuts], refs[cuts:]
    local_ref, jac_ref, shift_ref, sweep_ref, lines_ref, pick_ref, mix_ref, step_ref, *refs = refs
    new_ref, out_ref, halo_own, halo_oth, parts_ref, rest_ref, terms_ref, base_ref = refs
    core = lax.axis_index("inst")
    low = low_side()
    nvar, ninst, _, axial = own_ref.shape
    cut = nvar // cuts
    row = lax.broadcasted_iota(jnp.int32, (ROWS, axial), 0)
    spread = inflow_spread(planes, lines_ref, pick_ref, mix_ref)
    for v in range(nvar):
        for n in range(ninst):
            near, far = near_ref[v, n], far_refs[v // cut][v % cut, n]
            below = jnp.where(low, near, far)
            above = jnp.where(low, far, near)
            first = jnp.where(row < HALO, above, pltpu.roll(below, HALO, 0))
            second = jnp.where(row < HALO, pltpu.roll(above, HALO, 0), below)
            halo_own[v, n] = jnp.where(core == 0, first, second)
            halo_oth[v, n] = jnp.where(core == 0, second, first)

    def jac(which, u, v):
        at = (which * nvar + u) * nvar + v
        return jac_ref[at : at + 1, :]

    def lines_of(u, n):
        at = (u * ninst + n) * ROWS
        return slice(at, at + ROWS)

    for n in range(ninst):
        centre = [halo_own[v, n] for v in range(nvar)]
        for u in range(nvar):
            z = sum(jac(1, u, v) * centre[v] for v in range(nvar))
            rest = z + 4.0 * VISCOUS * centre[u]
            for j in range(ninst):
                if j != n:
                    rest += spectral_entry(n - j, 2 * ninst) * halo_own[u, j]
                rest += spectral_entry(n - j - ninst, 2 * ninst) * halo_oth[u, j]
            rest_ref[lines_of(u, n), :] = rest
            parts_ref[lines_of(u, n), 0:axial] = z
            parts_ref[lines_of(u, n), axial : 2 * axial] = centre[u]
    rest_ref[...] = rest_ref[...] - times(parts_ref[...], shift_ref[...])

    c0, c1, c2, c3 = sweep_weights()
    for n in range(ninst):
        slope, around = [], []
        for v in range(nvar):
            c = jnp.concatenate([own_ref[v, n], halo_own[v, n]], axis=0)
            nxt, prv = pltpu.roll(c, 2 * ROWS - 1, 0), pltpu.roll(c, 1, 0)
            slope.append(0.5 * (nxt - prv))
            around.append(nxt + prv)
        for u in range(nvar):
            at = lines_of(u, n)
            r0 = jnp.concatenate([local_ref[u, n], rest_ref[at, :]], axis=0) - VISCOUS * around[u]
            for v in range(nvar):
                r0 += jac(0, u, v) * slope[v]
            r1 = pltpu.roll(r0, 2 * ROWS - 1, 0) + pltpu.roll(r0, 1, 0)
            r2 = pltpu.roll(r1, 2 * ROWS - 1, 0) + pltpu.roll(r1, 1, 0)
            r3 = pltpu.roll(r2, 2 * ROWS - 1, 0) + pltpu.roll(r2, 1, 0)
            r0, r1, r2, r3 = (r[0:ROWS] for r in (r0, r1, r2, r3))
            base_ref[at, :] = c0 * r0 + c1 * r1 + c2 * r2 + c3 * r3
            terms_ref[at, 0:axial] = c1 * r0 + 2.0 * c2 * r1 + 3.0 * c3 * r2
            terms_ref[at, axial : 2 * axial] = c2 * r0 + 3.0 * c3 * r1
            terms_ref[at, 2 * axial : 3 * axial] = c3 * r0
    base_ref[...] = base_ref[...] + times(terms_ref[...], sweep_ref[...])

    step = step_ref[...]
    lane = lax.broadcasted_iota(jnp.int32, (ROWS, LANES), 1)
    for n in range(ninst):
        for u in range(nvar):
            tiles = [base_ref[lines_of(u, n), t : t + LANES] for t in range(0, axial, LANES)]
            group = (u * ninst + n) * GROUP
            for plane_no, plane in enumerate(planes):
                tile, at = divmod(plane - SWEEPS, LANES)
                assert at + GROUP <= LANES
                start = group // LANES * LANES
                moved = pltpu.roll(
                    spread[plane_no][:, start : start + LANES], (at - group) % LANES, 1
                )
                inside = (lane >= at) & (lane < at + GROUP)
                tiles[tile] = tiles[tile] + jnp.where(inside, moved, 0.0)
            swept = jnp.concatenate(tiles, axis=1)
            out_ref[u, n] = swept
            new_ref[u, n] = own_ref[u, n] - step * swept


def here(array):
    return pltpu.with_memory_space_constraint(array, pltpu.VMEM)


def shards(flow_state, jac_pitch, jac_axial, pseudo_step, partner, iface_index):
    nvar, ninst, rows, axial = flow_state.shape
    spaces = lax.axis_size("space")
    planes = interface_planes(axial, IFACES)
    both = ("space", "inst")
    vmem = pl.BlockSpec(memory_space=pltpu.VMEM)
    smem = pl.BlockSpec(memory_space=pltpu.SMEM)
    anywhere = pl.BlockSpec(memory_space=pl.ANY)
    params = pltpu.CompilerParams(vmem_limit_bytes=VMEM_LIMIT)
    block = pltpu.VMEM(flow_state.shape, jnp.float32)
    cores = [(0, 1), (1, 0)]

    other = here(lax.ppermute(flow_state, "inst", cores))
    own, shift, sweep = pl.pallas_call(
        functools.partial(stage_kernel, planes),
        out_shape=(
            block,
            pltpu.VMEM((2 * axial, axial), jnp.bfloat16),
            pltpu.VMEM((SWEEPS * axial, axial), jnp.bfloat16),
        ),
        in_specs=[vmem],
        out_specs=(vmem,) * 3,
        compiler_params=params,
    )(flow_state)
    own = here(own)
    line = pl.pallas_call(
        functools.partial(line_kernel, planes),
        out_shape=pltpu.VMEM((rows, LANES), jnp.float32),
        in_specs=[vmem, vmem],
        out_specs=vmem,
        compiler_params=params,
    )(own, other)

    lines, got = line, []
    for bit in round_bits(spaces):
        got.append(
            lax.ppermute(
                lines, both, [(2 * i + c, 2 * (i ^ (1 << bit)) + 1 - c) for i in range(spaces) for c in (0, 1)]
            )
        )
        lines = jnp.concatenate([lines, got[-1]], axis=0)

    edge = pl.pallas_call(
        edge_kernel,
        out_shape=block,
        in_specs=[vmem, vmem, anywhere],
        out_specs=vmem,
        compiler_params=params,
    )(own, other, line)
    pairs = []
    for i in range(spaces):
        odd = (i + 1) % spaces if i % 2 else (i - 1) % spaces
        pairs += [(2 * i, 2 * (i ^ 1)), (2 * i + 1, 2 * odd + 1)]
    near = lax.ppermute(edge, both, pairs)
    cut = nvar // 2
    far = [
        here(lax.ppermute(near[v : v + cut], "inst", cores)) for v in range(0, nvar, cut)
    ]

    step, local, jac, pick, mix = pl.pallas_call(
        functools.partial(prepare_kernel, planes, spaces),
        out_shape=(
            pltpu.VMEM(pseudo_step.shape, jnp.float32),
            block,
            pltpu.VMEM((2 * nvar * nvar, axial), jnp.float32),
            pltpu.VMEM((IFACES * 2 * rows, spaces * rows), jnp.float32),
            pltpu.VMEM((IFACES, LANES, 2 * LANES), jnp.float32),
        ),
        in_specs=[smem] * 4 + [vmem] * 3 + [anywhere],
        out_specs=(vmem,) * 5,
        compiler_params=params,
    )(jac_pitch, jac_axial, partner, iface_index, own, other, pseudo_step, got[0])

    lined = nvar * ninst * rows
    return pl.pallas_call(
        functools.partial(step_kernel, planes, len(far)),
        out_shape=(jax.ShapeDtypeStruct(flow_state.shape, jnp.float32),) * 2,
        in_specs=[vmem] * (11 + len(far)),
        out_specs=(vmem, vmem),
        scratch_shapes=[
            block,
            block,
            pltpu.VMEM((lined, 2 * axial), jnp.float32),
            pltpu.VMEM((lined, axial), jnp.float32),
            pltpu.VMEM((lined, SWEEPS * axial), jnp.float32),
            pltpu.VMEM((lined, axial), jnp.float32),
        ],
        compiler_params=params,
    )(
        own, other, here(near), *far,
        *[here(a) for a in (local, jac, shift, sweep, lines, pick, mix, step)],
    )


def solution(mesh):
    in_specs = (
        P("groups", "inst", "space", None),
        P("groups", None),
        P("groups", None),
        P("space", "groups"),
        P("groups", None),
        P("groups", "space"),
    )
    out_specs = (P("groups", "inst", "space", None), P("groups", "inst", "space", None))
    return jax.shard_map(shards, mesh=mesh, in_specs=in_specs, out_specs=out_specs, check_vma=False)
```

```python
import functools
import math

import jax
import jax.numpy as jnp
from jax import lax
from jax.experimental import pallas as pl
from jax.experimental.pallas import tpu as pltpu
from jax.sharding import PartitionSpec as P

IFACES = 2
SWEEPS = 3
VISCOUS = 0.25
SMOOTHING = 1.0
HALO = 4
ROWS = 8
LANES = 128
GROUP = 8
VMEM_LIMIT = 16 * 1024 * 1024


def spectral_entry(shift, instances):
    shift %= instances
    if shift == 0:
        return 0.0
    return 0.5 * (-1) ** shift / math.tan(math.pi * shift / instances)


def interface_planes(axial_cells, planes_count):
    return [(plane_no + 1) * axial_cells // (planes_count + 1) for plane_no in range(planes_count)]


def sweep_weights():
    k = SMOOTHING / (1.0 + 4.0 * SMOOTHING)
    base = 1.0 / (1.0 + 4.0 * SMOOTHING)
    return [base * k**m for m in range(SWEEPS)] + [k**SWEEPS]


def spread_weight(m, distance):
    weights = sweep_weights() + [0.0] * 4
    paths = {0: {0: 1, 2: 2}, 1: {1: 1, 3: 3}, 2: {2: 1}, 3: {3: 1}}[distance]
    return sum(count * math.comb(m + j, m) * weights[m + j] for j, count in paths.items())


def round_bits(spaces):
    bits = list(range(spaces.bit_length() - 1))
    return bits[1:] + bits[:1]


def stage_kernel(planes, flow_ref, own_ref, shift_ref, sweep_ref):
    own_ref[...] = flow_ref[...]
    axial = flow_ref.shape[3]
    source = lax.broadcasted_iota(jnp.int32, (axial, axial), 0)
    target = lax.broadcasted_iota(jnp.int32, (axial, axial), 1)
    ahead = target - source
    up, down = jnp.where(ahead == 1, 1.0, 0.0), jnp.where(ahead == -1, 1.0, 0.0)
    once = up + down
    for plane in planes:
        up = jnp.where(target == plane, 0.0, up)
    for plane in [*planes, axial]:
        down = jnp.where(target == plane - 1, jnp.where(ahead == 0, 1.0, 0.0), down)
    shift_ref[0:axial, :] = up.astype(jnp.bfloat16)
    shift_ref[axial : 2 * axial, :] = (VISCOUS * (up + down)).astype(jnp.bfloat16)
    far, edges = jnp.abs(ahead), source + target
    corner = (edges == 0) | (edges == 2 * axial - 2)
    beside = (edges == 1) | (edges == 2 * axial - 3)
    twice = jnp.where(far == 2, 1.0, jnp.where(far == 0, jnp.where(corner, 1.0, 2.0), 0.0))
    thrice = jnp.where(far == 3, 1.0, jnp.where(far == 1, jnp.where(beside, 2.0, 3.0), 0.0))
    for power, value in enumerate((once, twice, thrice)):
        sweep_ref[power * axial : (power + 1) * axial, :] = value.astype(jnp.bfloat16)


def line_kernel(planes, own_ref, oth_ref, line_ref):
    core = lax.axis_index("inst")
    nvar, ninst = own_ref.shape[:2]
    lane = lax.broadcasted_iota(jnp.int32, (ROWS, LANES), 1)
    line = jnp.zeros((ROWS, LANES), jnp.float32)
    for plane_no, plane in enumerate(planes):
        for v in range(nvar):
            for half, ref in enumerate((own_ref, oth_ref)):
                for n in range(ninst):
                    at = (plane_no * nvar + v) * 2 * ninst + half * ninst + n
                    cell = jnp.broadcast_to(ref[v, n, :, plane - 1 : plane], (ROWS, LANES))
                    line = jnp.where(lane == at, cell, line)
    swapped = jnp.where(
        lax.rem(lane, 2 * ninst) < ninst,
        pltpu.roll(line, LANES - ninst, 1),
        pltpu.roll(line, ninst, 1),
    )
    line_ref[...] = jnp.where(core == 0, line, swapped)


def low_side():
    return lax.rem(lax.axis_index("space") + lax.axis_index("inst"), 2) == 1


def edge_kernel(own_ref, oth_ref, after_ref, edge_ref):
    del after_ref
    core = lax.axis_index("inst")
    low = low_side()
    nvar, ninst, _, axial = own_ref.shape
    row = lax.broadcasted_iota(jnp.int32, (ROWS, axial), 0)
    for v in range(nvar):
        for n in range(ninst):
            own, oth = own_ref[v, n], oth_ref[v, n]
            first = jnp.where(core == 0, own, oth)
            second = jnp.where(core == 0, oth, own)
            low_rows = jnp.where(row < HALO, first, pltpu.roll(second, HALO, 0))
            high_rows = jnp.where(row < HALO, pltpu.roll(first, HALO, 0), second)
            edge_ref[v, n] = jnp.where(low, low_rows, high_rows)


def local_terms(planes, jac, own, oth, n):
    nvar, ninst, rows, axial = own.shape
    lane = lax.broadcasted_iota(jnp.int32, (rows, axial), 1)
    inward, spread = [], []
    for v in range(nvar):
        c = own[v, n]
        up, down = pltpu.roll(c, 1, 1), pltpu.roll(c, axial - 1, 1)
        for plane in [0, *planes]:
            up = jnp.where(lane == plane, 0.0, up)
        for plane in [*planes, axial]:
            down = jnp.where(lane == plane - 1, c, down)
        inward.append(c - up)
        spread.append(up + down - 4.0 * c)
    terms = []
    for u in range(nvar):
        total = -VISCOUS * spread[u]
        for v in range(nvar):
            total += jac(u, v) * inward[v]
        for j in range(ninst):
            if j != n:
                total += spectral_entry(n - j, 2 * ninst) * own[u, j]
            total += spectral_entry(n - j - ninst, 2 * ninst) * oth[u, j]
        terms.append(total)
    return terms


def prepare_kernel(
    planes,
    spaces,
    jac_pitch_ref,
    jac_axial_ref,
    partner_ref,
    index_ref,
    own_ref,
    oth_ref,
    step_in_ref,
    after_ref,
    step_ref,
    local_ref,
    jac_ref,
    pick_ref,
    mix_ref,
):
    del after_ref
    step_ref[...] = step_in_ref[...]
    core, space = lax.axis_index("inst"), lax.axis_index("space")
    nvar, ninst, _, axial = own_ref.shape
    for n in range(ninst):
        terms = local_terms(planes, lambda u, v: jac_axial_ref[u, v], own_ref, oth_ref, n)
        for u in range(nvar):
            local_ref[u, n] = terms[u]
    for which, ref in enumerate((jac_pitch_ref, jac_axial_ref)):
        for u in range(nvar):
            for v in range(nvar):
                at = (which * nvar + u) * nvar + v
                jac_ref[at : at + 1, :] = jnp.full((1, axial), ref[u, v], jnp.float32)

    total = spaces * ROWS
    row = lax.broadcasted_iota(jnp.int32, (2 * ROWS, total), 0)
    ahead = jnp.where(row < ROWS + HALO, row, row - 2 * ROWS)
    lane = lax.broadcasted_iota(jnp.int32, (2 * ROWS, total), 1)
    for plane_no in range(len(planes)):
        pitch = index_ref[plane_no, 0] + ahead
        pitch = jnp.where(pitch < 0, pitch + total, pitch)
        pitch = jnp.where(pitch >= total, pitch - total, pitch)
        apart = (pitch >> 3) ^ space
        place = pitch & 7
        for turn, bit in enumerate(round_bits(spaces)):
            place += ((apart >> bit) & 1) << (turn + 3)
        pick_ref[pl.ds(plane_no * 2 * ROWS, 2 * ROWS), :] = jnp.where(lane == place, 1.0, 0.0)

    lane = lax.broadcasted_iota(jnp.int32, (ROWS, 2 * LANES), 1) // GROUP
    row = lax.broadcasted_iota(jnp.int32, (ROWS, 2 * LANES), 0)
    to_var, to_inst = lane // ninst, lax.rem(lane, ninst) + ninst * core
    mix_ref[...] = jnp.zeros(mix_ref.shape, jnp.float32)
    for v in range(nvar):
        block = jnp.zeros((ROWS, 2 * LANES), jnp.float32)
        for u in range(nvar):
            value = -jac_axial_ref[u, v] - (VISCOUS if u == v else 0.0)
            block = jnp.where(to_var == u, value, block)
        for plane_no in range(len(planes)):
            source = lax.rem(to_inst + partner_ref[plane_no, 0], 2 * ninst)
            at = (plane_no * nvar + v) * 2 * ninst
            mix_ref[plane_no, at : at + ROWS, :] = jnp.where(row == source, block, 0.0)


def times(left, right):
    first = left.astype(jnp.bfloat16)
    second = (left - first.astype(jnp.float32)).astype(jnp.bfloat16)
    return jnp.dot(first, right, preferred_element_type=jnp.float32) + jnp.dot(
        second, right, preferred_element_type=jnp.float32
    )


def inflow_spread(planes, lines_refs, pick_ref, mix_ref):
    exact = dict(precision=lax.Precision.HIGHEST, preferred_element_type=jnp.float32)
    lines = jnp.concatenate([ref[...] for ref in lines_refs], axis=0)
    facing = jnp.dot(pick_ref[...], lines, **exact)
    lane = lax.rem(lax.broadcasted_iota(jnp.int32, (ROWS, 2 * LANES), 1), GROUP)
    spread = []
    for plane_no in range(len(planes)):
        power = jnp.dot(
            facing[plane_no * 2 * ROWS : (plane_no + 1) * 2 * ROWS], mix_ref[plane_no], **exact
        )
        total = jnp.zeros((ROWS, 2 * LANES), jnp.float32)
        for m in range(SWEEPS + 1):
            weight = jnp.zeros((ROWS, 2 * LANES), jnp.float32)
            for d in range(-SWEEPS, SWEEPS + 1):
                weight = jnp.where(lane == d + SWEEPS, spread_weight(m, abs(d)), weight)
            total += weight * power[0:ROWS]
            if m < SWEEPS:
                power = pltpu.roll(power, 2 * ROWS - 1, 0) + pltpu.roll(power, 1, 0)
        spread.append(total)
    return spread


def jac_row(jac_ref, nvar, which, u, v):
    at = (which * nvar + u) * nvar + v
    return jac_ref[at : at + 1, :]


def lines_of(ninst, u, n):
    at = (u * ninst + n) * ROWS
    return slice(at, at + ROWS)


def near_kernel(planes, *refs):
    own_ref, near_ref, local_ref, jac_ref, shift_ref, sweep_ref, base_ref, *refs = refs
    halo_own, halo_oth, parts_ref, rest_ref, terms_ref = refs
    core = lax.axis_index("inst")
    low = low_side()
    nvar, ninst, _, axial = own_ref.shape
    row = lax.broadcasted_iota(jnp.int32, (ROWS, axial), 0)
    keep = jnp.where(low, row, ROWS - 1 - row) >= HALO
    for v in range(nvar):
        for n in range(ninst):
            near = near_ref[v, n]
            turned = pltpu.roll(near, HALO, 0)
            first = jnp.where(keep, jnp.where(low, turned, near), 0.0)
            second = jnp.where(keep, jnp.where(low, near, turned), 0.0)
            halo_own[v, n] = jnp.where(core == 0, first, second)
            halo_oth[v, n] = jnp.where(core == 0, second, first)
    jac = functools.partial(jac_row, jac_ref, nvar)

    for n in range(ninst):
        centre = [halo_own[v, n] for v in range(nvar)]
        for u in range(nvar):
            z = sum(jac(1, u, v) * centre[v] for v in range(nvar))
            rest = z + 4.0 * VISCOUS * centre[u]
            for j in range(ninst):
                if j != n:
                    rest += spectral_entry(n - j, 2 * ninst) * halo_own[u, j]
                rest += spectral_entry(n - j - ninst, 2 * ninst) * halo_oth[u, j]
            at = lines_of(ninst, u, n)
            rest_ref[at, :] = rest
            parts_ref[at, 0:axial] = z
            parts_ref[at, axial : 2 * axial] = centre[u]
    rest_ref[...] = rest_ref[...] - times(parts_ref[...], shift_ref[...])

    c0, c1, c2, c3 = sweep_weights()
    for n in range(ninst):
        slope, around = [], []
        for v in range(nvar):
            c = jnp.concatenate([own_ref[v, n], halo_own[v, n]], axis=0)
            nxt, prv = pltpu.roll(c, 2 * ROWS - 1, 0), pltpu.roll(c, 1, 0)
            slope.append(0.5 * (nxt - prv))
            around.append(nxt + prv)
        for u in range(nvar):
            at = lines_of(ninst, u, n)
            r0 = jnp.concatenate([local_ref[u, n], rest_ref[at, :]], axis=0) - VISCOUS * around[u]
            for v in range(nvar):
                r0 += jac(0, u, v) * slope[v]
            r1 = pltpu.roll(r0, 2 * ROWS - 1, 0) + pltpu.roll(r0, 1, 0)
            r2 = pltpu.roll(r1, 2 * ROWS - 1, 0) + pltpu.roll(r1, 1, 0)
            r3 = pltpu.roll(r2, 2 * ROWS - 1, 0) + pltpu.roll(r2, 1, 0)
            r0, r1, r2, r3 = (r[0:ROWS] for r in (r0, r1, r2, r3))
            base_ref[at, :] = c0 * r0 + c1 * r1 + c2 * r2 + c3 * r3
            terms_ref[at, 0:axial] = c1 * r0 + 2.0 * c2 * r1 + 3.0 * c3 * r2
            terms_ref[at, axial : 2 * axial] = c2 * r0 + 3.0 * c3 * r1
            terms_ref[at, 2 * axial : 3 * axial] = c3 * r0
    base_ref[...] = base_ref[...] + times(terms_ref[...], sweep_ref[...])


def step_kernel(planes, cuts, *refs):
    before_ref, base_ref, *refs = refs
    far_refs, refs = refs[:cuts], refs[cuts:]
    jac_ref, shift_ref, sweep_ref, *lines_refs, pick_ref, mix_ref, step_ref = refs[:8]
    new_ref, out_ref, far_own, far_oth, parts_ref, rest_ref, terms_ref = refs[8:]
    core = lax.axis_index("inst")
    low = low_side()
    nvar, ninst, _, axial = new_ref.shape
    cut, packs = nvar // cuts, ninst // 2
    row = lax.broadcasted_iota(jnp.int32, (ROWS, axial), 0)
    side = jnp.where(low, row, ROWS - 1 - row)
    depth = side & (HALO - 1)
    spread = inflow_spread(planes, lines_refs, pick_ref, mix_ref)
    jac = functools.partial(jac_row, jac_ref, nvar)

    def shifted(tile, s):
        moved = pltpu.roll(tile, jnp.where(low, s, ROWS - s), 0)
        return jnp.where(depth >= s, moved, 0.0)

    for v in range(nvar):
        for n in range(ninst):
            tile = far_refs[v // cut][v % cut, n]
            turned = pltpu.roll(tile, HALO, 0)
            first = jnp.where(row < HALO, tile, turned)
            second = jnp.where(row < HALO, turned, tile)
            far_own[v, n] = jnp.where(core == 0, first, second)
            far_oth[v, n] = jnp.where(core == 0, second, first)

    def pack_of(ref, v, m):
        return jnp.where(row < HALO, ref[v, 2 * m], ref[v, 2 * m + 1])

    for m in range(packs):
        centre = [pack_of(far_own, v, m) for v in range(nvar)]
        weights = [
            [
                jnp.where(
                    row < HALO,
                    spectral_entry(2 * m - j - skip, 2 * ninst),
                    spectral_entry(2 * m + 1 - j - skip, 2 * ninst),
                )
                for j in range(ninst)
            ]
            for skip in (0, ninst)
        ]
        for u in range(nvar):
            z = sum(jac(1, u, v) * centre[v] for v in range(nvar))
            rest = z + 4.0 * VISCOUS * centre[u]
            for j in range(ninst):
                rest += weights[0][j] * far_own[u, j] + weights[1][j] * far_oth[u, j]
            at = lines_of(packs, u, m)
            rest_ref[at, :] = rest
            parts_ref[at, 0:axial] = z
            parts_ref[at, axial : 2 * axial] = centre[u]
    rest_ref[...] = rest_ref[...] - times(parts_ref[...], shift_ref[...])

    half = jnp.where(low, 0.5, -0.5)
    for m in range(packs):
        slope, around = [], []
        for v in range(nvar):
            c = pack_of(far_own, v, m)
            behind = shifted(c, 2)
            slope.append(half * (c - behind))
            around.append(c + behind)
        for u in range(nvar):
            at = lines_of(packs, u, m)
            r = shifted(rest_ref[at, :], 1) - VISCOUS * around[u]
            for v in range(nvar):
                r += jac(0, u, v) * slope[v]
            moved = [r, *(shifted(r, s) for s in range(1, SWEEPS + 1))]
            sums = [
                sum(spread_weight(j, SWEEPS - s) * moved[s] for s in range(j, SWEEPS + 1))
                for j in range(SWEEPS + 1)
            ]
            rest_ref[at, :] = sums[0]
            for j in range(1, SWEEPS + 1):
                terms_ref[at, (j - 1) * axial : j * axial] = sums[j]
    rest_ref[...] = rest_ref[...] + times(terms_ref[...], sweep_ref[...])

    step = step_ref[...]
    lane = lax.broadcasted_iota(jnp.int32, (ROWS, LANES), 1)
    reached = side >= HALO
    for n in range(ninst):
        for u in range(nvar):
            far = rest_ref[lines_of(packs, u, n // 2), :]
            turned = pltpu.roll(far, HALO, 0)
            stays = (1 - n % 2) == jnp.where(low, 0, 1)
            far = jnp.where(reached, jnp.where(stays, far, turned), 0.0)
            tiles = [far[:, t : t + LANES] for t in range(0, axial, LANES)]
            group = (u * ninst + n) * GROUP
            for plane_no, plane in enumerate(planes):
                tile, at = divmod(plane - SWEEPS, LANES)
                assert at + GROUP <= LANES
                start = group // LANES * LANES
                moved = pltpu.roll(
                    spread[plane_no][:, start : start + LANES], (at - group) % LANES, 1
                )
                inside = (lane >= at) & (lane < at + GROUP)
                tiles[tile] = tiles[tile] + jnp.where(inside, moved, 0.0)
            more = jnp.concatenate(tiles, axis=1)
            at = lines_of(ninst, u, n)
            out_ref[u, n] = base_ref[at, :] + more
            new_ref[u, n] = before_ref[at, :] - step * more


def here(array):
    return pltpu.with_memory_space_constraint(array, pltpu.VMEM)


def shards(flow_state, jac_pitch, jac_axial, pseudo_step, partner, iface_index):
    nvar, ninst, rows, axial = flow_state.shape
    spaces = lax.axis_size("space")
    planes = interface_planes(axial, IFACES)
    both = ("space", "inst")
    vmem = pl.BlockSpec(memory_space=pltpu.VMEM)
    smem = pl.BlockSpec(memory_space=pltpu.SMEM)
    anywhere = pl.BlockSpec(memory_space=pl.ANY)
    params = pltpu.CompilerParams(vmem_limit_bytes=VMEM_LIMIT)
    block = pltpu.VMEM(flow_state.shape, jnp.float32)
    cores = [(0, 1), (1, 0)]

    other = here(lax.ppermute(flow_state, "inst", cores))
    own, shift, sweep = pl.pallas_call(
        functools.partial(stage_kernel, planes),
        out_shape=(
            block,
            pltpu.VMEM((2 * axial, axial), jnp.bfloat16),
            pltpu.VMEM((SWEEPS * axial, axial), jnp.bfloat16),
        ),
        in_specs=[vmem],
        out_specs=(vmem,) * 3,
        compiler_params=params,
    )(flow_state)
    staged, own = own, here(own)
    line = pl.pallas_call(
        functools.partial(line_kernel, planes),
        out_shape=pltpu.VMEM((rows, LANES), jnp.float32),
        in_specs=[vmem, vmem],
        out_specs=vmem,
        compiler_params=params,
    )(own, other)

    lines, got = line, []
    for bit in round_bits(spaces):
        got.append(
            lax.ppermute(
                lines, both, [(2 * i + c, 2 * (i ^ (1 << bit)) + 1 - c) for i in range(spaces) for c in (0, 1)]
            )
        )
        parts = (lines, got[-1])
        lines = jnp.concatenate(parts, axis=0)

    edge = pl.pallas_call(
        edge_kernel,
        out_shape=block,
        in_specs=[vmem, vmem, anywhere],
        out_specs=vmem,
        compiler_params=params,
    )(own, other, line)
    pairs = []
    for i in range(spaces):
        odd = (i + 1) % spaces if i % 2 else (i - 1) % spaces
        pairs += [(2 * i, 2 * (i ^ 1)), (2 * i + 1, 2 * odd + 1)]
    near = lax.ppermute(edge, both, pairs)
    cut = nvar // 2
    far = [
        here(lax.ppermute(near[v : v + cut], "inst", cores)) for v in range(0, nvar, cut)
    ]

    step, local, jac, pick, mix = pl.pallas_call(
        functools.partial(prepare_kernel, planes, spaces),
        out_shape=(
            pltpu.VMEM(pseudo_step.shape, jnp.float32),
            block,
            pltpu.VMEM((2 * nvar * nvar, axial), jnp.float32),
            pltpu.VMEM((IFACES * 2 * rows, spaces * rows), jnp.float32),
            pltpu.VMEM((IFACES, LANES, 2 * LANES), jnp.float32),
        ),
        in_specs=[smem] * 4 + [vmem] * 3 + [anywhere],
        out_specs=(vmem,) * 5,
        compiler_params=params,
    )(jac_pitch, jac_axial, partner, iface_index, own, other, pseudo_step, got[0])

    lined = nvar * ninst * rows
    base = pl.pallas_call(
        functools.partial(near_kernel, planes),
        out_shape=pltpu.VMEM((lined, axial), jnp.float32),
        in_specs=[vmem] * 6,
        out_specs=vmem,
        scratch_shapes=[
            block,
            block,
            pltpu.VMEM((lined, 2 * axial), jnp.float32),
            pltpu.VMEM((lined, axial), jnp.float32),
            pltpu.VMEM((lined, SWEEPS * axial), jnp.float32),
        ],
        compiler_params=params,
    )(own, *[here(a) for a in (near, local, jac, shift, sweep)])

    before = (staged - step * base.reshape(staged.shape)).reshape(lined, axial)

    return pl.pallas_call(
        functools.partial(step_kernel, planes, len(far)),
        out_shape=(jax.ShapeDtypeStruct(flow_state.shape, jnp.float32),) * 2,
        in_specs=[vmem] * (10 + len(far)),
        out_specs=(vmem, vmem),
        scratch_shapes=[
            block,
            block,
            pltpu.VMEM((lined // 2, 2 * axial), jnp.float32),
            pltpu.VMEM((lined // 2, axial), jnp.float32),
            pltpu.VMEM((lined // 2, SWEEPS * axial), jnp.float32),
        ],
        compiler_params=params,
    )(here(before), here(base), *far, *[here(a) for a in (jac, shift, sweep, *parts, pick, mix, step)])


def solution(mesh):
    in_specs = (
        P("groups", "inst", "space", None),
        P("groups", None),
        P("groups", None),
        P("space", "groups"),
        P("groups", None),
        P("groups", "space"),
    )
    out_specs = (P("groups", "inst", "space", None), P("groups", "inst", "space", None))
    return jax.shard_map(shards, mesh=mesh, in_specs=in_specs, out_specs=out_specs, check_vma=False)
```

```python
import functools
import math

import jax
import jax.numpy as jnp
from jax import lax
from jax.experimental import pallas as pl
from jax.experimental.pallas import tpu as pltpu
from jax.sharding import PartitionSpec as P

IFACES = 2
SWEEPS = 3
VISCOUS = 0.25
SMOOTHING = 1.0
HALO = 4
ROWS = 8
LANES = 128
GROUP = 8
VMEM_LIMIT = 16 * 1024 * 1024


def spectral_entry(shift, instances):
    shift %= instances
    if shift == 0:
        return 0.0
    return 0.5 * (-1) ** shift / math.tan(math.pi * shift / instances)


def interface_planes(axial_cells, planes_count):
    return [(plane_no + 1) * axial_cells // (planes_count + 1) for plane_no in range(planes_count)]


def sweep_weights():
    k = SMOOTHING / (1.0 + 4.0 * SMOOTHING)
    base = 1.0 / (1.0 + 4.0 * SMOOTHING)
    return [base * k**m for m in range(SWEEPS)] + [k**SWEEPS]


def spread_weight(m, distance):
    weights = sweep_weights() + [0.0] * 4
    paths = {0: {0: 1, 2: 2}, 1: {1: 1, 3: 3}, 2: {2: 1}, 3: {3: 1}}[distance]
    return sum(count * math.comb(m + j, m) * weights[m + j] for j, count in paths.items())


def round_bits(spaces):
    bits = list(range(spaces.bit_length() - 1))
    return bits[:1] + bits[:0:-1]


def pack_lines(planes, field_ref, half, line):
    nvar, ninst = field_ref.shape[:2]
    lane = lax.broadcasted_iota(jnp.int32, (ROWS, LANES), 1)
    for plane_no, plane in enumerate(planes):
        for v in range(nvar):
            for n in range(ninst):
                at = (plane_no * nvar + v) * 2 * ninst + half * ninst + n
                cell = jnp.broadcast_to(field_ref[v, n, :, plane - 1 : plane], (ROWS, LANES))
                line = jnp.where(lane == at, cell, line)
    return line


def line_kernel(planes, half_ref, oth_ref, line_ref):
    ninst = oth_ref.shape[1]
    line = pack_lines(planes, oth_ref, 1, half_ref[...])
    lane = lax.broadcasted_iota(jnp.int32, (ROWS, LANES), 1)
    swapped = jnp.where(
        lax.rem(lane, 2 * ninst) < ninst,
        pltpu.roll(line, LANES - ninst, 1),
        pltpu.roll(line, ninst, 1),
    )
    line_ref[...] = jnp.where(lax.axis_index("inst") == 0, line, swapped)


def stage_kernel(planes, flow_ref, own_ref, half_ref, shift_ref, sweep_ref):
    own_ref[...] = flow_ref[...]
    half_ref[...] = pack_lines(planes, flow_ref, 0, jnp.zeros((ROWS, LANES), jnp.float32))
    axial = flow_ref.shape[3]
    source = lax.broadcasted_iota(jnp.int32, (axial, axial), 0)
    target = lax.broadcasted_iota(jnp.int32, (axial, axial), 1)
    ahead = target - source
    up, down = jnp.where(ahead == 1, 1.0, 0.0), jnp.where(ahead == -1, 1.0, 0.0)
    once = up + down
    for plane in planes:
        up = jnp.where(target == plane, 0.0, up)
    for plane in [*planes, axial]:
        down = jnp.where(target == plane - 1, jnp.where(ahead == 0, 1.0, 0.0), down)
    shift_ref[0:axial, :] = up.astype(jnp.bfloat16)
    shift_ref[axial : 2 * axial, :] = (VISCOUS * (up + down)).astype(jnp.bfloat16)
    far, edges = jnp.abs(ahead), source + target
    corner = (edges == 0) | (edges == 2 * axial - 2)
    beside = (edges == 1) | (edges == 2 * axial - 3)
    twice = jnp.where(far == 2, 1.0, jnp.where(far == 0, jnp.where(corner, 1.0, 2.0), 0.0))
    thrice = jnp.where(far == 3, 1.0, jnp.where(far == 1, jnp.where(beside, 2.0, 3.0), 0.0))
    for power, value in enumerate((once, twice, thrice)):
        sweep_ref[power * axial : (power + 1) * axial, :] = value.astype(jnp.bfloat16)


def low_side():
    return lax.rem(lax.axis_index("space") + lax.axis_index("inst"), 2) == 1


def edge_kernel(own_ref, oth_ref, after_ref, edge_ref):
    del after_ref
    core = lax.axis_index("inst")
    low = low_side()
    nvar, ninst, _, axial = own_ref.shape
    row = lax.broadcasted_iota(jnp.int32, (ROWS, axial), 0)
    for v in range(nvar):
        for n in range(ninst):
            own, oth = own_ref[v, n], oth_ref[v, n]
            first = jnp.where(core == 0, own, oth)
            second = jnp.where(core == 0, oth, own)
            low_rows = jnp.where(row < HALO, first, pltpu.roll(second, HALO, 0))
            high_rows = jnp.where(row < HALO, pltpu.roll(first, HALO, 0), second)
            edge_ref[v, n] = jnp.where(low, low_rows, high_rows)


def local_terms(planes, jac, own, oth, n):
    nvar, ninst, rows, axial = own.shape
    lane = lax.broadcasted_iota(jnp.int32, (rows, axial), 1)
    inward, spread = [], []
    for v in range(nvar):
        c = own[v, n]
        up, down = pltpu.roll(c, 1, 1), pltpu.roll(c, axial - 1, 1)
        for plane in [0, *planes]:
            up = jnp.where(lane == plane, 0.0, up)
        for plane in [*planes, axial]:
            down = jnp.where(lane == plane - 1, c, down)
        inward.append(c - up)
        spread.append(up + down - 4.0 * c)
    terms = []
    for u in range(nvar):
        total = -VISCOUS * spread[u]
        for v in range(nvar):
            total += jac(u, v) * inward[v]
        for j in range(ninst):
            if j != n:
                total += spectral_entry(n - j, 2 * ninst) * own[u, j]
            total += spectral_entry(n - j - ninst, 2 * ninst) * oth[u, j]
        terms.append(total)
    return terms


def prepare_kernel(
    planes,
    spaces,
    jac_pitch_ref,
    jac_axial_ref,
    partner_ref,
    index_ref,
    own_ref,
    oth_ref,
    step_in_ref,
    after_ref,
    step_ref,
    local_ref,
    jac_ref,
    pick_ref,
    mix_ref,
):
    del after_ref
    step_ref[...] = step_in_ref[...]
    core, space = lax.axis_index("inst"), lax.axis_index("space")
    nvar, ninst, _, axial = own_ref.shape
    for n in range(ninst):
        terms = local_terms(planes, lambda u, v: jac_axial_ref[u, v], own_ref, oth_ref, n)
        for u in range(nvar):
            local_ref[u, n] = terms[u]
    for which, ref in enumerate((jac_pitch_ref, jac_axial_ref)):
        for u in range(nvar):
            for v in range(nvar):
                at = (which * nvar + u) * nvar + v
                jac_ref[at : at + 1, :] = jnp.full((1, axial), ref[u, v], jnp.float32)

    total = spaces * ROWS
    row = lax.broadcasted_iota(jnp.int32, (2 * ROWS, total), 0)
    ahead = jnp.where(row < ROWS + HALO, row, row - 2 * ROWS)
    lane = lax.broadcasted_iota(jnp.int32, (2 * ROWS, total), 1)
    for plane_no in range(len(planes)):
        pitch = index_ref[plane_no, 0] + ahead
        pitch = jnp.where(pitch < 0, pitch + total, pitch)
        pitch = jnp.where(pitch >= total, pitch - total, pitch)
        apart = (pitch >> 3) ^ space
        place = pitch & 7
        for turn, bit in enumerate(round_bits(spaces)):
            place += ((apart >> bit) & 1) << (turn + 3)
        pick_ref[pl.ds(plane_no * 2 * ROWS, 2 * ROWS), :] = jnp.where(lane == place, 1.0, 0.0)

    lane = lax.broadcasted_iota(jnp.int32, (ROWS, 2 * LANES), 1) // GROUP
    row = lax.broadcasted_iota(jnp.int32, (ROWS, 2 * LANES), 0)
    to_var, to_inst = lane // ninst, lax.rem(lane, ninst) + ninst * core
    mix_ref[...] = jnp.zeros(mix_ref.shape, jnp.float32)
    for v in range(nvar):
        block = jnp.zeros((ROWS, 2 * LANES), jnp.float32)
        for u in range(nvar):
            value = -jac_axial_ref[u, v] - (VISCOUS if u == v else 0.0)
            block = jnp.where(to_var == u, value, block)
        for plane_no in range(len(planes)):
            source = lax.rem(to_inst + partner_ref[plane_no, 0], 2 * ninst)
            at = (plane_no * nvar + v) * 2 * ninst
            mix_ref[plane_no, at : at + ROWS, :] = jnp.where(row == source, block, 0.0)


def times(left, right):
    first = left.astype(jnp.bfloat16)
    second = (left - first.astype(jnp.float32)).astype(jnp.bfloat16)
    return jnp.dot(first, right, preferred_element_type=jnp.float32) + jnp.dot(
        second, right, preferred_element_type=jnp.float32
    )


def inflow_spread(planes, lines_refs, pick_ref, mix_ref):
    exact = dict(precision=lax.Precision.HIGHEST, preferred_element_type=jnp.float32)
    lines = jnp.concatenate([ref[...] for ref in lines_refs], axis=0)
    facing = jnp.dot(pick_ref[...], lines, **exact)
    lane = lax.rem(lax.broadcasted_iota(jnp.int32, (ROWS, 2 * LANES), 1), GROUP)
    spread = []
    for plane_no in range(len(planes)):
        power = jnp.dot(
            facing[plane_no * 2 * ROWS : (plane_no + 1) * 2 * ROWS], mix_ref[plane_no], **exact
        )
        total = jnp.zeros((ROWS, 2 * LANES), jnp.float32)
        for m in range(SWEEPS + 1):
            weight = jnp.zeros((ROWS, 2 * LANES), jnp.float32)
            for d in range(-SWEEPS, SWEEPS + 1):
                weight = jnp.where(lane == d + SWEEPS, spread_weight(m, abs(d)), weight)
            total += weight * power[0:ROWS]
            if m < SWEEPS:
                power = pltpu.roll(power, 2 * ROWS - 1, 0) + pltpu.roll(power, 1, 0)
        spread.append(total)
    return spread


def jac_row(jac_ref, nvar, which, u, v):
    at = (which * nvar + u) * nvar + v
    return jac_ref[at : at + 1, :]


def lines_of(ninst, u, n):
    at = (u * ninst + n) * ROWS
    return slice(at, at + ROWS)


def near_kernel(planes, *refs):
    own_ref, near_ref, local_ref, jac_ref, shift_ref, sweep_ref, base_ref, *refs = refs
    halo_own, halo_oth, parts_ref, rest_ref, terms_ref = refs
    core = lax.axis_index("inst")
    low = low_side()
    nvar, ninst, _, axial = own_ref.shape
    row = lax.broadcasted_iota(jnp.int32, (ROWS, axial), 0)
    keep = jnp.where(low, row, ROWS - 1 - row) >= HALO
    for v in range(nvar):
        for n in range(ninst):
            near = near_ref[v, n]
            turned = pltpu.roll(near, HALO, 0)
            first = jnp.where(keep, jnp.where(low, turned, near), 0.0)
            second = jnp.where(keep, jnp.where(low, near, turned), 0.0)
            halo_own[v, n] = jnp.where(core == 0, first, second)
            halo_oth[v, n] = jnp.where(core == 0, second, first)
    jac = functools.partial(jac_row, jac_ref, nvar)

    for n in range(ninst):
        centre = [halo_own[v, n] for v in range(nvar)]
        for u in range(nvar):
            z = sum(jac(1, u, v) * centre[v] for v in range(nvar))
            rest = z + 4.0 * VISCOUS * centre[u]
            for j in range(ninst):
                if j != n:
                    rest += spectral_entry(n - j, 2 * ninst) * halo_own[u, j]
                rest += spectral_entry(n - j - ninst, 2 * ninst) * halo_oth[u, j]
            at = lines_of(ninst, u, n)
            rest_ref[at, :] = rest
            parts_ref[at, 0:axial] = z
            parts_ref[at, axial : 2 * axial] = centre[u]
    rest_ref[...] = rest_ref[...] - times(parts_ref[...], shift_ref[...])

    c0, c1, c2, c3 = sweep_weights()
    for n in range(ninst):
        slope, around = [], []
        for v in range(nvar):
            c = jnp.concatenate([own_ref[v, n], halo_own[v, n]], axis=0)
            nxt, prv = pltpu.roll(c, 2 * ROWS - 1, 0), pltpu.roll(c, 1, 0)
            slope.append(0.5 * (nxt - prv))
            around.append(nxt + prv)
        for u in range(nvar):
            at = lines_of(ninst, u, n)
            r0 = jnp.concatenate([local_ref[u, n], rest_ref[at, :]], axis=0) - VISCOUS * around[u]
            for v in range(nvar):
                r0 += jac(0, u, v) * slope[v]
            r1 = pltpu.roll(r0, 2 * ROWS - 1, 0) + pltpu.roll(r0, 1, 0)
            r2 = pltpu.roll(r1, 2 * ROWS - 1, 0) + pltpu.roll(r1, 1, 0)
            r3 = pltpu.roll(r2, 2 * ROWS - 1, 0) + pltpu.roll(r2, 1, 0)
            r0, r1, r2, r3 = (r[0:ROWS] for r in (r0, r1, r2, r3))
            base_ref[at, :] = c0 * r0 + c1 * r1 + c2 * r2 + c3 * r3
            terms_ref[at, 0:axial] = c1 * r0 + 2.0 * c2 * r1 + 3.0 * c3 * r2
            terms_ref[at, axial : 2 * axial] = c2 * r0 + 3.0 * c3 * r1
            terms_ref[at, 2 * axial : 3 * axial] = c3 * r0
    base_ref[...] = base_ref[...] + times(terms_ref[...], sweep_ref[...])


def step_kernel(planes, cuts, *refs):
    before_ref, base_ref, *refs = refs
    far_refs, refs = refs[:cuts], refs[cuts:]
    jac_ref, shift_ref, sweep_ref, *lines_refs, pick_ref, mix_ref, step_ref = refs[:8]
    new_ref, out_ref, far_own, far_oth, parts_ref, rest_ref, terms_ref = refs[8:]
    core = lax.axis_index("inst")
    low = low_side()
    nvar, ninst, _, axial = new_ref.shape
    cut, packs = nvar // cuts, ninst // 2
    row = lax.broadcasted_iota(jnp.int32, (ROWS, axial), 0)
    side = jnp.where(low, row, ROWS - 1 - row)
    depth = side & (HALO - 1)
    spread = inflow_spread(planes, lines_refs, pick_ref, mix_ref)
    jac = functools.partial(jac_row, jac_ref, nvar)

    def shifted(tile, s):
        moved = pltpu.roll(tile, jnp.where(low, s, ROWS - s), 0)
        return jnp.where(depth >= s, moved, 0.0)

    for v in range(nvar):
        for n in range(ninst):
            tile = far_refs[v // cut][v % cut, n]
            turned = pltpu.roll(tile, HALO, 0)
            first = jnp.where(row < HALO, tile, turned)
            second = jnp.where(row < HALO, turned, tile)
            far_own[v, n] = jnp.where(core == 0, first, second)
            far_oth[v, n] = jnp.where(core == 0, second, first)

    def pack_of(ref, v, m):
        return jnp.where(row < HALO, ref[v, 2 * m], ref[v, 2 * m + 1])

    for m in range(packs):
        centre = [pack_of(far_own, v, m) for v in range(nvar)]
        weights = [
            [
                jnp.where(
                    row < HALO,
                    spectral_entry(2 * m - j - skip, 2 * ninst),
                    spectral_entry(2 * m + 1 - j - skip, 2 * ninst),
                )
                for j in range(ninst)
            ]
            for skip in (0, ninst)
        ]
        for u in range(nvar):
            z = sum(jac(1, u, v) * centre[v] for v in range(nvar))
            rest = z + 4.0 * VISCOUS * centre[u]
            for j in range(ninst):
                rest += weights[0][j] * far_own[u, j] + weights[1][j] * far_oth[u, j]
            at = lines_of(packs, u, m)
            rest_ref[at, :] = rest
            parts_ref[at, 0:axial] = z
            parts_ref[at, axial : 2 * axial] = centre[u]
    rest_ref[...] = rest_ref[...] - times(parts_ref[...], shift_ref[...])

    half = jnp.where(low, 0.5, -0.5)
    for m in range(packs):
        slope, around = [], []
        for v in range(nvar):
            c = pack_of(far_own, v, m)
            behind = shifted(c, 2)
            slope.append(half * (c - behind))
            around.append(c + behind)
        for u in range(nvar):
            at = lines_of(packs, u, m)
            r = shifted(rest_ref[at, :], 1) - VISCOUS * around[u]
            for v in range(nvar):
                r += jac(0, u, v) * slope[v]
            moved = [r, *(shifted(r, s) for s in range(1, SWEEPS + 1))]
            sums = [
                sum(spread_weight(j, SWEEPS - s) * moved[s] for s in range(j, SWEEPS + 1))
                for j in range(SWEEPS + 1)
            ]
            rest_ref[at, :] = sums[0]
            for j in range(1, SWEEPS + 1):
                terms_ref[at, (j - 1) * axial : j * axial] = sums[j]
    rest_ref[...] = rest_ref[...] + times(terms_ref[...], sweep_ref[...])

    step = step_ref[...]
    lane = lax.broadcasted_iota(jnp.int32, (ROWS, LANES), 1)
    reached = side >= HALO
    for n in range(ninst):
        for u in range(nvar):
            far = rest_ref[lines_of(packs, u, n // 2), :]
            turned = pltpu.roll(far, HALO, 0)
            stays = (1 - n % 2) == jnp.where(low, 0, 1)
            far = jnp.where(reached, jnp.where(stays, far, turned), 0.0)
            tiles = [far[:, t : t + LANES] for t in range(0, axial, LANES)]
            group = (u * ninst + n) * GROUP
            for plane_no, plane in enumerate(planes):
                tile, at = divmod(plane - SWEEPS, LANES)
                assert at + GROUP <= LANES
                start = group // LANES * LANES
                moved = pltpu.roll(
                    spread[plane_no][:, start : start + LANES], (at - group) % LANES, 1
                )
                inside = (lane >= at) & (lane < at + GROUP)
                tiles[tile] = tiles[tile] + jnp.where(inside, moved, 0.0)
            more = jnp.concatenate(tiles, axis=1)
            at = lines_of(ninst, u, n)
            out_ref[u, n] = base_ref[at, :] + more
            new_ref[u, n] = before_ref[at, :] - step * more


def here(array):
    return pltpu.with_memory_space_constraint(array, pltpu.VMEM)


def shards(flow_state, jac_pitch, jac_axial, pseudo_step, partner, iface_index):
    nvar, ninst, rows, axial = flow_state.shape
    spaces = lax.axis_size("space")
    planes = interface_planes(axial, IFACES)
    both = ("space", "inst")
    vmem = pl.BlockSpec(memory_space=pltpu.VMEM)
    smem = pl.BlockSpec(memory_space=pltpu.SMEM)
    anywhere = pl.BlockSpec(memory_space=pl.ANY)
    params = pltpu.CompilerParams(vmem_limit_bytes=VMEM_LIMIT)
    block = pltpu.VMEM(flow_state.shape, jnp.float32)
    cores = [(0, 1), (1, 0)]

    other = here(lax.ppermute(flow_state, "inst", cores))
    own, half, shift, sweep = pl.pallas_call(
        functools.partial(stage_kernel, planes),
        out_shape=(
            block,
            pltpu.VMEM((rows, LANES), jnp.float32),
            pltpu.VMEM((2 * axial, axial), jnp.bfloat16),
            pltpu.VMEM((SWEEPS * axial, axial), jnp.bfloat16),
        ),
        in_specs=[vmem],
        out_specs=(vmem,) * 4,
        compiler_params=params,
    )(flow_state)
    staged, own = own, here(own)
    line = pl.pallas_call(
        functools.partial(line_kernel, planes),
        out_shape=pltpu.VMEM((rows, LANES), jnp.float32),
        in_specs=[vmem, vmem],
        out_specs=vmem,
        compiler_params=params,
    )(here(half), other)

    lines, got = line, []
    for bit in round_bits(spaces):
        got.append(
            lax.ppermute(
                lines, both, [(2 * i + c, 2 * (i ^ (1 << bit)) + 1 - c) for i in range(spaces) for c in (0, 1)]
            )
        )
        parts = (lines, got[-1])
        lines = jnp.concatenate(parts, axis=0)

    edge = pl.pallas_call(
        edge_kernel,
        out_shape=block,
        in_specs=[vmem, vmem, anywhere],
        out_specs=vmem,
        compiler_params=params,
    )(own, other, line)
    pairs = []
    for i in range(spaces):
        odd = (i + 1) % spaces if i % 2 else (i - 1) % spaces
        pairs += [(2 * i, 2 * (i ^ 1)), (2 * i + 1, 2 * odd + 1)]
    near = lax.ppermute(edge, both, pairs)
    cut = nvar // 2
    far = [
        here(lax.ppermute(near[v : v + cut], "inst", cores)) for v in range(0, nvar, cut)
    ]

    step, local, jac, pick, mix = pl.pallas_call(
        functools.partial(prepare_kernel, planes, spaces),
        out_shape=(
            pltpu.VMEM(pseudo_step.shape, jnp.float32),
            block,
            pltpu.VMEM((2 * nvar * nvar, axial), jnp.float32),
            pltpu.VMEM((IFACES * 2 * rows, spaces * rows), jnp.float32),
            pltpu.VMEM((IFACES, LANES, 2 * LANES), jnp.float32),
        ),
        in_specs=[smem] * 4 + [vmem] * 3 + [anywhere],
        out_specs=(vmem,) * 5,
        compiler_params=params,
    )(jac_pitch, jac_axial, partner, iface_index, own, other, pseudo_step, got[0])

    lined = nvar * ninst * rows
    base = pl.pallas_call(
        functools.partial(near_kernel, planes),
        out_shape=pltpu.VMEM((lined, axial), jnp.float32),
        in_specs=[vmem] * 6,
        out_specs=vmem,
        scratch_shapes=[
            block,
            block,
            pltpu.VMEM((lined, 2 * axial), jnp.float32),
            pltpu.VMEM((lined, axial), jnp.float32),
            pltpu.VMEM((lined, SWEEPS * axial), jnp.float32),
        ],
        compiler_params=params,
    )(own, *[here(a) for a in (near, local, jac, shift, sweep)])

    before = (staged - step * base.reshape(staged.shape)).reshape(lined, axial)

    return pl.pallas_call(
        functools.partial(step_kernel, planes, len(far)),
        out_shape=(jax.ShapeDtypeStruct(flow_state.shape, jnp.float32),) * 2,
        in_specs=[vmem] * (10 + len(far)),
        out_specs=(vmem, vmem),
        scratch_shapes=[
            block,
            block,
            pltpu.VMEM((lined // 2, 2 * axial), jnp.float32),
            pltpu.VMEM((lined // 2, axial), jnp.float32),
            pltpu.VMEM((lined // 2, SWEEPS * axial), jnp.float32),
        ],
        compiler_params=params,
    )(here(before), here(base), *far, *[here(a) for a in (jac, shift, sweep, *parts, pick, mix, step)])


def solution(mesh):
    in_specs = (
        P("groups", "inst", "space", None),
        P("groups", None),
        P("groups", None),
        P("space", "groups"),
        P("groups", None),
        P("groups", "space"),
    )
    out_specs = (P("groups", "inst", "space", None), P("groups", "inst", "space", None))
    return jax.shard_map(shards, mesh=mesh, in_specs=in_specs, out_specs=out_specs, check_vma=False)
```

```python
import functools
import math

import jax
import jax.numpy as jnp
from jax import lax
from jax.experimental import pallas as pl
from jax.experimental.pallas import tpu as pltpu
from jax.sharding import PartitionSpec as P

IFACES = 2
SWEEPS = 3
VISCOUS = 0.25
SMOOTHING = 1.0
HALO = 4
ROWS = 8
LANES = 128
GROUP = 8
VMEM_LIMIT = 16 * 1024 * 1024


def spectral_entry(shift, instances):
    shift %= instances
    if shift == 0:
        return 0.0
    return 0.5 * (-1) ** shift / math.tan(math.pi * shift / instances)


def interface_planes(axial_cells, planes_count):
    return [(plane_no + 1) * axial_cells // (planes_count + 1) for plane_no in range(planes_count)]


def sweep_weights():
    k = SMOOTHING / (1.0 + 4.0 * SMOOTHING)
    base = 1.0 / (1.0 + 4.0 * SMOOTHING)
    return [base * k**m for m in range(SWEEPS)] + [k**SWEEPS]


def spread_weight(m, distance):
    weights = sweep_weights() + [0.0] * 4
    paths = {0: {0: 1, 2: 2}, 1: {1: 1, 3: 3}, 2: {2: 1}, 3: {3: 1}}[distance]
    return sum(count * math.comb(m + j, m) * weights[m + j] for j, count in paths.items())


def round_bits(spaces):
    bits = list(range(spaces.bit_length() - 1))
    return bits[:1] + bits[:0:-1]


def pack_lines(planes, field_ref, half, line):
    nvar, ninst = field_ref.shape[:2]
    lane = lax.broadcasted_iota(jnp.int32, (ROWS, LANES), 1)
    for plane_no, plane in enumerate(planes):
        for v in range(nvar):
            for n in range(ninst):
                at = (plane_no * nvar + v) * 2 * ninst + half * ninst + n
                cell = jnp.broadcast_to(field_ref[v, n, :, plane - 1 : plane], (ROWS, LANES))
                line = jnp.where(lane == at, cell, line)
    return line


def line_kernel(planes, half_ref, oth_ref, line_ref):
    ninst = oth_ref.shape[1]
    line = pack_lines(planes, oth_ref, 1, half_ref[...])
    lane = lax.broadcasted_iota(jnp.int32, (ROWS, LANES), 1)
    swapped = jnp.where(
        lax.rem(lane, 2 * ninst) < ninst,
        pltpu.roll(line, LANES - ninst, 1),
        pltpu.roll(line, ninst, 1),
    )
    line_ref[...] = jnp.where(lax.axis_index("inst") == 0, line, swapped)


def stage_kernel(planes, flow_ref, own_ref, half_ref, shift_ref, sweep_ref):
    own_ref[...] = flow_ref[...]
    half_ref[...] = pack_lines(planes, flow_ref, 0, jnp.zeros((ROWS, LANES), jnp.float32))
    axial = flow_ref.shape[3]
    source = lax.broadcasted_iota(jnp.int32, (axial, axial), 0)
    target = lax.broadcasted_iota(jnp.int32, (axial, axial), 1)
    ahead = target - source
    up, down = jnp.where(ahead == 1, 1.0, 0.0), jnp.where(ahead == -1, 1.0, 0.0)
    once = up + down
    for plane in planes:
        up = jnp.where(target == plane, 0.0, up)
    for plane in [*planes, axial]:
        down = jnp.where(target == plane - 1, jnp.where(ahead == 0, 1.0, 0.0), down)
    shift_ref[0:axial, :] = up.astype(jnp.bfloat16)
    shift_ref[axial : 2 * axial, :] = (VISCOUS * (up + down)).astype(jnp.bfloat16)
    far, edges = jnp.abs(ahead), source + target
    corner = (edges == 0) | (edges == 2 * axial - 2)
    beside = (edges == 1) | (edges == 2 * axial - 3)
    twice = jnp.where(far == 2, 1.0, jnp.where(far == 0, jnp.where(corner, 1.0, 2.0), 0.0))
    thrice = jnp.where(far == 3, 1.0, jnp.where(far == 1, jnp.where(beside, 2.0, 3.0), 0.0))
    for power, value in enumerate((once, twice, thrice)):
        sweep_ref[power * axial : (power + 1) * axial, :] = value.astype(jnp.bfloat16)


def low_side():
    return lax.rem(lax.axis_index("space") + lax.axis_index("inst"), 2) == 1


def edge_kernel(own_ref, oth_ref, after_ref, edge_ref):
    del after_ref
    core = lax.axis_index("inst")
    low = low_side()
    nvar, ninst, _, axial = own_ref.shape
    row = lax.broadcasted_iota(jnp.int32, (ROWS, axial), 0)
    for v in range(nvar):
        for n in range(ninst):
            own, oth = own_ref[v, n], oth_ref[v, n]
            first = jnp.where(core == 0, own, oth)
            second = jnp.where(core == 0, oth, own)
            low_rows = jnp.where(row < HALO, first, pltpu.roll(second, HALO, 0))
            high_rows = jnp.where(row < HALO, pltpu.roll(first, HALO, 0), second)
            edge_ref[v, n] = jnp.where(low, low_rows, high_rows)


def local_terms(planes, jac, own, oth, n):
    nvar, ninst, rows, axial = own.shape
    lane = lax.broadcasted_iota(jnp.int32, (rows, axial), 1)
    inward, spread = [], []
    for v in range(nvar):
        c = own[v, n]
        up, down = pltpu.roll(c, 1, 1), pltpu.roll(c, axial - 1, 1)
        for plane in [0, *planes]:
            up = jnp.where(lane == plane, 0.0, up)
        for plane in [*planes, axial]:
            down = jnp.where(lane == plane - 1, c, down)
        inward.append(c - up)
        spread.append(up + down - 4.0 * c)
    terms = []
    for u in range(nvar):
        total = -VISCOUS * spread[u]
        for v in range(nvar):
            total += jac(u, v) * inward[v]
        for j in range(ninst):
            if j != n:
                total += spectral_entry(n - j, 2 * ninst) * own[u, j]
            total += spectral_entry(n - j - ninst, 2 * ninst) * oth[u, j]
        terms.append(total)
    return terms


def prepare_kernel(
    planes,
    spaces,
    jac_pitch_ref,
    jac_axial_ref,
    partner_ref,
    index_ref,
    own_ref,
    oth_ref,
    step_in_ref,
    after_ref,
    step_ref,
    local_ref,
    jac_ref,
    pick_ref,
    mix_ref,
):
    del after_ref
    step_ref[...] = step_in_ref[...]
    core, space = lax.axis_index("inst"), lax.axis_index("space")
    nvar, ninst, _, axial = own_ref.shape
    for n in range(ninst):
        terms = local_terms(planes, lambda u, v: jac_axial_ref[u, v], own_ref, oth_ref, n)
        for u in range(nvar):
            local_ref[u, n] = terms[u]
    for which, ref in enumerate((jac_pitch_ref, jac_axial_ref)):
        for u in range(nvar):
            for v in range(nvar):
                at = (which * nvar + u) * nvar + v
                jac_ref[at : at + 1, :] = jnp.full((1, axial), ref[u, v], jnp.float32)

    total = spaces * ROWS
    row = lax.broadcasted_iota(jnp.int32, (2 * ROWS, total), 0)
    ahead = jnp.where(row < ROWS + HALO, row, row - 2 * ROWS)
    lane = lax.broadcasted_iota(jnp.int32, (2 * ROWS, total), 1)
    for plane_no in range(len(planes)):
        pitch = index_ref[plane_no, 0] + ahead
        pitch = jnp.where(pitch < 0, pitch + total, pitch)
        pitch = jnp.where(pitch >= total, pitch - total, pitch)
        apart = (pitch >> 3) ^ space
        place = pitch & 7
        for turn, bit in enumerate(round_bits(spaces)):
            place += ((apart >> bit) & 1) << (turn + 3)
        pick_ref[pl.ds(plane_no * 2 * ROWS, 2 * ROWS), :] = jnp.where(lane == place, 1.0, 0.0)

    lane = lax.broadcasted_iota(jnp.int32, (ROWS, 2 * LANES), 1) // GROUP
    row = lax.broadcasted_iota(jnp.int32, (ROWS, 2 * LANES), 0)
    to_var, to_inst = lane // ninst, lax.rem(lane, ninst) + ninst * core
    mix_ref[...] = jnp.zeros(mix_ref.shape, jnp.float32)
    for v in range(nvar):
        block = jnp.zeros((ROWS, 2 * LANES), jnp.float32)
        for u in range(nvar):
            value = -jac_axial_ref[u, v] - (VISCOUS if u == v else 0.0)
            block = jnp.where(to_var == u, value, block)
        for plane_no in range(len(planes)):
            source = lax.rem(to_inst + partner_ref[plane_no, 0], 2 * ninst)
            at = (plane_no * nvar + v) * 2 * ninst
            mix_ref[plane_no, at : at + ROWS, :] = jnp.where(row == source, block, 0.0)


def times(left, right):
    first = left.astype(jnp.bfloat16)
    second = (left - first.astype(jnp.float32)).astype(jnp.bfloat16)
    return jnp.dot(first, right, preferred_element_type=jnp.float32) + jnp.dot(
        second, right, preferred_element_type=jnp.float32
    )


def inflow_spread(planes, lines_refs, pick_ref, mix_ref):
    lines = jnp.concatenate([ref[...] for ref in lines_refs], axis=0)
    pick, first = pick_ref[...].astype(jnp.bfloat16), lines.astype(jnp.bfloat16)
    second = (lines - first.astype(jnp.float32)).astype(jnp.bfloat16)
    plain = dict(preferred_element_type=jnp.float32)
    facing = jnp.dot(pick, first, **plain) + jnp.dot(pick, second, **plain)
    lane = lax.rem(lax.broadcasted_iota(jnp.int32, (ROWS, 2 * LANES), 1), GROUP)
    spread = []
    for plane_no in range(len(planes)):
        seen = facing[plane_no * 2 * ROWS : (plane_no + 1) * 2 * ROWS]
        seen_first, mix_first = seen.astype(jnp.bfloat16), mix_ref[plane_no].astype(jnp.bfloat16)
        seen_second = (seen - seen_first.astype(jnp.float32)).astype(jnp.bfloat16)
        mix_second = (mix_ref[plane_no] - mix_first.astype(jnp.float32)).astype(jnp.bfloat16)
        power = jnp.dot(seen_first, mix_first, **plain)
        power += jnp.dot(seen_second, mix_first, **plain) + jnp.dot(seen_first, mix_second, **plain)
        total = jnp.zeros((ROWS, 2 * LANES), jnp.float32)
        for m in range(SWEEPS + 1):
            weight = jnp.zeros((ROWS, 2 * LANES), jnp.float32)
            for d in range(-SWEEPS, SWEEPS + 1):
                weight = jnp.where(lane == d + SWEEPS, spread_weight(m, abs(d)), weight)
            total += weight * power[0:ROWS]
            if m < SWEEPS:
                power = pltpu.roll(power, 2 * ROWS - 1, 0) + pltpu.roll(power, 1, 0)
        spread.append(total)
    return spread


def jac_row(jac_ref, nvar, which, u, v):
    at = (which * nvar + u) * nvar + v
    return jac_ref[at : at + 1, :]


def lines_of(ninst, u, n):
    at = (u * ninst + n) * ROWS
    return slice(at, at + ROWS)


def near_kernel(planes, *refs):
    own_ref, near_ref, local_ref, jac_ref, shift_ref, sweep_ref, base_ref, *refs = refs
    halo_own, halo_oth, parts_ref, rest_ref, terms_ref = refs
    core = lax.axis_index("inst")
    low = low_side()
    nvar, ninst, _, axial = own_ref.shape
    row = lax.broadcasted_iota(jnp.int32, (ROWS, axial), 0)
    keep = jnp.where(low, row, ROWS - 1 - row) >= HALO
    for v in range(nvar):
        for n in range(ninst):
            near = near_ref[v, n]
            turned = pltpu.roll(near, HALO, 0)
            first = jnp.where(keep, jnp.where(low, turned, near), 0.0)
            second = jnp.where(keep, jnp.where(low, near, turned), 0.0)
            halo_own[v, n] = jnp.where(core == 0, first, second)
            halo_oth[v, n] = jnp.where(core == 0, second, first)
    jac = functools.partial(jac_row, jac_ref, nvar)

    for n in range(ninst):
        centre = [halo_own[v, n] for v in range(nvar)]
        for u in range(nvar):
            z = sum(jac(1, u, v) * centre[v] for v in range(nvar))
            rest = z + 4.0 * VISCOUS * centre[u]
            for j in range(ninst):
                if j != n:
                    rest += spectral_entry(n - j, 2 * ninst) * halo_own[u, j]
                rest += spectral_entry(n - j - ninst, 2 * ninst) * halo_oth[u, j]
            at = lines_of(ninst, u, n)
            rest_ref[at, :] = rest
            parts_ref[at, 0:axial] = z
            parts_ref[at, axial : 2 * axial] = centre[u]
    rest_ref[...] = rest_ref[...] - times(parts_ref[...], shift_ref[...])

    c0, c1, c2, c3 = sweep_weights()
    for n in range(ninst):
        slope, around = [], []
        for v in range(nvar):
            c = jnp.concatenate([own_ref[v, n], halo_own[v, n]], axis=0)
            nxt, prv = pltpu.roll(c, 2 * ROWS - 1, 0), pltpu.roll(c, 1, 0)
            slope.append(0.5 * (nxt - prv))
            around.append(nxt + prv)
        for u in range(nvar):
            at = lines_of(ninst, u, n)
            r0 = jnp.concatenate([local_ref[u, n], rest_ref[at, :]], axis=0) - VISCOUS * around[u]
            for v in range(nvar):
                r0 += jac(0, u, v) * slope[v]
            r1 = pltpu.roll(r0, 2 * ROWS - 1, 0) + pltpu.roll(r0, 1, 0)
            r2 = pltpu.roll(r1, 2 * ROWS - 1, 0) + pltpu.roll(r1, 1, 0)
            r3 = pltpu.roll(r2, 2 * ROWS - 1, 0) + pltpu.roll(r2, 1, 0)
            r0, r1, r2, r3 = (r[0:ROWS] for r in (r0, r1, r2, r3))
            base_ref[at, :] = c0 * r0 + c1 * r1 + c2 * r2 + c3 * r3
            terms_ref[at, 0:axial] = c1 * r0 + 2.0 * c2 * r1 + 3.0 * c3 * r2
            terms_ref[at, axial : 2 * axial] = c2 * r0 + 3.0 * c3 * r1
            terms_ref[at, 2 * axial : 3 * axial] = c3 * r0
    base_ref[...] = base_ref[...] + times(terms_ref[...], sweep_ref[...])


def step_kernel(planes, cuts, *refs):
    before_ref, base_ref, *refs = refs
    far_refs, refs = refs[:cuts], refs[cuts:]
    jac_ref, shift_ref, sweep_ref, *lines_refs, pick_ref, mix_ref, step_ref = refs[:8]
    new_ref, out_ref, far_own, far_oth, parts_ref, rest_ref, terms_ref = refs[8:]
    core = lax.axis_index("inst")
    low = low_side()
    nvar, ninst, _, axial = new_ref.shape
    cut, packs = nvar // cuts, ninst // 2
    row = lax.broadcasted_iota(jnp.int32, (ROWS, axial), 0)
    side = jnp.where(low, row, ROWS - 1 - row)
    depth = side & (HALO - 1)
    spread = inflow_spread(planes, lines_refs, pick_ref, mix_ref)
    jac = functools.partial(jac_row, jac_ref, nvar)

    def shifted(tile, s):
        moved = pltpu.roll(tile, jnp.where(low, s, ROWS - s), 0)
        return jnp.where(depth >= s, moved, 0.0)

    for v in range(nvar):
        for n in range(ninst):
            tile = far_refs[v // cut][v % cut, n]
            turned = pltpu.roll(tile, HALO, 0)
            first = jnp.where(row < HALO, tile, turned)
            second = jnp.where(row < HALO, turned, tile)
            far_own[v, n] = jnp.where(core == 0, first, second)
            far_oth[v, n] = jnp.where(core == 0, second, first)

    def pack_of(ref, v, m):
        return jnp.where(row < HALO, ref[v, 2 * m], ref[v, 2 * m + 1])

    for m in range(packs):
        centre = [pack_of(far_own, v, m) for v in range(nvar)]
        weights = [
            [
                jnp.where(
                    row < HALO,
                    spectral_entry(2 * m - j - skip, 2 * ninst),
                    spectral_entry(2 * m + 1 - j - skip, 2 * ninst),
                )
                for j in range(ninst)
            ]
            for skip in (0, ninst)
        ]
        for u in range(nvar):
            z = sum(jac(1, u, v) * centre[v] for v in range(nvar))
            rest = z + 4.0 * VISCOUS * centre[u]
            for j in range(ninst):
                rest += weights[0][j] * far_own[u, j] + weights[1][j] * far_oth[u, j]
            at = lines_of(packs, u, m)
            rest_ref[at, :] = rest
            parts_ref[at, 0:axial] = z
            parts_ref[at, axial : 2 * axial] = centre[u]
    rest_ref[...] = rest_ref[...] - times(parts_ref[...], shift_ref[...])

    half = jnp.where(low, 0.5, -0.5)
    for m in range(packs):
        slope, around = [], []
        for v in range(nvar):
            c = pack_of(far_own, v, m)
            behind = shifted(c, 2)
            slope.append(half * (c - behind))
            around.append(c + behind)
        for u in range(nvar):
            at = lines_of(packs, u, m)
            r = shifted(rest_ref[at, :], 1) - VISCOUS * around[u]
            for v in range(nvar):
                r += jac(0, u, v) * slope[v]
            moved = [r, *(shifted(r, s) for s in range(1, SWEEPS + 1))]
            sums = [
                sum(spread_weight(j, SWEEPS - s) * moved[s] for s in range(j, SWEEPS + 1))
                for j in range(SWEEPS + 1)
            ]
            rest_ref[at, :] = sums[0]
            for j in range(1, SWEEPS + 1):
                terms_ref[at, (j - 1) * axial : j * axial] = sums[j]
    rest_ref[...] = rest_ref[...] + times(terms_ref[...], sweep_ref[...])

    step = step_ref[...]
    lane = lax.broadcasted_iota(jnp.int32, (ROWS, LANES), 1)
    reached = side >= HALO
    for n in range(ninst):
        for u in range(nvar):
            far = rest_ref[lines_of(packs, u, n // 2), :]
            turned = pltpu.roll(far, HALO, 0)
            stays = (1 - n % 2) == jnp.where(low, 0, 1)
            far = jnp.where(reached, jnp.where(stays, far, turned), 0.0)
            tiles = [far[:, t : t + LANES] for t in range(0, axial, LANES)]
            group = (u * ninst + n) * GROUP
            for plane_no, plane in enumerate(planes):
                tile, at = divmod(plane - SWEEPS, LANES)
                assert at + GROUP <= LANES
                start = group // LANES * LANES
                moved = pltpu.roll(
                    spread[plane_no][:, start : start + LANES], (at - group) % LANES, 1
                )
                inside = (lane >= at) & (lane < at + GROUP)
                tiles[tile] = tiles[tile] + jnp.where(inside, moved, 0.0)
            more = jnp.concatenate(tiles, axis=1)
            at = lines_of(ninst, u, n)
            out_ref[u, n] = base_ref[at, :] + more
            new_ref[u, n] = before_ref[at, :] - step * more


def here(array):
    return pltpu.with_memory_space_constraint(array, pltpu.VMEM)


def shards(flow_state, jac_pitch, jac_axial, pseudo_step, partner, iface_index):
    nvar, ninst, rows, axial = flow_state.shape
    spaces = lax.axis_size("space")
    planes = interface_planes(axial, IFACES)
    both = ("space", "inst")
    vmem = pl.BlockSpec(memory_space=pltpu.VMEM)
    smem = pl.BlockSpec(memory_space=pltpu.SMEM)
    anywhere = pl.BlockSpec(memory_space=pl.ANY)
    params = pltpu.CompilerParams(vmem_limit_bytes=VMEM_LIMIT)
    block = pltpu.VMEM(flow_state.shape, jnp.float32)
    cores = [(0, 1), (1, 0)]

    other = here(lax.ppermute(flow_state, "inst", cores))
    own, half, shift, sweep = pl.pallas_call(
        functools.partial(stage_kernel, planes),
        out_shape=(
            block,
            pltpu.VMEM((rows, LANES), jnp.float32),
            pltpu.VMEM((2 * axial, axial), jnp.bfloat16),
            pltpu.VMEM((SWEEPS * axial, axial), jnp.bfloat16),
        ),
        in_specs=[vmem],
        out_specs=(vmem,) * 4,
        compiler_params=params,
    )(flow_state)
    staged, own = own, here(own)
    line = pl.pallas_call(
        functools.partial(line_kernel, planes),
        out_shape=pltpu.VMEM((rows, LANES), jnp.float32),
        in_specs=[vmem, vmem],
        out_specs=vmem,
        compiler_params=params,
    )(here(half), other)

    lines, got = line, []
    for turn, bit in enumerate(round_bits(spaces)):
        cross = 1 if turn == 0 else 0
        swaps = [
            (2 * i + c, 2 * (i ^ (1 << bit)) + (c ^ cross)) for i in range(spaces) for c in (0, 1)
        ]
        got.append(lax.ppermute(lines, both, swaps))
        parts = (lines, got[-1])
        lines = jnp.concatenate(parts, axis=0)

    edge = pl.pallas_call(
        edge_kernel,
        out_shape=block,
        in_specs=[vmem, vmem, anywhere],
        out_specs=vmem,
        compiler_params=params,
    )(own, other, line)
    pairs = []
    for i in range(spaces):
        odd = (i + 1) % spaces if i % 2 else (i - 1) % spaces
        pairs += [(2 * i, 2 * (i ^ 1)), (2 * i + 1, 2 * odd + 1)]
    near = lax.ppermute(edge, both, pairs)
    cut = nvar // 2
    far = [
        here(lax.ppermute(near[v : v + cut], "inst", cores)) for v in range(0, nvar, cut)
    ]

    step, local, jac, pick, mix = pl.pallas_call(
        functools.partial(prepare_kernel, planes, spaces),
        out_shape=(
            pltpu.VMEM(pseudo_step.shape, jnp.float32),
            block,
            pltpu.VMEM((2 * nvar * nvar, axial), jnp.float32),
            pltpu.VMEM((IFACES * 2 * rows, spaces * rows), jnp.float32),
            pltpu.VMEM((IFACES, LANES, 2 * LANES), jnp.float32),
        ),
        in_specs=[smem] * 4 + [vmem] * 3 + [anywhere],
        out_specs=(vmem,) * 5,
        compiler_params=params,
    )(jac_pitch, jac_axial, partner, iface_index, own, other, pseudo_step, got[0])

    lined = nvar * ninst * rows
    base = pl.pallas_call(
        functools.partial(near_kernel, planes),
        out_shape=pltpu.VMEM((lined, axial), jnp.float32),
        in_specs=[vmem] * 6,
        out_specs=vmem,
        scratch_shapes=[
            block,
            block,
            pltpu.VMEM((lined, 2 * axial), jnp.float32),
            pltpu.VMEM((lined, axial), jnp.float32),
            pltpu.VMEM((lined, SWEEPS * axial), jnp.float32),
        ],
        compiler_params=params,
    )(own, *[here(a) for a in (near, local, jac, shift, sweep)])

    before = (staged - step * base.reshape(staged.shape)).reshape(lined, axial)

    return pl.pallas_call(
        functools.partial(step_kernel, planes, len(far)),
        out_shape=(jax.ShapeDtypeStruct(flow_state.shape, jnp.float32),) * 2,
        in_specs=[vmem] * (10 + len(far)),
        out_specs=(vmem, vmem),
        scratch_shapes=[
            block,
            block,
            pltpu.VMEM((lined // 2, 2 * axial), jnp.float32),
            pltpu.VMEM((lined // 2, axial), jnp.float32),
            pltpu.VMEM((lined // 2, SWEEPS * axial), jnp.float32),
        ],
        compiler_params=params,
    )(here(before), here(base), *far, *[here(a) for a in (jac, shift, sweep, *parts, pick, mix, step)])


def solution(mesh):
    in_specs = (
        P("groups", "inst", "space", None),
        P("groups", None),
        P("groups", None),
        P("space", "groups"),
        P("groups", None),
        P("groups", "space"),
    )
    out_specs = (P("groups", "inst", "space", None), P("groups", "inst", "space", None))
    return jax.shard_map(shards, mesh=mesh, in_specs=in_specs, out_specs=out_specs, check_vma=False)
```

```python
import functools
import math

import jax
import jax.numpy as jnp
from jax import lax
from jax.experimental import pallas as pl
from jax.experimental.pallas import tpu as pltpu
from jax.sharding import PartitionSpec as P

IFACES = 2
SWEEPS = 3
VISCOUS = 0.25
SMOOTHING = 1.0
HALO = 4
ROWS = 8
LANES = 128
GROUP = 8
VMEM_LIMIT = 16 * 1024 * 1024


def spectral_entry(shift, instances):
    shift %= instances
    if shift == 0:
        return 0.0
    return 0.5 * (-1) ** shift / math.tan(math.pi * shift / instances)


def interface_planes(axial_cells, planes_count):
    return [(plane_no + 1) * axial_cells // (planes_count + 1) for plane_no in range(planes_count)]


def sweep_weights():
    k = SMOOTHING / (1.0 + 4.0 * SMOOTHING)
    base = 1.0 / (1.0 + 4.0 * SMOOTHING)
    return [base * k**m for m in range(SWEEPS)] + [k**SWEEPS]


def spread_weight(m, distance):
    weights = sweep_weights() + [0.0] * 4
    paths = {0: {0: 1, 2: 2}, 1: {1: 1, 3: 3}, 2: {2: 1}, 3: {3: 1}}[distance]
    return sum(count * math.comb(m + j, m) * weights[m + j] for j, count in paths.items())


def round_bits(spaces):
    bits = list(range(spaces.bit_length() - 1))
    return bits[:1] + bits[:0:-1]


def pack_lines(planes, field_ref, half, line):
    nvar, ninst = field_ref.shape[:2]
    lane = lax.broadcasted_iota(jnp.int32, (ROWS, LANES), 1)
    for plane_no, plane in enumerate(planes):
        for v in range(nvar):
            for n in range(ninst):
                at = (plane_no * nvar + v) * 2 * ninst + half * ninst + n
                cell = jnp.broadcast_to(field_ref[v, n, :, plane - 1 : plane], (ROWS, LANES))
                line = jnp.where(lane == at, cell, line)
    return line


def line_kernel(planes, half_ref, oth_ref, line_ref):
    ninst = oth_ref.shape[1]
    line = pack_lines(planes, oth_ref, 1, half_ref[...])
    lane = lax.broadcasted_iota(jnp.int32, (ROWS, LANES), 1)
    swapped = jnp.where(
        lax.rem(lane, 2 * ninst) < ninst,
        pltpu.roll(line, LANES - ninst, 1),
        pltpu.roll(line, ninst, 1),
    )
    line_ref[...] = jnp.where(lax.axis_index("inst") == 0, line, swapped)


def stage_kernel(planes, flow_ref, own_ref, half_ref, shift_ref, sweep_ref):
    own_ref[...] = flow_ref[...]
    half_ref[...] = pack_lines(planes, flow_ref, 0, jnp.zeros((ROWS, LANES), jnp.float32))
    axial = flow_ref.shape[3]
    source = lax.broadcasted_iota(jnp.int32, (axial, axial), 0)
    target = lax.broadcasted_iota(jnp.int32, (axial, axial), 1)
    ahead = target - source
    up, down = jnp.where(ahead == 1, 1.0, 0.0), jnp.where(ahead == -1, 1.0, 0.0)
    once = up + down
    for plane in planes:
        up = jnp.where(target == plane, 0.0, up)
    for plane in [*planes, axial]:
        down = jnp.where(target == plane - 1, jnp.where(ahead == 0, 1.0, 0.0), down)
    shift_ref[0:axial, :] = up.astype(jnp.bfloat16)
    shift_ref[axial : 2 * axial, :] = (VISCOUS * (up + down)).astype(jnp.bfloat16)
    far, edges = jnp.abs(ahead), source + target
    corner = (edges == 0) | (edges == 2 * axial - 2)
    beside = (edges == 1) | (edges == 2 * axial - 3)
    twice = jnp.where(far == 2, 1.0, jnp.where(far == 0, jnp.where(corner, 1.0, 2.0), 0.0))
    thrice = jnp.where(far == 3, 1.0, jnp.where(far == 1, jnp.where(beside, 2.0, 3.0), 0.0))
    for power, value in enumerate((once, twice, thrice)):
        sweep_ref[power * axial : (power + 1) * axial, :] = value.astype(jnp.bfloat16)


def low_side():
    return lax.rem(lax.axis_index("space") + lax.axis_index("inst"), 2) == 1


def edge_kernel(own_ref, oth_ref, after_ref, edge_ref):
    del after_ref
    core = lax.axis_index("inst")
    low = low_side()
    nvar, ninst, _, axial = own_ref.shape
    row = lax.broadcasted_iota(jnp.int32, (ROWS, axial), 0)
    for v in range(nvar):
        for n in range(ninst):
            own, oth = own_ref[v, n], oth_ref[v, n]
            first = jnp.where(core == 0, own, oth)
            second = jnp.where(core == 0, oth, own)
            low_rows = jnp.where(row < HALO, first, pltpu.roll(second, HALO, 0))
            high_rows = jnp.where(row < HALO, pltpu.roll(first, HALO, 0), second)
            edge_ref[v, n] = jnp.where(low, low_rows, high_rows)


def local_terms(planes, jac, own, oth, n):
    nvar, ninst, rows, axial = own.shape
    lane = lax.broadcasted_iota(jnp.int32, (rows, axial), 1)
    inward, spread = [], []
    for v in range(nvar):
        c = own[v, n]
        up, down = pltpu.roll(c, 1, 1), pltpu.roll(c, axial - 1, 1)
        for plane in [0, *planes]:
            up = jnp.where(lane == plane, 0.0, up)
        for plane in [*planes, axial]:
            down = jnp.where(lane == plane - 1, c, down)
        inward.append(c - up)
        spread.append(up + down - 4.0 * c)
    terms = []
    for u in range(nvar):
        total = -VISCOUS * spread[u]
        for v in range(nvar):
            total += jac(u, v) * inward[v]
        for j in range(ninst):
            if j != n:
                total += spectral_entry(n - j, 2 * ninst) * own[u, j]
            total += spectral_entry(n - j - ninst, 2 * ninst) * oth[u, j]
        terms.append(total)
    return terms


def prepare_kernel(
    planes,
    spaces,
    jac_pitch_ref,
    jac_axial_ref,
    partner_ref,
    index_ref,
    own_ref,
    oth_ref,
    step_in_ref,
    after_ref,
    step_ref,
    local_ref,
    jac_ref,
    pick_ref,
    mix_ref,
):
    del after_ref
    step_ref[...] = step_in_ref[...]
    core, space = lax.axis_index("inst"), lax.axis_index("space")
    nvar, ninst, _, axial = own_ref.shape
    for n in range(ninst):
        terms = local_terms(planes, lambda u, v: jac_axial_ref[u, v], own_ref, oth_ref, n)
        for u in range(nvar):
            local_ref[u, n] = terms[u]
    for which, ref in enumerate((jac_pitch_ref, jac_axial_ref)):
        for u in range(nvar):
            for v in range(nvar):
                at = (which * nvar + u) * nvar + v
                jac_ref[at : at + 1, :] = jnp.full((1, axial), ref[u, v], jnp.float32)

    total = spaces * ROWS
    row = lax.broadcasted_iota(jnp.int32, (2 * ROWS, total), 0)
    ahead = jnp.where(row < ROWS + HALO, row, row - 2 * ROWS)
    lane = lax.broadcasted_iota(jnp.int32, (2 * ROWS, total), 1)
    for plane_no in range(len(planes)):
        pitch = index_ref[plane_no, 0] + ahead
        pitch = jnp.where(pitch < 0, pitch + total, pitch)
        pitch = jnp.where(pitch >= total, pitch - total, pitch)
        apart = (pitch >> 3) ^ space
        place = pitch & 7
        for turn, bit in enumerate(round_bits(spaces)):
            place += ((apart >> bit) & 1) << (turn + 3)
        pick_ref[pl.ds(plane_no * 2 * ROWS, 2 * ROWS), :] = jnp.where(lane == place, 1.0, 0.0)

    lane = lax.broadcasted_iota(jnp.int32, (ROWS, 2 * LANES), 1) // GROUP
    row = lax.broadcasted_iota(jnp.int32, (ROWS, 2 * LANES), 0)
    to_var, to_inst = lane // ninst, lax.rem(lane, ninst) + ninst * core
    mix_ref[...] = jnp.zeros(mix_ref.shape, jnp.float32)
    for v in range(nvar):
        block = jnp.zeros((ROWS, 2 * LANES), jnp.float32)
        for u in range(nvar):
            value = -jac_axial_ref[u, v] - (VISCOUS if u == v else 0.0)
            block = jnp.where(to_var == u, value, block)
        for plane_no in range(len(planes)):
            source = lax.rem(to_inst + partner_ref[plane_no, 0], 2 * ninst)
            at = (plane_no * nvar + v) * 2 * ninst
            mix_ref[plane_no, at : at + ROWS, :] = jnp.where(row == source, block, 0.0)


def times(left, right):
    first = left.astype(jnp.bfloat16)
    second = (left - first.astype(jnp.float32)).astype(jnp.bfloat16)
    return jnp.dot(first, right, preferred_element_type=jnp.float32) + jnp.dot(
        second, right, preferred_element_type=jnp.float32
    )


def inflow_spread(planes, lines_refs, pick_ref, mix_ref):
    lines = jnp.concatenate([ref[...] for ref in lines_refs], axis=0)
    pick, first = pick_ref[...].astype(jnp.bfloat16), lines.astype(jnp.bfloat16)
    second = (lines - first.astype(jnp.float32)).astype(jnp.bfloat16)
    plain = dict(preferred_element_type=jnp.float32)
    facing = jnp.dot(pick, first, **plain) + jnp.dot(pick, second, **plain)
    lane = lax.rem(lax.broadcasted_iota(jnp.int32, (ROWS, 2 * LANES), 1), GROUP)
    spread = []
    for plane_no in range(len(planes)):
        seen = facing[plane_no * 2 * ROWS : (plane_no + 1) * 2 * ROWS]
        seen_first, mix_first = seen.astype(jnp.bfloat16), mix_ref[plane_no].astype(jnp.bfloat16)
        seen_second = (seen - seen_first.astype(jnp.float32)).astype(jnp.bfloat16)
        mix_second = (mix_ref[plane_no] - mix_first.astype(jnp.float32)).astype(jnp.bfloat16)
        power = jnp.dot(seen_first, mix_first, **plain)
        power += jnp.dot(seen_second, mix_first, **plain) + jnp.dot(seen_first, mix_second, **plain)
        total = jnp.zeros((ROWS, 2 * LANES), jnp.float32)
        for m in range(SWEEPS + 1):
            weight = jnp.zeros((ROWS, 2 * LANES), jnp.float32)
            for d in range(-SWEEPS, SWEEPS + 1):
                weight = jnp.where(lane == d + SWEEPS, spread_weight(m, abs(d)), weight)
            total += weight * power[0:ROWS]
            if m < SWEEPS:
                power = pltpu.roll(power, 2 * ROWS - 1, 0) + pltpu.roll(power, 1, 0)
        spread.append(total)
    return spread


def jac_row(jac_ref, nvar, which, u, v):
    at = (which * nvar + u) * nvar + v
    return jac_ref[at : at + 1, :]


def lines_of(ninst, u, n):
    at = (u * ninst + n) * ROWS
    return slice(at, at + ROWS)


def near_kernel(planes, *refs):
    own_ref, near_ref, local_ref, jac_ref, shift_ref, sweep_ref, base_ref, *refs = refs
    halo_own, halo_oth, parts_ref, rest_ref, terms_ref = refs
    core = lax.axis_index("inst")
    low = low_side()
    nvar, ninst, _, axial = own_ref.shape
    row = lax.broadcasted_iota(jnp.int32, (ROWS, axial), 0)
    keep = jnp.where(low, row, ROWS - 1 - row) >= HALO
    for v in range(nvar):
        for n in range(ninst):
            near = near_ref[v, n]
            turned = pltpu.roll(near, HALO, 0)
            first = jnp.where(keep, jnp.where(low, turned, near), 0.0)
            second = jnp.where(keep, jnp.where(low, near, turned), 0.0)
            halo_own[v, n] = jnp.where(core == 0, first, second)
            halo_oth[v, n] = jnp.where(core == 0, second, first)
    jac = functools.partial(jac_row, jac_ref, nvar)

    for n in range(ninst):
        centre = [halo_own[v, n] for v in range(nvar)]
        for u in range(nvar):
            z = sum(jac(1, u, v) * centre[v] for v in range(nvar))
            rest = z + 4.0 * VISCOUS * centre[u]
            for j in range(ninst):
                if j != n:
                    rest += spectral_entry(n - j, 2 * ninst) * halo_own[u, j]
                rest += spectral_entry(n - j - ninst, 2 * ninst) * halo_oth[u, j]
            at = lines_of(ninst, u, n)
            rest_ref[at, :] = rest
            parts_ref[at, 0:axial] = z
            parts_ref[at, axial : 2 * axial] = centre[u]
    rest_ref[...] = rest_ref[...] - times(parts_ref[...], shift_ref[...])

    c0, c1, c2, c3 = sweep_weights()
    for n in range(ninst):
        slope, around = [], []
        for v in range(nvar):
            c = jnp.concatenate([own_ref[v, n], halo_own[v, n]], axis=0)
            nxt, prv = pltpu.roll(c, 2 * ROWS - 1, 0), pltpu.roll(c, 1, 0)
            slope.append(0.5 * (nxt - prv))
            around.append(nxt + prv)
        for u in range(nvar):
            at = lines_of(ninst, u, n)
            r0 = jnp.concatenate([local_ref[u, n], rest_ref[at, :]], axis=0) - VISCOUS * around[u]
            for v in range(nvar):
                r0 += jac(0, u, v) * slope[v]
            r1 = pltpu.roll(r0, 2 * ROWS - 1, 0) + pltpu.roll(r0, 1, 0)
            r2 = pltpu.roll(r1, 2 * ROWS - 1, 0) + pltpu.roll(r1, 1, 0)
            r3 = pltpu.roll(r2, 2 * ROWS - 1, 0) + pltpu.roll(r2, 1, 0)
            r0, r1, r2, r3 = (r[0:ROWS] for r in (r0, r1, r2, r3))
            base_ref[at, :] = c0 * r0 + c1 * r1 + c2 * r2 + c3 * r3
            terms_ref[at, 0:axial] = c1 * r0 + 2.0 * c2 * r1 + 3.0 * c3 * r2
            terms_ref[at, axial : 2 * axial] = c2 * r0 + 3.0 * c3 * r1
            terms_ref[at, 2 * axial : 3 * axial] = c3 * r0
    base_ref[...] = base_ref[...] + times(terms_ref[...], sweep_ref[...])


def step_kernel(planes, cuts, *refs):
    before_ref, base_ref, *refs = refs
    far_refs, refs = refs[:cuts], refs[cuts:]
    jac_ref, shift_ref, sweep_ref, *lines_refs, pick_ref, mix_ref, step_ref = refs[:8]
    new_ref, out_ref, far_own, far_oth, parts_ref, rest_ref, terms_ref = refs[8:]
    core = lax.axis_index("inst")
    low = low_side()
    nvar, ninst, _, axial = new_ref.shape
    cut, packs = nvar // cuts, ninst // 2
    row = lax.broadcasted_iota(jnp.int32, (ROWS, axial), 0)
    side = jnp.where(low, row, ROWS - 1 - row)
    depth = side & (HALO - 1)
    spread = inflow_spread(planes, lines_refs, pick_ref, mix_ref)
    jac = functools.partial(jac_row, jac_ref, nvar)

    def shifted(tile, s):
        moved = pltpu.roll(tile, jnp.where(low, s, ROWS - s), 0)
        return jnp.where(depth >= s, moved, 0.0)

    for v in range(nvar):
        for n in range(ninst):
            tile = far_refs[v // cut][v % cut, n]
            turned = pltpu.roll(tile, HALO, 0)
            first = jnp.where(row < HALO, tile, turned)
            second = jnp.where(row < HALO, turned, tile)
            far_own[v, n] = jnp.where(core == 0, first, second)
            far_oth[v, n] = jnp.where(core == 0, second, first)

    def pack_of(ref, v, m):
        return jnp.where(row < HALO, ref[v, 2 * m], ref[v, 2 * m + 1])

    for m in range(packs):
        centre = [pack_of(far_own, v, m) for v in range(nvar)]
        weights = [
            [
                jnp.where(
                    row < HALO,
                    spectral_entry(2 * m - j - skip, 2 * ninst),
                    spectral_entry(2 * m + 1 - j - skip, 2 * ninst),
                )
                for j in range(ninst)
            ]
            for skip in (0, ninst)
        ]
        for u in range(nvar):
            z = sum(jac(1, u, v) * centre[v] for v in range(nvar))
            rest = z + 4.0 * VISCOUS * centre[u]
            for j in range(ninst):
                rest += weights[0][j] * far_own[u, j] + weights[1][j] * far_oth[u, j]
            at = lines_of(packs, u, m)
            rest_ref[at, :] = rest
            parts_ref[at, 0:axial] = z
            parts_ref[at, axial : 2 * axial] = centre[u]
    rest_ref[...] = rest_ref[...] - times(parts_ref[...], shift_ref[...])

    half = jnp.where(low, 0.5, -0.5)
    for m in range(packs):
        slope, around = [], []
        for v in range(nvar):
            c = pack_of(far_own, v, m)
            behind = shifted(c, 2)
            slope.append(half * (c - behind))
            around.append(c + behind)
        for u in range(nvar):
            at = lines_of(packs, u, m)
            r = shifted(rest_ref[at, :], 1) - VISCOUS * around[u]
            for v in range(nvar):
                r += jac(0, u, v) * slope[v]
            moved = [r, *(shifted(r, s) for s in range(1, SWEEPS + 1))]
            sums = [
                sum(spread_weight(j, SWEEPS - s) * moved[s] for s in range(j, SWEEPS + 1))
                for j in range(SWEEPS + 1)
            ]
            rest_ref[at, :] = sums[0]
            for j in range(1, SWEEPS + 1):
                terms_ref[at, (j - 1) * axial : j * axial] = sums[j]
    rest_ref[...] = rest_ref[...] + times(terms_ref[...], sweep_ref[...])

    step = step_ref[...]
    lane = lax.broadcasted_iota(jnp.int32, (ROWS, LANES), 1)
    reached = side >= HALO
    for n in range(ninst):
        for u in range(nvar):
            far = rest_ref[lines_of(packs, u, n // 2), :]
            turned = pltpu.roll(far, HALO, 0)
            stays = (1 - n % 2) == jnp.where(low, 0, 1)
            far = jnp.where(reached, jnp.where(stays, far, turned), 0.0)
            tiles = [far[:, t : t + LANES] for t in range(0, axial, LANES)]
            group = (u * ninst + n) * GROUP
            for plane_no, plane in enumerate(planes):
                tile, at = divmod(plane - SWEEPS, LANES)
                assert at + GROUP <= LANES
                start = group // LANES * LANES
                moved = pltpu.roll(
                    spread[plane_no][:, start : start + LANES], (at - group) % LANES, 1
                )
                inside = (lane >= at) & (lane < at + GROUP)
                tiles[tile] = tiles[tile] + jnp.where(inside, moved, 0.0)
            more = jnp.concatenate(tiles, axis=1)
            at = lines_of(ninst, u, n)
            out_ref[u, n] = base_ref[at, :] + more
            new_ref[u, n] = before_ref[at, :] - step * more


def here(array):
    return pltpu.with_memory_space_constraint(array, pltpu.VMEM)


def shards(flow_state, jac_pitch, jac_axial, pseudo_step, partner, iface_index):
    nvar, ninst, rows, axial = flow_state.shape
    spaces = lax.axis_size("space")
    planes = interface_planes(axial, IFACES)
    both = ("space", "inst")
    vmem = pl.BlockSpec(memory_space=pltpu.VMEM)
    smem = pl.BlockSpec(memory_space=pltpu.SMEM)
    anywhere = pl.BlockSpec(memory_space=pl.ANY)
    params = pltpu.CompilerParams(vmem_limit_bytes=VMEM_LIMIT)
    block = pltpu.VMEM(flow_state.shape, jnp.float32)
    cores = [(0, 1), (1, 0)]

    other = here(lax.ppermute(flow_state, "inst", cores))
    own, half, shift, sweep = pl.pallas_call(
        functools.partial(stage_kernel, planes),
        out_shape=(
            block,
            pltpu.VMEM((rows, LANES), jnp.float32),
            pltpu.VMEM((2 * axial, axial), jnp.bfloat16),
            pltpu.VMEM((SWEEPS * axial, axial), jnp.bfloat16),
        ),
        in_specs=[vmem],
        out_specs=(vmem,) * 4,
        compiler_params=params,
    )(flow_state)
    staged, own = own, here(own)
    line = pl.pallas_call(
        functools.partial(line_kernel, planes),
        out_shape=pltpu.VMEM((rows, LANES), jnp.float32),
        in_specs=[vmem, vmem],
        out_specs=vmem,
        compiler_params=params,
    )(here(half), other)

    lines, got = line, []
    for turn, bit in enumerate(round_bits(spaces)):
        cross = 1 if turn == 0 else 0
        swaps = [
            (2 * i + c, 2 * (i ^ (1 << bit)) + (c ^ cross)) for i in range(spaces) for c in (0, 1)
        ]
        got.append(lax.ppermute(lines, both, swaps))
        parts = (lines, got[-1])
        lines = jnp.concatenate(parts, axis=0)

    edge = pl.pallas_call(
        edge_kernel,
        out_shape=block,
        in_specs=[vmem, vmem, anywhere],
        out_specs=vmem,
        compiler_params=params,
    )(own, other, line)
    pairs = []
    for i in range(spaces):
        odd = (i + 1) % spaces if i % 2 else (i - 1) % spaces
        pairs += [(2 * i, 2 * (i ^ 1)), (2 * i + 1, 2 * odd + 1)]
    near = lax.ppermute(edge, both, pairs)
    far = [here(lax.ppermute(near, "inst", cores))]

    step, local, jac, pick, mix = pl.pallas_call(
        functools.partial(prepare_kernel, planes, spaces),
        out_shape=(
            pltpu.VMEM(pseudo_step.shape, jnp.float32),
            block,
            pltpu.VMEM((2 * nvar * nvar, axial), jnp.float32),
            pltpu.VMEM((IFACES * 2 * rows, spaces * rows), jnp.float32),
            pltpu.VMEM((IFACES, LANES, 2 * LANES), jnp.float32),
        ),
        in_specs=[smem] * 4 + [vmem] * 3 + [anywhere],
        out_specs=(vmem,) * 5,
        compiler_params=params,
    )(jac_pitch, jac_axial, partner, iface_index, own, other, pseudo_step, got[0])

    lined = nvar * ninst * rows
    base = pl.pallas_call(
        functools.partial(near_kernel, planes),
        out_shape=pltpu.VMEM((lined, axial), jnp.float32),
        in_specs=[vmem] * 6,
        out_specs=vmem,
        scratch_shapes=[
            block,
            block,
            pltpu.VMEM((lined, 2 * axial), jnp.float32),
            pltpu.VMEM((lined, axial), jnp.float32),
            pltpu.VMEM((lined, SWEEPS * axial), jnp.float32),
        ],
        compiler_params=params,
    )(own, *[here(a) for a in (near, local, jac, shift, sweep)])

    before = (staged - step * base.reshape(staged.shape)).reshape(lined, axial)

    return pl.pallas_call(
        functools.partial(step_kernel, planes, len(far)),
        out_shape=(jax.ShapeDtypeStruct(flow_state.shape, jnp.float32),) * 2,
        in_specs=[vmem] * (10 + len(far)),
        out_specs=(vmem, vmem),
        scratch_shapes=[
            block,
            block,
            pltpu.VMEM((lined // 2, 2 * axial), jnp.float32),
            pltpu.VMEM((lined // 2, axial), jnp.float32),
            pltpu.VMEM((lined // 2, SWEEPS * axial), jnp.float32),
        ],
        compiler_params=params,
    )(here(before), here(base), *far, *[here(a) for a in (jac, shift, sweep, *parts, pick, mix, step)])


def solution(mesh):
    in_specs = (
        P("groups", "inst", "space", None),
        P("groups", None),
        P("groups", None),
        P("space", "groups"),
        P("groups", None),
        P("groups", "space"),
    )
    out_specs = (P("groups", "inst", "space", None), P("groups", "inst", "space", None))
    return jax.shard_map(shards, mesh=mesh, in_specs=in_specs, out_specs=out_specs, check_vma=False)
```

```python
import functools
import math

import jax
import jax.numpy as jnp
from jax import lax
from jax.experimental import pallas as pl
from jax.experimental.pallas import tpu as pltpu
from jax.sharding import PartitionSpec as P

IFACES = 2
SWEEPS = 3
VISCOUS = 0.25
SMOOTHING = 1.0
HALO = 4
ROWS = 8
LANES = 128
GROUP = 8
VMEM_LIMIT = 16 * 1024 * 1024


def spectral_entry(shift, instances):
    shift %= instances
    if shift == 0:
        return 0.0
    return 0.5 * (-1) ** shift / math.tan(math.pi * shift / instances)


def interface_planes(axial_cells, planes_count):
    return [(plane_no + 1) * axial_cells // (planes_count + 1) for plane_no in range(planes_count)]


def sweep_weights():
    k = SMOOTHING / (1.0 + 4.0 * SMOOTHING)
    base = 1.0 / (1.0 + 4.0 * SMOOTHING)
    return [base * k**m for m in range(SWEEPS)] + [k**SWEEPS]


def spread_weight(m, distance):
    weights = sweep_weights() + [0.0] * 4
    paths = {0: {0: 1, 2: 2}, 1: {1: 1, 3: 3}, 2: {2: 1}, 3: {3: 1}}[distance]
    return sum(count * math.comb(m + j, m) * weights[m + j] for j, count in paths.items())


def round_bits(spaces):
    bits = list(range(spaces.bit_length() - 1))
    return bits[:1] + bits[:0:-1]


def pack_lines(planes, field_ref, half, line):
    nvar, ninst = field_ref.shape[:2]
    lane = lax.broadcasted_iota(jnp.int32, (ROWS, LANES), 1)
    for plane_no, plane in enumerate(planes):
        for v in range(nvar):
            for n in range(ninst):
                at = (plane_no * nvar + v) * 2 * ninst + half * ninst + n
                cell = jnp.broadcast_to(field_ref[v, n, :, plane - 1 : plane], (ROWS, LANES))
                line = jnp.where(lane == at, cell, line)
    return line


def line_kernel(planes, half_ref, oth_ref, line_ref):
    ninst = oth_ref.shape[1]
    line = pack_lines(planes, oth_ref, 1, half_ref[...])
    lane = lax.broadcasted_iota(jnp.int32, (ROWS, LANES), 1)
    swapped = jnp.where(
        lax.rem(lane, 2 * ninst) < ninst,
        pltpu.roll(line, LANES - ninst, 1),
        pltpu.roll(line, ninst, 1),
    )
    line_ref[...] = jnp.where(lax.axis_index("inst") == 0, line, swapped)


def stage_kernel(planes, flow_ref, own_ref, half_ref, shift_ref, sweep_ref):
    own_ref[...] = flow_ref[...]
    half_ref[...] = pack_lines(planes, flow_ref, 0, jnp.zeros((ROWS, LANES), jnp.float32))
    axial = flow_ref.shape[3]
    source = lax.broadcasted_iota(jnp.int32, (axial, axial), 0)
    target = lax.broadcasted_iota(jnp.int32, (axial, axial), 1)
    ahead = target - source
    up, down = jnp.where(ahead == 1, 1.0, 0.0), jnp.where(ahead == -1, 1.0, 0.0)
    once = up + down
    for plane in planes:
        up = jnp.where(target == plane, 0.0, up)
    for plane in [*planes, axial]:
        down = jnp.where(target == plane - 1, jnp.where(ahead == 0, 1.0, 0.0), down)
    shift_ref[0:axial, :] = up.astype(jnp.bfloat16)
    shift_ref[axial : 2 * axial, :] = (VISCOUS * (up + down)).astype(jnp.bfloat16)
    far, edges = jnp.abs(ahead), source + target
    corner = (edges == 0) | (edges == 2 * axial - 2)
    beside = (edges == 1) | (edges == 2 * axial - 3)
    twice = jnp.where(far == 2, 1.0, jnp.where(far == 0, jnp.where(corner, 1.0, 2.0), 0.0))
    thrice = jnp.where(far == 3, 1.0, jnp.where(far == 1, jnp.where(beside, 2.0, 3.0), 0.0))
    for power, value in enumerate((once, twice, thrice)):
        sweep_ref[power * axial : (power + 1) * axial, :] = value.astype(jnp.bfloat16)


def low_side():
    return lax.rem(lax.axis_index("space") + lax.axis_index("inst"), 2) == 1


def edge_kernel(own_ref, oth_ref, after_ref, edge_ref):
    del after_ref
    core = lax.axis_index("inst")
    low = low_side()
    nvar, ninst, _, axial = own_ref.shape
    row = lax.broadcasted_iota(jnp.int32, (ROWS, axial), 0)
    for v in range(nvar):
        for n in range(ninst):
            own, oth = own_ref[v, n], oth_ref[v, n]
            first = jnp.where(core == 0, own, oth)
            second = jnp.where(core == 0, oth, own)
            low_rows = jnp.where(row < HALO, first, pltpu.roll(second, HALO, 0))
            high_rows = jnp.where(row < HALO, pltpu.roll(first, HALO, 0), second)
            edge_ref[v, n] = jnp.where(low, low_rows, high_rows)


def local_terms(planes, jac, own, oth, n):
    nvar, ninst, rows, axial = own.shape
    lane = lax.broadcasted_iota(jnp.int32, (rows, axial), 1)
    inward, spread = [], []
    for v in range(nvar):
        c = own[v, n]
        up, down = pltpu.roll(c, 1, 1), pltpu.roll(c, axial - 1, 1)
        for plane in [0, *planes]:
            up = jnp.where(lane == plane, 0.0, up)
        for plane in [*planes, axial]:
            down = jnp.where(lane == plane - 1, c, down)
        inward.append(c - up)
        spread.append(up + down - 4.0 * c)
    terms = []
    for u in range(nvar):
        total = -VISCOUS * spread[u]
        for v in range(nvar):
            total += jac(u, v) * inward[v]
        for j in range(ninst):
            if j != n:
                total += spectral_entry(n - j, 2 * ninst) * own[u, j]
            total += spectral_entry(n - j - ninst, 2 * ninst) * oth[u, j]
        terms.append(total)
    return terms


def prepare_kernel(
    planes,
    spaces,
    jac_pitch_ref,
    jac_axial_ref,
    partner_ref,
    index_ref,
    own_ref,
    oth_ref,
    step_in_ref,
    after_ref,
    step_ref,
    local_ref,
    jac_ref,
    pick_ref,
    mix_ref,
):
    del after_ref
    step_ref[...] = step_in_ref[...]
    core, space = lax.axis_index("inst"), lax.axis_index("space")
    nvar, ninst, _, axial = own_ref.shape
    for n in range(ninst):
        terms = local_terms(planes, lambda u, v: jac_axial_ref[u, v], own_ref, oth_ref, n)
        for u in range(nvar):
            local_ref[u, n] = terms[u]
    for which, ref in enumerate((jac_pitch_ref, jac_axial_ref)):
        for u in range(nvar):
            for v in range(nvar):
                at = (which * nvar + u) * nvar + v
                jac_ref[at : at + 1, :] = jnp.full((1, axial), ref[u, v], jnp.float32)

    total = spaces * ROWS
    row = lax.broadcasted_iota(jnp.int32, (2 * ROWS, total), 0)
    ahead = jnp.where(row < ROWS + HALO, row, row - 2 * ROWS)
    lane = lax.broadcasted_iota(jnp.int32, (2 * ROWS, total), 1)
    for plane_no in range(len(planes)):
        pitch = index_ref[plane_no, 0] + ahead
        pitch = jnp.where(pitch < 0, pitch + total, pitch)
        pitch = jnp.where(pitch >= total, pitch - total, pitch)
        apart = (pitch >> 3) ^ space
        place = pitch & 7
        for turn, bit in enumerate(round_bits(spaces)):
            place += ((apart >> bit) & 1) << (turn + 3)
        pick_ref[pl.ds(plane_no * 2 * ROWS, 2 * ROWS), :] = jnp.where(lane == place, 1.0, 0.0)

    lane = lax.broadcasted_iota(jnp.int32, (ROWS, 2 * LANES), 1) // GROUP
    row = lax.broadcasted_iota(jnp.int32, (ROWS, 2 * LANES), 0)
    to_var, to_inst = lane // ninst, lax.rem(lane, ninst) + ninst * core
    mix_ref[...] = jnp.zeros(mix_ref.shape, jnp.float32)
    for v in range(nvar):
        block = jnp.zeros((ROWS, 2 * LANES), jnp.float32)
        for u in range(nvar):
            value = -jac_axial_ref[u, v] - (VISCOUS if u == v else 0.0)
            block = jnp.where(to_var == u, value, block)
        for plane_no in range(len(planes)):
            source = lax.rem(to_inst + partner_ref[plane_no, 0], 2 * ninst)
            at = (plane_no * nvar + v) * 2 * ninst
            mix_ref[plane_no, at : at + ROWS, :] = jnp.where(row == source, block, 0.0)


def times(left, right):
    first = left.astype(jnp.bfloat16)
    second = (left - first.astype(jnp.float32)).astype(jnp.bfloat16)
    return jnp.dot(first, right, preferred_element_type=jnp.float32) + jnp.dot(
        second, right, preferred_element_type=jnp.float32
    )


def inflow_spread(planes, lines_refs, pick_ref, mix_ref):
    lines = jnp.concatenate([ref[...] for ref in lines_refs], axis=0)
    pick, first = pick_ref[...].astype(jnp.bfloat16), lines.astype(jnp.bfloat16)
    second = (lines - first.astype(jnp.float32)).astype(jnp.bfloat16)
    plain = dict(preferred_element_type=jnp.float32)
    facing = jnp.dot(pick, first, **plain) + jnp.dot(pick, second, **plain)
    lane = lax.rem(lax.broadcasted_iota(jnp.int32, (ROWS, 2 * LANES), 1), GROUP)
    spread = []
    for plane_no in range(len(planes)):
        seen = facing[plane_no * 2 * ROWS : (plane_no + 1) * 2 * ROWS]
        seen_first, mix_first = seen.astype(jnp.bfloat16), mix_ref[plane_no].astype(jnp.bfloat16)
        seen_second = (seen - seen_first.astype(jnp.float32)).astype(jnp.bfloat16)
        mix_second = (mix_ref[plane_no] - mix_first.astype(jnp.float32)).astype(jnp.bfloat16)
        power = jnp.dot(seen_first, mix_first, **plain)
        power += jnp.dot(seen_second, mix_first, **plain) + jnp.dot(seen_first, mix_second, **plain)
        total = jnp.zeros((ROWS, 2 * LANES), jnp.float32)
        for m in range(SWEEPS + 1):
            weight = jnp.zeros((ROWS, 2 * LANES), jnp.float32)
            for d in range(-SWEEPS, SWEEPS + 1):
                weight = jnp.where(lane == d + SWEEPS, spread_weight(m, abs(d)), weight)
            total += weight * power[0:ROWS]
            if m < SWEEPS:
                power = pltpu.roll(power, 2 * ROWS - 1, 0) + pltpu.roll(power, 1, 0)
        spread.append(total)
    return spread


def jac_row(jac_ref, nvar, which, u, v):
    at = (which * nvar + u) * nvar + v
    return jac_ref[at : at + 1, :]


def lines_of(ninst, u, n):
    at = (u * ninst + n) * ROWS
    return slice(at, at + ROWS)


def near_kernel(planes, *refs):
    own_ref, near_ref, local_ref, jac_ref, shift_ref, sweep_ref, base_ref, *refs = refs
    halo_own, halo_oth, parts_ref, rest_ref, terms_ref = refs
    core = lax.axis_index("inst")
    low = low_side()
    nvar, ninst, _, axial = own_ref.shape
    row = lax.broadcasted_iota(jnp.int32, (ROWS, axial), 0)
    keep = jnp.where(low, row, ROWS - 1 - row) >= HALO
    for v in range(nvar):
        for n in range(ninst):
            near = near_ref[v, n]
            turned = pltpu.roll(near, HALO, 0)
            first = jnp.where(keep, jnp.where(low, turned, near), 0.0)
            second = jnp.where(keep, jnp.where(low, near, turned), 0.0)
            halo_own[v, n] = jnp.where(core == 0, first, second)
            halo_oth[v, n] = jnp.where(core == 0, second, first)
    jac = functools.partial(jac_row, jac_ref, nvar)

    for n in range(ninst):
        centre = [halo_own[v, n] for v in range(nvar)]
        for u in range(nvar):
            z = sum(jac(1, u, v) * centre[v] for v in range(nvar))
            rest = z + 4.0 * VISCOUS * centre[u]
            for j in range(ninst):
                if j != n:
                    rest += spectral_entry(n - j, 2 * ninst) * halo_own[u, j]
                rest += spectral_entry(n - j - ninst, 2 * ninst) * halo_oth[u, j]
            at = lines_of(ninst, u, n)
            rest_ref[at, :] = rest
            parts_ref[at, 0:axial] = z
            parts_ref[at, axial : 2 * axial] = centre[u]
    rest_ref[...] = rest_ref[...] - times(parts_ref[...], shift_ref[...])

    c0, c1, c2, c3 = sweep_weights()
    for n in range(ninst):
        slope, around = [], []
        for v in range(nvar):
            c = jnp.concatenate([own_ref[v, n], halo_own[v, n]], axis=0)
            nxt, prv = pltpu.roll(c, 2 * ROWS - 1, 0), pltpu.roll(c, 1, 0)
            slope.append(0.5 * (nxt - prv))
            around.append(nxt + prv)
        for u in range(nvar):
            at = lines_of(ninst, u, n)
            r0 = jnp.concatenate([local_ref[u, n], rest_ref[at, :]], axis=0) - VISCOUS * around[u]
            for v in range(nvar):
                r0 += jac(0, u, v) * slope[v]
            r1 = pltpu.roll(r0, 2 * ROWS - 1, 0) + pltpu.roll(r0, 1, 0)
            r2 = pltpu.roll(r1, 2 * ROWS - 1, 0) + pltpu.roll(r1, 1, 0)
            r3 = pltpu.roll(r2, 2 * ROWS - 1, 0) + pltpu.roll(r2, 1, 0)
            r0, r1, r2, r3 = (r[0:ROWS] for r in (r0, r1, r2, r3))
            base_ref[at, :] = c0 * r0 + c1 * r1 + c2 * r2 + c3 * r3
            terms_ref[at, 0:axial] = c1 * r0 + 2.0 * c2 * r1 + 3.0 * c3 * r2
            terms_ref[at, axial : 2 * axial] = c2 * r0 + 3.0 * c3 * r1
            terms_ref[at, 2 * axial : 3 * axial] = c3 * r0
    base_ref[...] = base_ref[...] + times(terms_ref[...], sweep_ref[...])


def step_kernel(planes, cuts, *refs):
    before_ref, base_ref, *refs = refs
    far_refs, refs = refs[:cuts], refs[cuts:]
    jac_ref, shift_ref, sweep_ref, *lines_refs, pick_ref, mix_ref, step_ref = refs[:8]
    new_ref, out_ref, far_own, far_oth, parts_ref, rest_ref, terms_ref = refs[8:]
    core = lax.axis_index("inst")
    low = low_side()
    nvar, ninst, _, axial = new_ref.shape
    cut, packs = nvar // cuts, ninst // 2
    row = lax.broadcasted_iota(jnp.int32, (ROWS, axial), 0)
    side = jnp.where(low, row, ROWS - 1 - row)
    depth = side & (HALO - 1)
    spread = inflow_spread(planes, lines_refs, pick_ref, mix_ref)
    jac = functools.partial(jac_row, jac_ref, nvar)

    def shifted(tile, s):
        moved = pltpu.roll(tile, jnp.where(low, s, ROWS - s), 0)
        return jnp.where(depth >= s, moved, 0.0)

    for v in range(nvar):
        for n in range(ninst):
            tile = far_refs[v // cut][v % cut, n]
            turned = pltpu.roll(tile, HALO, 0)
            first = jnp.where(row < HALO, tile, turned)
            second = jnp.where(row < HALO, turned, tile)
            far_own[v, n] = jnp.where(core == 0, first, second)
            far_oth[v, n] = jnp.where(core == 0, second, first)

    def pack_of(ref, v, m):
        return jnp.where(row < HALO, ref[v, 2 * m], ref[v, 2 * m + 1])

    for m in range(packs):
        centre = [pack_of(far_own, v, m) for v in range(nvar)]
        weights = [
            [
                jnp.where(
                    row < HALO,
                    spectral_entry(2 * m - j - skip, 2 * ninst),
                    spectral_entry(2 * m + 1 - j - skip, 2 * ninst),
                )
                for j in range(ninst)
            ]
            for skip in (0, ninst)
        ]
        for u in range(nvar):
            z = sum(jac(1, u, v) * centre[v] for v in range(nvar))
            rest = z + 4.0 * VISCOUS * centre[u]
            for j in range(ninst):
                rest += weights[0][j] * far_own[u, j] + weights[1][j] * far_oth[u, j]
            at = lines_of(packs, u, m)
            rest_ref[at, :] = rest
            parts_ref[at, 0:axial] = z
            parts_ref[at, axial : 2 * axial] = centre[u]
    rest_ref[...] = rest_ref[...] - times(parts_ref[...], shift_ref[...])

    half = jnp.where(low, 0.5, -0.5)
    for m in range(packs):
        slope, around = [], []
        for v in range(nvar):
            c = pack_of(far_own, v, m)
            behind = shifted(c, 2)
            slope.append(half * (c - behind))
            around.append(c + behind)
        for u in range(nvar):
            at = lines_of(packs, u, m)
            r = shifted(rest_ref[at, :], 1) - VISCOUS * around[u]
            for v in range(nvar):
                r += jac(0, u, v) * slope[v]
            moved = [r, *(shifted(r, s) for s in range(1, SWEEPS + 1))]
            sums = [
                sum(spread_weight(j, SWEEPS - s) * moved[s] for s in range(j, SWEEPS + 1))
                for j in range(SWEEPS + 1)
            ]
            rest_ref[at, :] = sums[0]
            for j in range(1, SWEEPS + 1):
                terms_ref[at, (j - 1) * axial : j * axial] = sums[j]
    rest_ref[...] = rest_ref[...] + times(terms_ref[...], sweep_ref[...])

    step = step_ref[...]
    lane = lax.broadcasted_iota(jnp.int32, (ROWS, LANES), 1)
    reached = side >= HALO
    for n in range(ninst):
        for u in range(nvar):
            far = rest_ref[lines_of(packs, u, n // 2), :]
            turned = pltpu.roll(far, HALO, 0)
            stays = (1 - n % 2) == jnp.where(low, 0, 1)
            far = jnp.where(reached, jnp.where(stays, far, turned), 0.0)
            tiles = [far[:, t : t + LANES] for t in range(0, axial, LANES)]
            group = (u * ninst + n) * GROUP
            for plane_no, plane in enumerate(planes):
                tile, at = divmod(plane - SWEEPS, LANES)
                assert at + GROUP <= LANES
                start = group // LANES * LANES
                moved = pltpu.roll(
                    spread[plane_no][:, start : start + LANES], (at - group) % LANES, 1
                )
                inside = (lane >= at) & (lane < at + GROUP)
                tiles[tile] = tiles[tile] + jnp.where(inside, moved, 0.0)
            more = jnp.concatenate(tiles, axis=1)
            at = lines_of(ninst, u, n)
            out_ref[u, n] = base_ref[at, :] + more
            new_ref[u, n] = before_ref[at, :] - step * more


def here(array):
    return pltpu.with_memory_space_constraint(array, pltpu.VMEM)


def shards(flow_state, jac_pitch, jac_axial, pseudo_step, partner, iface_index):
    nvar, ninst, rows, axial = flow_state.shape
    spaces = lax.axis_size("space")
    planes = interface_planes(axial, IFACES)
    both = ("space", "inst")
    vmem = pl.BlockSpec(memory_space=pltpu.VMEM)
    smem = pl.BlockSpec(memory_space=pltpu.SMEM)
    anywhere = pl.BlockSpec(memory_space=pl.ANY)
    params = pltpu.CompilerParams(vmem_limit_bytes=VMEM_LIMIT)
    block = pltpu.VMEM(flow_state.shape, jnp.float32)
    cores = [(0, 1), (1, 0)]

    other = here(lax.ppermute(flow_state, "inst", cores))
    own, half, shift, sweep = pl.pallas_call(
        functools.partial(stage_kernel, planes),
        out_shape=(
            block,
            pltpu.VMEM((rows, LANES), jnp.float32),
            pltpu.VMEM((2 * axial, axial), jnp.bfloat16),
            pltpu.VMEM((SWEEPS * axial, axial), jnp.bfloat16),
        ),
        in_specs=[vmem],
        out_specs=(vmem,) * 4,
        compiler_params=params,
    )(flow_state)
    staged, own = own, here(own)
    line = pl.pallas_call(
        functools.partial(line_kernel, planes),
        out_shape=pltpu.VMEM((rows, LANES), jnp.float32),
        in_specs=[vmem, vmem],
        out_specs=vmem,
        compiler_params=params,
    )(here(half), other)

    lines, got = line, []
    for turn, bit in enumerate(round_bits(spaces)):
        cross = 1 if turn != 1 else 0
        swaps = [
            (2 * i + c, 2 * (i ^ (1 << bit)) + (c ^ cross)) for i in range(spaces) for c in (0, 1)
        ]
        got.append(lax.ppermute(lines, both, swaps))
        parts = (lines, got[-1])
        lines = jnp.concatenate(parts, axis=0)

    edge = pl.pallas_call(
        edge_kernel,
        out_shape=block,
        in_specs=[vmem, vmem, anywhere],
        out_specs=vmem,
        compiler_params=params,
    )(own, other, line)
    pairs = []
    for i in range(spaces):
        odd = (i + 1) % spaces if i % 2 else (i - 1) % spaces
        pairs += [(2 * i, 2 * (i ^ 1)), (2 * i + 1, 2 * odd + 1)]
    near = lax.ppermute(edge, both, pairs)
    far = [here(lax.ppermute(near, "inst", cores))]

    step, local, jac, pick, mix = pl.pallas_call(
        functools.partial(prepare_kernel, planes, spaces),
        out_shape=(
            pltpu.VMEM(pseudo_step.shape, jnp.float32),
            block,
            pltpu.VMEM((2 * nvar * nvar, axial), jnp.float32),
            pltpu.VMEM((IFACES * 2 * rows, spaces * rows), jnp.float32),
            pltpu.VMEM((IFACES, LANES, 2 * LANES), jnp.float32),
        ),
        in_specs=[smem] * 4 + [vmem] * 3 + [anywhere],
        out_specs=(vmem,) * 5,
        compiler_params=params,
    )(jac_pitch, jac_axial, partner, iface_index, own, other, pseudo_step, got[0])

    lined = nvar * ninst * rows
    base = pl.pallas_call(
        functools.partial(near_kernel, planes),
        out_shape=pltpu.VMEM((lined, axial), jnp.float32),
        in_specs=[vmem] * 6,
        out_specs=vmem,
        scratch_shapes=[
            block,
            block,
            pltpu.VMEM((lined, 2 * axial), jnp.float32),
            pltpu.VMEM((lined, axial), jnp.float32),
            pltpu.VMEM((lined, SWEEPS * axial), jnp.float32),
        ],
        compiler_params=params,
    )(own, *[here(a) for a in (near, local, jac, shift, sweep)])

    before = (staged - step * base.reshape(staged.shape)).reshape(lined, axial)

    return pl.pallas_call(
        functools.partial(step_kernel, planes, len(far)),
        out_shape=(jax.ShapeDtypeStruct(flow_state.shape, jnp.float32),) * 2,
        in_specs=[vmem] * (10 + len(far)),
        out_specs=(vmem, vmem),
        scratch_shapes=[
            block,
            block,
            pltpu.VMEM((lined // 2, 2 * axial), jnp.float32),
            pltpu.VMEM((lined // 2, axial), jnp.float32),
            pltpu.VMEM((lined // 2, SWEEPS * axial), jnp.float32),
        ],
        compiler_params=params,
    )(here(before), here(base), *far, *[here(a) for a in (jac, shift, sweep, *parts, pick, mix, step)])


def solution(mesh):
    in_specs = (
        P("groups", "inst", "space", None),
        P("groups", None),
        P("groups", None),
        P("space", "groups"),
        P("groups", None),
        P("groups", "space"),
    )
    out_specs = (P("groups", "inst", "space", None), P("groups", "inst", "space", None))
    return jax.shard_map(shards, mesh=mesh, in_specs=in_specs, out_specs=out_specs, check_vma=False)
```

```python
import functools
import itertools
import math

import jax
import jax.numpy as jnp
from jax import lax
from jax.experimental import pallas as pl
from jax.experimental.pallas import tpu as pltpu
from jax.sharding import PartitionSpec as P

IFACES = 2
SWEEPS = 3
VISCOUS = 0.25
SMOOTHING = 1.0
HALO = 4
ROWS = 8
LANES = 128
GROUP = 8
VMEM_LIMIT = 16 * 1024 * 1024


def spectral_entry(shift, instances):
    shift %= instances
    if shift == 0:
        return 0.0
    return 0.5 * (-1) ** shift / math.tan(math.pi * shift / instances)


def interface_planes(axial_cells, planes_count):
    return [(plane_no + 1) * axial_cells // (planes_count + 1) for plane_no in range(planes_count)]


def sweep_weights():
    k = SMOOTHING / (1.0 + 4.0 * SMOOTHING)
    base = 1.0 / (1.0 + 4.0 * SMOOTHING)
    return [base * k**m for m in range(SWEEPS)] + [k**SWEEPS]


def spread_weight(m, distance):
    weights = sweep_weights() + [0.0] * 4
    paths = {0: {0: 1, 2: 2}, 1: {1: 1, 3: 3}, 2: {2: 1}, 3: {3: 1}}[distance]
    return sum(count * math.comb(m + j, m) * weights[m + j] for j, count in paths.items())


def round_bits(spaces):
    bits = list(range(spaces.bit_length() - 1))
    return bits[:1] + bits[:0:-1]


def pack_lines(planes, field_ref, half, line):
    nvar, ninst = field_ref.shape[:2]
    lane = lax.broadcasted_iota(jnp.int32, (ROWS, LANES), 1)
    for plane_no, plane in enumerate(planes):
        for v in range(nvar):
            for n in range(ninst):
                at = (plane_no * nvar + v) * 2 * ninst + half * ninst + n
                cell = jnp.broadcast_to(field_ref[v, n, :, plane - 1 : plane], (ROWS, LANES))
                line = jnp.where(lane == at, cell, line)
    return line


def line_kernel(planes, half_ref, oth_ref, line_ref):
    ninst = oth_ref.shape[1]
    line = pack_lines(planes, oth_ref, 1, half_ref[...])
    lane = lax.broadcasted_iota(jnp.int32, (ROWS, LANES), 1)
    swapped = jnp.where(
        lax.rem(lane, 2 * ninst) < ninst,
        pltpu.roll(line, LANES - ninst, 1),
        pltpu.roll(line, ninst, 1),
    )
    line_ref[...] = jnp.where(lax.axis_index("inst") == 0, line, swapped)


def stage_kernel(planes, flow_ref, own_ref, half_ref, shift_ref, sweep_ref):
    own_ref[...] = flow_ref[...]
    half_ref[...] = pack_lines(planes, flow_ref, 0, jnp.zeros((ROWS, LANES), jnp.float32))
    axial = flow_ref.shape[3]
    source = lax.broadcasted_iota(jnp.int32, (axial, axial), 0)
    target = lax.broadcasted_iota(jnp.int32, (axial, axial), 1)
    ahead = target - source
    up, down = jnp.where(ahead == 1, 1.0, 0.0), jnp.where(ahead == -1, 1.0, 0.0)
    once = up + down
    for plane in planes:
        up = jnp.where(target == plane, 0.0, up)
    for plane in [*planes, axial]:
        down = jnp.where(target == plane - 1, jnp.where(ahead == 0, 1.0, 0.0), down)
    shift_ref[0:axial, :] = up.astype(jnp.bfloat16)
    shift_ref[axial : 2 * axial, :] = (VISCOUS * (up + down)).astype(jnp.bfloat16)
    far, edges = jnp.abs(ahead), source + target
    corner = (edges == 0) | (edges == 2 * axial - 2)
    beside = (edges == 1) | (edges == 2 * axial - 3)
    twice = jnp.where(far == 2, 1.0, jnp.where(far == 0, jnp.where(corner, 1.0, 2.0), 0.0))
    thrice = jnp.where(far == 3, 1.0, jnp.where(far == 1, jnp.where(beside, 2.0, 3.0), 0.0))
    for power, value in enumerate((once, twice, thrice)):
        sweep_ref[power * axial : (power + 1) * axial, :] = value.astype(jnp.bfloat16)


def low_side():
    return lax.rem(lax.axis_index("space") + lax.axis_index("inst"), 2) == 1


def edge_kernel(own_ref, oth_ref, after_ref, edge_ref):
    del after_ref
    core = lax.axis_index("inst")
    low = low_side()
    nvar, ninst, _, axial = own_ref.shape
    row = lax.broadcasted_iota(jnp.int32, (ROWS, axial), 0)
    for v in range(nvar):
        for n in range(ninst):
            own, oth = own_ref[v, n], oth_ref[v, n]
            first = jnp.where(core == 0, own, oth)
            second = jnp.where(core == 0, oth, own)
            low_rows = jnp.where(row < HALO, first, pltpu.roll(second, HALO, 0))
            high_rows = jnp.where(row < HALO, pltpu.roll(first, HALO, 0), second)
            edge_ref[v, n] = jnp.where(low, low_rows, high_rows)


def local_terms(planes, jac, own, oth, n):
    nvar, ninst, rows, axial = own.shape
    lane = lax.broadcasted_iota(jnp.int32, (rows, axial), 1)
    inward, spread = [], []
    for v in range(nvar):
        c = own[v, n]
        up, down = pltpu.roll(c, 1, 1), pltpu.roll(c, axial - 1, 1)
        for plane in [0, *planes]:
            up = jnp.where(lane == plane, 0.0, up)
        for plane in [*planes, axial]:
            down = jnp.where(lane == plane - 1, c, down)
        inward.append(c - up)
        spread.append(up + down - 4.0 * c)
    terms = []
    for u in range(nvar):
        total = -VISCOUS * spread[u]
        for v in range(nvar):
            total += jac(u, v) * inward[v]
        for j in range(ninst):
            if j != n:
                total += spectral_entry(n - j, 2 * ninst) * own[u, j]
            total += spectral_entry(n - j - ninst, 2 * ninst) * oth[u, j]
        terms.append(total)
    return terms


def prepare_kernel(
    planes,
    spaces,
    jac_pitch_ref,
    jac_axial_ref,
    partner_ref,
    index_ref,
    own_ref,
    oth_ref,
    step_in_ref,
    after_ref,
    step_ref,
    local_ref,
    jac_ref,
    pick_ref,
    mix_ref,
):
    del after_ref
    step_ref[...] = step_in_ref[...]
    core, space = lax.axis_index("inst"), lax.axis_index("space")
    nvar, ninst, _, axial = own_ref.shape
    for n in range(ninst):
        terms = local_terms(planes, lambda u, v: jac_axial_ref[u, v], own_ref, oth_ref, n)
        for u in range(nvar):
            local_ref[u, n] = terms[u]
    for which, ref in enumerate((jac_pitch_ref, jac_axial_ref)):
        for u in range(nvar):
            for v in range(nvar):
                at = (which * nvar + u) * nvar + v
                jac_ref[at : at + 1, :] = jnp.full((1, axial), ref[u, v], jnp.float32)

    total = spaces * ROWS
    row = lax.broadcasted_iota(jnp.int32, (2 * ROWS, total), 0)
    ahead = jnp.where(row < ROWS + HALO, row, row - 2 * ROWS)
    lane = lax.broadcasted_iota(jnp.int32, (2 * ROWS, total), 1)
    for plane_no in range(len(planes)):
        pitch = index_ref[plane_no, 0] + ahead
        pitch = jnp.where(pitch < 0, pitch + total, pitch)
        pitch = jnp.where(pitch >= total, pitch - total, pitch)
        apart = (pitch >> 3) ^ space
        place = pitch & 7
        for turn, bit in enumerate(round_bits(spaces)):
            place += ((apart >> bit) & 1) << (turn + 3)
        pick_ref[pl.ds(plane_no * 2 * ROWS, 2 * ROWS), :] = jnp.where(lane == place, 1.0, 0.0)

    lane = lax.broadcasted_iota(jnp.int32, (ROWS, 2 * LANES), 1) // GROUP
    row = lax.broadcasted_iota(jnp.int32, (ROWS, 2 * LANES), 0)
    to_var, to_inst = lane // ninst, lax.rem(lane, ninst) + ninst * core
    mix_ref[...] = jnp.zeros(mix_ref.shape, jnp.float32)
    for v in range(nvar):
        block = jnp.zeros((ROWS, 2 * LANES), jnp.float32)
        for u in range(nvar):
            value = -jac_axial_ref[u, v] - (VISCOUS if u == v else 0.0)
            block = jnp.where(to_var == u, value, block)
        for plane_no in range(len(planes)):
            source = lax.rem(to_inst + partner_ref[plane_no, 0], 2 * ninst)
            at = (plane_no * nvar + v) * 2 * ninst
            mix_ref[plane_no, at : at + ROWS, :] = jnp.where(row == source, block, 0.0)


def times(left, right):
    first = left.astype(jnp.bfloat16)
    second = (left - first.astype(jnp.float32)).astype(jnp.bfloat16)
    return jnp.dot(first, right, preferred_element_type=jnp.float32) + jnp.dot(
        second, right, preferred_element_type=jnp.float32
    )


def inflow_spread(planes, lines_refs, pick_ref, mix_ref):
    lines = jnp.concatenate([ref[...] for ref in lines_refs], axis=0)
    pick, first = pick_ref[...].astype(jnp.bfloat16), lines.astype(jnp.bfloat16)
    second = (lines - first.astype(jnp.float32)).astype(jnp.bfloat16)
    plain = dict(preferred_element_type=jnp.float32)
    facing = jnp.dot(pick, first, **plain) + jnp.dot(pick, second, **plain)
    lane = lax.rem(lax.broadcasted_iota(jnp.int32, (ROWS, 2 * LANES), 1), GROUP)
    spread = []
    for plane_no in range(len(planes)):
        seen = facing[plane_no * 2 * ROWS : (plane_no + 1) * 2 * ROWS]
        seen_first, mix_first = seen.astype(jnp.bfloat16), mix_ref[plane_no].astype(jnp.bfloat16)
        seen_second = (seen - seen_first.astype(jnp.float32)).astype(jnp.bfloat16)
        mix_second = (mix_ref[plane_no] - mix_first.astype(jnp.float32)).astype(jnp.bfloat16)
        power = jnp.dot(seen_first, mix_first, **plain)
        power += jnp.dot(seen_second, mix_first, **plain) + jnp.dot(seen_first, mix_second, **plain)
        total = jnp.zeros((ROWS, 2 * LANES), jnp.float32)
        for m in range(SWEEPS + 1):
            weight = jnp.zeros((ROWS, 2 * LANES), jnp.float32)
            for d in range(-SWEEPS, SWEEPS + 1):
                weight = jnp.where(lane == d + SWEEPS, spread_weight(m, abs(d)), weight)
            total += weight * power[0:ROWS]
            if m < SWEEPS:
                power = pltpu.roll(power, 2 * ROWS - 1, 0) + pltpu.roll(power, 1, 0)
        spread.append(total)
    return spread


def jac_row(jac_ref, nvar, which, u, v):
    at = (which * nvar + u) * nvar + v
    return jac_ref[at : at + 1, :]


def lines_of(ninst, u, n):
    at = (u * ninst + n) * ROWS
    return slice(at, at + ROWS)


def near_kernel(planes, *refs):
    own_ref, near_ref, local_ref, jac_ref, shift_ref, sweep_ref, base_ref, *refs = refs
    halo_own, halo_oth, parts_ref, rest_ref, terms_ref = refs
    core = lax.axis_index("inst")
    low = low_side()
    nvar, ninst, _, axial = own_ref.shape
    row = lax.broadcasted_iota(jnp.int32, (ROWS, axial), 0)
    keep = jnp.where(low, row, ROWS - 1 - row) >= HALO
    for v in range(nvar):
        for n in range(ninst):
            near = near_ref[v, n]
            turned = pltpu.roll(near, HALO, 0)
            first = jnp.where(keep, jnp.where(low, turned, near), 0.0)
            second = jnp.where(keep, jnp.where(low, near, turned), 0.0)
            halo_own[v, n] = jnp.where(core == 0, first, second)
            halo_oth[v, n] = jnp.where(core == 0, second, first)
    jac = functools.partial(jac_row, jac_ref, nvar)

    for n in range(ninst):
        centre = [halo_own[v, n] for v in range(nvar)]
        for u in range(nvar):
            z = sum(jac(1, u, v) * centre[v] for v in range(nvar))
            rest = z + 4.0 * VISCOUS * centre[u]
            for j in range(ninst):
                if j != n:
                    rest += spectral_entry(n - j, 2 * ninst) * halo_own[u, j]
                rest += spectral_entry(n - j - ninst, 2 * ninst) * halo_oth[u, j]
            at = lines_of(ninst, u, n)
            rest_ref[at, :] = rest
            parts_ref[at, 0:axial] = z
            parts_ref[at, axial : 2 * axial] = centre[u]
    rest_ref[...] = rest_ref[...] - times(parts_ref[...], shift_ref[...])

    c0, c1, c2, c3 = sweep_weights()
    for n in range(ninst):
        slope, around = [], []
        for v in range(nvar):
            c = jnp.concatenate([own_ref[v, n], halo_own[v, n]], axis=0)
            nxt, prv = pltpu.roll(c, 2 * ROWS - 1, 0), pltpu.roll(c, 1, 0)
            slope.append(0.5 * (nxt - prv))
            around.append(nxt + prv)
        for u in range(nvar):
            at = lines_of(ninst, u, n)
            r0 = jnp.concatenate([local_ref[u, n], rest_ref[at, :]], axis=0) - VISCOUS * around[u]
            for v in range(nvar):
                r0 += jac(0, u, v) * slope[v]
            r1 = pltpu.roll(r0, 2 * ROWS - 1, 0) + pltpu.roll(r0, 1, 0)
            r2 = pltpu.roll(r1, 2 * ROWS - 1, 0) + pltpu.roll(r1, 1, 0)
            r3 = pltpu.roll(r2, 2 * ROWS - 1, 0) + pltpu.roll(r2, 1, 0)
            r0, r1, r2, r3 = (r[0:ROWS] for r in (r0, r1, r2, r3))
            base_ref[at, :] = c0 * r0 + c1 * r1 + c2 * r2 + c3 * r3
            terms_ref[at, 0:axial] = c1 * r0 + 2.0 * c2 * r1 + 3.0 * c3 * r2
            terms_ref[at, axial : 2 * axial] = c2 * r0 + 3.0 * c3 * r1
            terms_ref[at, 2 * axial : 3 * axial] = c3 * r0
    base_ref[...] = base_ref[...] + times(terms_ref[...], sweep_ref[...])


def step_kernel(planes, cuts, *refs):
    before_ref, base_ref, *refs = refs
    far_refs, refs = refs[:cuts], refs[cuts:]
    jac_ref, shift_ref, sweep_ref, *lines_refs, pick_ref, mix_ref, step_ref = refs[:8]
    new_hbm, out_hbm, far_own, far_oth, parts_ref, rest_ref, terms_ref, *refs = refs[8:]
    new_ref, out_ref, sems = refs
    core = lax.axis_index("inst")
    low = low_side()
    nvar, ninst, _, axial = new_ref.shape
    cut, packs = nvar // cuts, ninst // 2
    row = lax.broadcasted_iota(jnp.int32, (ROWS, axial), 0)
    side = jnp.where(low, row, ROWS - 1 - row)
    depth = side & (HALO - 1)
    spread = inflow_spread(planes, lines_refs, pick_ref, mix_ref)
    jac = functools.partial(jac_row, jac_ref, nvar)

    def shifted(tile, s):
        moved = pltpu.roll(tile, jnp.where(low, s, ROWS - s), 0)
        return jnp.where(depth >= s, moved, 0.0)

    for v in range(nvar):
        for n in range(ninst):
            tile = far_refs[v // cut][v % cut, n]
            turned = pltpu.roll(tile, HALO, 0)
            first = jnp.where(row < HALO, tile, turned)
            second = jnp.where(row < HALO, turned, tile)
            far_own[v, n] = jnp.where(core == 0, first, second)
            far_oth[v, n] = jnp.where(core == 0, second, first)

    def pack_of(ref, v, m):
        return jnp.where(row < HALO, ref[v, 2 * m], ref[v, 2 * m + 1])

    for m in range(packs):
        centre = [pack_of(far_own, v, m) for v in range(nvar)]
        weights = [
            [
                jnp.where(
                    row < HALO,
                    spectral_entry(2 * m - j - skip, 2 * ninst),
                    spectral_entry(2 * m + 1 - j - skip, 2 * ninst),
                )
                for j in range(ninst)
            ]
            for skip in (0, ninst)
        ]
        for u in range(nvar):
            z = sum(jac(1, u, v) * centre[v] for v in range(nvar))
            rest = z + 4.0 * VISCOUS * centre[u]
            for j in range(ninst):
                rest += weights[0][j] * far_own[u, j] + weights[1][j] * far_oth[u, j]
            at = lines_of(packs, u, m)
            rest_ref[at, :] = rest
            parts_ref[at, 0:axial] = z
            parts_ref[at, axial : 2 * axial] = centre[u]
    rest_ref[...] = rest_ref[...] - times(parts_ref[...], shift_ref[...])

    half = jnp.where(low, 0.5, -0.5)
    for m in range(packs):
        slope, around = [], []
        for v in range(nvar):
            c = pack_of(far_own, v, m)
            behind = shifted(c, 2)
            slope.append(half * (c - behind))
            around.append(c + behind)
        for u in range(nvar):
            at = lines_of(packs, u, m)
            r = shifted(rest_ref[at, :], 1) - VISCOUS * around[u]
            for v in range(nvar):
                r += jac(0, u, v) * slope[v]
            moved = [r, *(shifted(r, s) for s in range(1, SWEEPS + 1))]
            sums = [
                sum(spread_weight(j, SWEEPS - s) * moved[s] for s in range(j, SWEEPS + 1))
                for j in range(SWEEPS + 1)
            ]
            rest_ref[at, :] = sums[0]
            for j in range(1, SWEEPS + 1):
                terms_ref[at, (j - 1) * axial : j * axial] = sums[j]
    rest_ref[...] = rest_ref[...] + times(terms_ref[...], sweep_ref[...])

    step = step_ref[...]
    lane = lax.broadcasted_iota(jnp.int32, (ROWS, LANES), 1)
    reached = side >= HALO
    copies = []
    for start in range(0, nvar, nvar // 2):
        part = slice(start, start + nvar // 2)
        for u, n in itertools.product(range(part.start, part.stop), range(ninst)):
            far = rest_ref[lines_of(packs, u, n // 2), :]
            turned = pltpu.roll(far, HALO, 0)
            stays = (1 - n % 2) == jnp.where(low, 0, 1)
            far = jnp.where(reached, jnp.where(stays, far, turned), 0.0)
            tiles = [far[:, t : t + LANES] for t in range(0, axial, LANES)]
            group = (u * ninst + n) * GROUP
            for plane_no, plane in enumerate(planes):
                tile, at = divmod(plane - SWEEPS, LANES)
                assert at + GROUP <= LANES
                begin = group // LANES * LANES
                moved = pltpu.roll(
                    spread[plane_no][:, begin : begin + LANES], (at - group) % LANES, 1
                )
                inside = (lane >= at) & (lane < at + GROUP)
                tiles[tile] = tiles[tile] + jnp.where(inside, moved, 0.0)
            more = jnp.concatenate(tiles, axis=1)
            at = lines_of(ninst, u, n)
            out_ref[u, n] = base_ref[at, :] + more
            new_ref[u, n] = before_ref[at, :] - step * more
        pairs = ((out_ref, out_hbm), (new_ref, new_hbm))
        for which, (ref, hbm) in enumerate(pairs):
            sem = sems.at[which, start // (nvar // 2)]
            copies.append(pltpu.make_async_copy(ref.at[part], hbm.at[part], sem))
            copies[-1].start()
    for copy in copies:
        copy.wait()


def here(array):
    return pltpu.with_memory_space_constraint(array, pltpu.VMEM)


def shards(flow_state, jac_pitch, jac_axial, pseudo_step, partner, iface_index):
    nvar, ninst, rows, axial = flow_state.shape
    spaces = lax.axis_size("space")
    planes = interface_planes(axial, IFACES)
    both = ("space", "inst")
    vmem = pl.BlockSpec(memory_space=pltpu.VMEM)
    smem = pl.BlockSpec(memory_space=pltpu.SMEM)
    anywhere = pl.BlockSpec(memory_space=pl.ANY)
    params = pltpu.CompilerParams(vmem_limit_bytes=VMEM_LIMIT)
    block = pltpu.VMEM(flow_state.shape, jnp.float32)
    cores = [(0, 1), (1, 0)]

    other = here(lax.ppermute(flow_state, "inst", cores))
    own, half, shift, sweep = pl.pallas_call(
        functools.partial(stage_kernel, planes),
        out_shape=(
            block,
            pltpu.VMEM((rows, LANES), jnp.float32),
            pltpu.VMEM((2 * axial, axial), jnp.bfloat16),
            pltpu.VMEM((SWEEPS * axial, axial), jnp.bfloat16),
        ),
        in_specs=[vmem],
        out_specs=(vmem,) * 4,
        compiler_params=params,
    )(flow_state)
    staged, own = own, here(own)
    line = pl.pallas_call(
        functools.partial(line_kernel, planes),
        out_shape=pltpu.VMEM((rows, LANES), jnp.float32),
        in_specs=[vmem, vmem],
        out_specs=vmem,
        compiler_params=params,
    )(here(half), other)

    lines, got = line, []
    for turn, bit in enumerate(round_bits(spaces)):
        cross = 1 if turn == 0 else 0
        swaps = [
            (2 * i + c, 2 * (i ^ (1 << bit)) + (c ^ cross)) for i in range(spaces) for c in (0, 1)
        ]
        got.append(lax.ppermute(lines, both, swaps))
        parts = (lines, got[-1])
        lines = jnp.concatenate(parts, axis=0)

    edge = pl.pallas_call(
        edge_kernel,
        out_shape=block,
        in_specs=[vmem, vmem, anywhere],
        out_specs=vmem,
        compiler_params=params,
    )(own, other, line)
    pairs = []
    for i in range(spaces):
        odd = (i + 1) % spaces if i % 2 else (i - 1) % spaces
        pairs += [(2 * i, 2 * (i ^ 1)), (2 * i + 1, 2 * odd + 1)]
    near = lax.ppermute(edge, both, pairs)
    far = [here(lax.ppermute(near, "inst", cores))]

    step, local, jac, pick, mix = pl.pallas_call(
        functools.partial(prepare_kernel, planes, spaces),
        out_shape=(
            pltpu.VMEM(pseudo_step.shape, jnp.float32),
            block,
            pltpu.VMEM((2 * nvar * nvar, axial), jnp.float32),
            pltpu.VMEM((IFACES * 2 * rows, spaces * rows), jnp.float32),
            pltpu.VMEM((IFACES, LANES, 2 * LANES), jnp.float32),
        ),
        in_specs=[smem] * 4 + [vmem] * 3 + [anywhere],
        out_specs=(vmem,) * 5,
        compiler_params=params,
    )(jac_pitch, jac_axial, partner, iface_index, own, other, pseudo_step, got[0])

    lined = nvar * ninst * rows
    base = pl.pallas_call(
        functools.partial(near_kernel, planes),
        out_shape=pltpu.VMEM((lined, axial), jnp.float32),
        in_specs=[vmem] * 6,
        out_specs=vmem,
        scratch_shapes=[
            block,
            block,
            pltpu.VMEM((lined, 2 * axial), jnp.float32),
            pltpu.VMEM((lined, axial), jnp.float32),
            pltpu.VMEM((lined, SWEEPS * axial), jnp.float32),
        ],
        compiler_params=params,
    )(own, *[here(a) for a in (near, local, jac, shift, sweep)])

    before = (staged - step * base.reshape(staged.shape)).reshape(lined, axial)

    return pl.pallas_call(
        functools.partial(step_kernel, planes, len(far)),
        out_shape=(jax.ShapeDtypeStruct(flow_state.shape, jnp.float32),) * 2,
        in_specs=[vmem] * (10 + len(far)),
        out_specs=(anywhere, anywhere),
        scratch_shapes=[
            block,
            block,
            pltpu.VMEM((lined // 2, 2 * axial), jnp.float32),
            pltpu.VMEM((lined // 2, axial), jnp.float32),
            pltpu.VMEM((lined // 2, SWEEPS * axial), jnp.float32),
            block,
            block,
            pltpu.SemaphoreType.DMA((2, 2)),
        ],
        compiler_params=params,
    )(here(before), here(base), *far, *[here(a) for a in (jac, shift, sweep, *parts, pick, mix, step)])


def solution(mesh):
    in_specs = (
        P("groups", "inst", "space", None),
        P("groups", None),
        P("groups", None),
        P("space", "groups"),
        P("groups", None),
        P("groups", "space"),
    )
    out_specs = (P("groups", "inst", "space", None), P("groups", "inst", "space", None))
    return jax.shard_map(shards, mesh=mesh, in_specs=in_specs, out_specs=out_specs, check_vma=False)
```
